32 devices in a mesh: parts: 1, wide: 8 (over z, y), narrow: 4 (over x, core), sub: 1.
Axes of the slice: x: 2, y: 2, z: 4, core: 2. Of those that a mesh axis runs over, the one named last changes fastest.
Arguments:
- pair: bfloat16 [128, 128, 128], P(('parts', 'wide', 'narrow'), 'sub'), may hold values from -6 to 6
- valid: int32 [128], P('parts'), may hold values from 0 to 1, as said below
- norm_gain: float32 [128], replicated, may hold values from 0.5 to 1.5
- norm_bias: float32 [128], replicated, may hold values from -3 to 3
- w_proj: bfloat16 [128, 640], replicated, may hold values from -0.5 to 0.5
- out_gain: float32 [128], replicated, may hold values from 0.5 to 1.5
- out_bias: float32 [128], replicated, may hold values from -3 to 3
- w_out: bfloat16 [128, 128], replicated, may hold values from -0.5 to 0.5
Outputs:
- update: bfloat16 [128, 128, 128], P(('parts', 'wide', 'narrow'), 'sub')
The draws below stay inside these ranges and needn't reach their ends.
Inputs may be any that keep to these rules, and one draw needn't show every extreme that they name: valid is 1 on a prefix of at least 64 positions and 0 after it.
All inputs are finite; a program needn't handle non-finite values.
Results may differ from the reference program's by a relative error of at most 0.012.
Values may be sent and summed in bfloat16 or wider, within the bound.
No kernel may reach another device: no remote copies, remote signals or barrier semaphores. Data moves between devices by JAX's collectives and lax.ppermute only.
A program may use at most 64 MiB of HBM per device.

```python
import math
import jax
import jax.numpy as jnp
from jax import lax

C = 128
N = 128


def draw_valid(key, part):
    key = jax.random.fold_in(key, 11)
    length = jax.random.randint(key, (), N // 2, N + 1)
    return (jnp.arange(N) < length).astype(jnp.int32)


def block_levels(own_key, dims, pieces, least, top_value):
    def one(dim, blocks):
        draws = jax.random.uniform(jax.random.fold_in(jax.random.fold_in(own_key, 6), dim), (blocks,), jnp.float32, least / len(pieces), top_value / len(pieces))
        return jnp.repeat(jnp.exp(draws), dims[dim] // blocks).reshape((-1,) + (1,) * (len(dims) - dim - 1))

    loudness = one(*pieces[0])
    for cut in pieces[1:]:
        loudness = loudness * one(*cut)
    return loudness


def noise(own_key, dims, spread, limit, pieces=(), held_as=jnp.bfloat16):
    result = spread * jax.random.normal(own_key, dims, jnp.float32)
    if pieces:
        result = result * block_levels(own_key, dims, pieces, -0.22, 0.18)
    return jnp.clip(result, -limit, limit).astype(held_as)


def setup_inputs(seed: int = 0, part: int = 0) -> dict:
    seeds = jax.random.split(jax.random.key(seed), 9)
    part_keys = jax.random.split(jax.random.fold_in(seeds[8], part), 9)
    pair = noise(part_keys[0], (N, N, C), 1.0, 6.0, ((0, 32),))
    valid = draw_valid(jax.random.fold_in(jax.random.fold_in(seeds[8], part), 71), part)
    norm_gain = jnp.clip(jax.random.uniform(seeds[2], (C,), jnp.float32, 0.5, 1.5), 0.5, 1.5)
    norm_bias = noise(seeds[3], (C,), 0.5, 3.0, (), jnp.float32)
    w_proj = noise(seeds[4], (C, 5 * C), C ** -0.5, 0.5)
    out_gain = jnp.clip(jax.random.uniform(seeds[5], (C,), jnp.float32, 0.5, 1.5), 0.5, 1.5)
    out_bias = noise(seeds[6], (C,), 0.5, 3.0, (), jnp.float32)
    w_out = noise(seeds[7], (C, C), C ** -0.5, 0.5)
    return dict(pair=pair, valid=valid, norm_gain=norm_gain, norm_bias=norm_bias, w_proj=w_proj, out_gain=out_gain, out_bias=out_bias, w_out=w_out)


epsilon = 1e-05

def layer_norm(values, gain_vec, bias_vec, axis_dim):
    average = lax.optimization_barrier(jnp.mean(values, axis=axis_dim, keepdims=True))
    centered = values - average
    variance = lax.optimization_barrier(jnp.mean(centered * centered, axis=axis_dim, keepdims=True))
    return centered * lax.rsqrt(variance + epsilon) * gain_vec + bias_vec

def reference(pair, valid, norm_gain, norm_bias, w_proj, out_gain, out_bias, w_out):
    total = pair.shape[0]
    chan_count = pair.shape[2]
    block_rows = math.gcd(total, 64)
    block_count = total // block_rows
    flag_values = valid.astype(jnp.float32)

    def project(index):
        start = (index * block_rows).astype(jnp.int32)
        pair_block = lax.dynamic_slice_in_dim(pair, start, block_rows, 0).astype(jnp.float32)
        flag_block = lax.dynamic_slice_in_dim(flag_values, start, block_rows, 0)
        normed = layer_norm(pair_block, norm_gain, norm_bias, 2).astype(jnp.bfloat16)
        projected = jnp.dot(normed.reshape(-1, chan_count), w_proj, preferred_element_type=jnp.float32)
        projected = projected.reshape(block_rows, total, 5 * chan_count)
        pair_flags = flag_block[:, None, None] * flag_values[None, :, None]
        left_side = jax.nn.sigmoid(projected[..., :chan_count]) * projected[..., chan_count:2 * chan_count] * pair_flags
        right_side = jax.nn.sigmoid(projected[..., 2 * chan_count:3 * chan_count]) * projected[..., 3 * chan_count:4 * chan_count] * pair_flags
        gate_values = jax.nn.sigmoid(projected[..., 4 * chan_count:])
        return (left_side.astype(jnp.bfloat16), right_side.astype(jnp.bfloat16), gate_values.astype(jnp.bfloat16))
    left_side, right_side, gate_values = lax.map(project, jnp.arange(block_count, dtype=jnp.int32))
    left_side = left_side.reshape(total, total, chan_count)
    right_side = right_side.reshape(total, total, chan_count)
    gate_values = gate_values.reshape(total, total, chan_count)
    chan_block = 16

    def contract(index):
        start = (index * chan_block).astype(jnp.int32)
        left_block = lax.dynamic_slice_in_dim(left_side, start, chan_block, 2).astype(jnp.float32)
        right_block = lax.dynamic_slice_in_dim(right_side, start, chan_block, 2).astype(jnp.float32)
        return jnp.einsum('ikc,jkc->cij', left_block, right_block).astype(jnp.bfloat16)
    triangle = lax.map(contract, jnp.arange(chan_count // chan_block, dtype=jnp.int32))
    triangle = triangle.reshape(chan_count, total, total)

    def finish(index):
        start = (index * block_rows).astype(jnp.int32)
        tri_block = lax.dynamic_slice_in_dim(triangle, start, block_rows, 1).astype(jnp.float32)
        normed_out = layer_norm(tri_block, out_gain[:, None, None], out_bias[:, None, None], 0).astype(jnp.bfloat16)
        result_out = jnp.einsum('crj,cd->rjd', normed_out.astype(jnp.float32), w_out.astype(jnp.float32))
        gate_block = lax.dynamic_slice_in_dim(gate_values, start, block_rows, 0).astype(jnp.float32)
        return (gate_block * result_out).astype(jnp.bfloat16)
    update = lax.map(finish, jnp.arange(block_count, dtype=jnp.int32))
    return update.reshape(total, total, chan_count)
```

```python
import jax
import jax.numpy as jnp
from jax import lax
from jax.sharding import PartitionSpec as P

epsilon = 1e-05


def layer_norm(values, gain_vec, bias_vec, axis_dim):
    average = jnp.mean(values, axis=axis_dim, keepdims=True)
    centered = values - average
    variance = jnp.mean(centered * centered, axis=axis_dim, keepdims=True)
    return centered * lax.rsqrt(variance + epsilon) * gain_vec + bias_vec


def local(pair, valid, norm_gain, norm_bias, w_proj, out_gain, out_bias, w_out):
    row_count, col_count, chan_count = pair.shape
    row_start = lax.axis_index(("wide", "narrow")) * row_count
    col_start = lax.axis_index("sub") * col_count
    row_flags = lax.dynamic_slice_in_dim(valid, row_start, row_count, 0).astype(jnp.float32)
    col_flags = lax.dynamic_slice_in_dim(valid, col_start, col_count, 0).astype(jnp.float32)
    pair_flags = row_flags[:, None] * col_flags[None, :]
    normed = layer_norm(pair.astype(jnp.float32), norm_gain, norm_bias, 2).astype(jnp.bfloat16)
    projected = jnp.einsum(
        "rkc,cd->drk", normed, w_proj[:, : 4 * chan_count], preferred_element_type=jnp.float32
    )
    left_side = (
        jax.nn.sigmoid(projected[:chan_count]) * projected[chan_count : 2 * chan_count] * pair_flags
    ).astype(jnp.bfloat16)
    right_side = (
        jax.nn.sigmoid(projected[2 * chan_count : 3 * chan_count])
        * projected[3 * chan_count :]
        * pair_flags
    ).astype(jnp.bfloat16)
    gate_values = jax.nn.sigmoid(
        jnp.einsum(
            "rkc,cd->rkd", normed, w_proj[:, 4 * chan_count :], preferred_element_type=jnp.float32
        )
    ).astype(jnp.bfloat16)
    both_sides = jnp.stack([left_side, right_side], axis=1)
    both_group = lax.all_to_all(
        both_sides, ("wide", "narrow"), split_axis=0, concat_axis=2, tiled=True
    )
    left_group, right_group = both_group[:, 0], both_group[:, 1]
    partial_sums = jnp.einsum(
        "cik,cjk->cij", left_group, right_group, preferred_element_type=jnp.float32
    )
    summed = lax.psum_scatter(partial_sums, "sub", scatter_dimension=2, tiled=True).astype(
        jnp.bfloat16
    )
    returned = lax.all_to_all(summed, ("wide", "narrow"), split_axis=1, concat_axis=0, tiled=True)
    normed_out = layer_norm(
        returned.astype(jnp.float32), out_gain[:, None, None], out_bias[:, None, None], 0
    ).astype(jnp.bfloat16)
    result_out = jnp.einsum("crj,cd->rjd", normed_out, w_out, preferred_element_type=jnp.float32)
    return (gate_values.astype(jnp.float32) * result_out).astype(jnp.bfloat16)


def solution(mesh):
    in_specs = (
        P(("parts", "wide", "narrow"), "sub", None),
        P("parts"),
        P(),
        P(),
        P(),
        P(),
        P(),
        P(),
    )
    out_specs = P(("parts", "wide", "narrow"), "sub", None)
    return jax.shard_map(local, mesh=mesh, in_specs=in_specs, out_specs=out_specs, check_vma=False)
```

```python
import jax
import jax.numpy as jnp
from jax import lax
from jax.sharding import PartitionSpec as P

epsilon = 1e-05


def layer_norm(values, gain_vec, bias_vec, axis_dim):
    average = jnp.mean(values, axis=axis_dim, keepdims=True)
    centered = values - average
    variance = jnp.mean(centered * centered, axis=axis_dim, keepdims=True)
    return centered * lax.rsqrt(variance + epsilon) * gain_vec + bias_vec


def local_exchange(pair, valid, norm_gain, norm_bias, w_proj, out_gain, out_bias, w_out):
    row_count, col_count, chan_count = pair.shape
    row_start = lax.axis_index(("wide", "narrow")) * row_count
    col_start = lax.axis_index("sub") * col_count
    row_flags = lax.dynamic_slice_in_dim(valid, row_start, row_count, 0).astype(jnp.float32)
    col_flags = lax.dynamic_slice_in_dim(valid, col_start, col_count, 0).astype(jnp.float32)
    pair_flags = row_flags[:, None] * col_flags[None, :]
    normed = layer_norm(pair.astype(jnp.float32), norm_gain, norm_bias, 2).astype(jnp.bfloat16)
    projected = jnp.einsum(
        "rkc,cd->drk", normed, w_proj[:, : 4 * chan_count], preferred_element_type=jnp.float32
    )
    left_side = (
        jax.nn.sigmoid(projected[:chan_count]) * projected[chan_count : 2 * chan_count] * pair_flags
    ).astype(jnp.bfloat16)
    right_side = (
        jax.nn.sigmoid(projected[2 * chan_count : 3 * chan_count])
        * projected[3 * chan_count :]
        * pair_flags
    ).astype(jnp.bfloat16)
    gate_values = jax.nn.sigmoid(
        jnp.einsum(
            "rkc,cd->rkd", normed, w_proj[:, 4 * chan_count :], preferred_element_type=jnp.float32
        )
    ).astype(jnp.bfloat16)
    both_sides = jnp.stack([left_side, right_side], axis=1)
    both_group = lax.all_to_all(
        both_sides, ("wide", "narrow"), split_axis=0, concat_axis=2, tiled=True
    )
    left_group, right_group = both_group[:, 0], both_group[:, 1]
    partial_sums = jnp.einsum(
        "cik,cjk->cij", left_group, right_group, preferred_element_type=jnp.float32
    )
    summed = lax.psum_scatter(partial_sums, "sub", scatter_dimension=2, tiled=True).astype(
        jnp.bfloat16
    )
    returned = lax.all_to_all(summed, ("wide", "narrow"), split_axis=1, concat_axis=0, tiled=True)
    normed_out = layer_norm(
        returned.astype(jnp.float32), out_gain[:, None, None], out_bias[:, None, None], 0
    ).astype(jnp.bfloat16)
    result_out = jnp.einsum("crj,cd->rjd", normed_out, w_out, preferred_element_type=jnp.float32)
    return (gate_values.astype(jnp.float32) * result_out).astype(jnp.bfloat16)


def local_gather(pair, valid, norm_gain, norm_bias, w_proj, out_gain, out_bias, w_out):
    row_count, col_count, chan_count = pair.shape
    row_start = lax.axis_index(("wide", "narrow")) * row_count
    col_start = lax.axis_index("sub") * col_count
    row_flags = lax.dynamic_slice_in_dim(valid, row_start, row_count, 0).astype(jnp.float32)
    col_flags = lax.dynamic_slice_in_dim(valid, col_start, col_count, 0).astype(jnp.float32)
    pair_flags = row_flags[:, None] * col_flags[None, :]
    normed = layer_norm(pair.astype(jnp.float32), norm_gain, norm_bias, 2).astype(jnp.bfloat16)
    projected = jnp.einsum("rkc,cd->rkd", normed, w_proj, preferred_element_type=jnp.float32)
    parts = [projected[..., i * chan_count : (i + 1) * chan_count] for i in range(5)]
    right_side = (jax.nn.sigmoid(parts[2]) * parts[3] * pair_flags[:, :, None]).astype(jnp.bfloat16)
    right_all = lax.all_gather(right_side, ("wide", "narrow"), axis=0, tiled=True)
    left_side = (jax.nn.sigmoid(parts[0]) * parts[1] * pair_flags[:, :, None]).astype(jnp.bfloat16)
    gate_values = jax.nn.sigmoid(parts[4]).astype(jnp.bfloat16)
    partial_sums = jnp.einsum(
        "ikc,jkc->ijc", left_side, right_all, preferred_element_type=jnp.float32
    )
    triangle = lax.psum_scatter(partial_sums, "sub", scatter_dimension=1, tiled=True).astype(
        jnp.bfloat16
    )
    normed_out = layer_norm(
        triangle.astype(jnp.float32), out_gain, out_bias, 2
    ).astype(jnp.bfloat16)
    result_out = jnp.einsum("rjc,cd->rjd", normed_out, w_out, preferred_element_type=jnp.float32)
    return (gate_values.astype(jnp.float32) * result_out).astype(jnp.bfloat16)


def local(pair, *rest):
    shards = lax.axis_size(("wide", "narrow"))
    small = shards * pair.size * pair.dtype.itemsize <= 8 * 2**20
    return (local_gather if small else local_exchange)(pair, *rest)


def solution(mesh):
    in_specs = (
        P(("parts", "wide", "narrow"), "sub", None),
        P("parts"),
        P(),
        P(),
        P(),
        P(),
        P(),
        P(),
    )
    out_specs = P(("parts", "wide", "narrow"), "sub", None)
    return jax.shard_map(local, mesh=mesh, in_specs=in_specs, out_specs=out_specs, check_vma=False)
```

```python
import functools

import jax
import jax.numpy as jnp
from jax import lax
from jax.experimental import pallas as pl
from jax.experimental.pallas import tpu as pltpu
from jax.sharding import PartitionSpec as P

epsilon = 1e-05
axes = ("wide", "narrow")


def layer_norm(values, gain_vec, bias_vec, axis_dim):
    average = jnp.mean(values, axis=axis_dim, keepdims=True)
    centered = values - average
    variance = jnp.mean(centered * centered, axis=axis_dim, keepdims=True)
    return centered * lax.rsqrt(variance + epsilon) * gain_vec + bias_vec


def swap_halves(low, high):
    first = lax.broadcasted_iota(jnp.int32, low.shape, 0) < 4
    return (
        jnp.where(first, low, pltpu.roll(high, 4, 0)),
        jnp.where(first, pltpu.roll(low, 4, 0), high),
    )


def project_kernel(flags_ref, valid_ref, pair_ref, gain_ref, bias_ref, w_ref, out_ref, normed_ref):
    row_count, col_count, chan_count = pair_ref.shape
    row_start = lax.axis_index(axes) * row_count
    tokens = pair_ref[...].reshape(row_count * col_count, chan_count).astype(jnp.float32)
    normed = layer_norm(tokens, gain_ref[...], bias_ref[...], 1).astype(jnp.bfloat16)
    normed_ref[...] = normed
    projected = lax.dot_general(
        w_ref[:, : 4 * chan_count], normed, (((0,), (1,)), ((), ())),
        preferred_element_type=jnp.float32,
    )
    col_flags = valid_ref[...].astype(jnp.float32)
    flags = jnp.concatenate(
        [col_flags * flags_ref[row_start + r].astype(jnp.float32) for r in range(row_count)], axis=1
    )
    for chan in range(0, chan_count, 8):
        a_gate, a, b_gate, b = (
            projected[i * chan_count + chan : i * chan_count + chan + 8] for i in range(4)
        )
        left = jax.nn.sigmoid(a_gate) * a * flags
        right = jax.nn.sigmoid(b_gate) * b * flags
        for half, block in enumerate(swap_halves(left, right)):
            for r in range(0, row_count, 2):
                rows = jnp.concatenate(
                    [block[:, (r + i) * col_count : (r + i + 1) * col_count] for i in range(2)], axis=0
                )
                out_ref[chan // 4 + half, r * 8 : (r + 2) * 8, :] = rows.astype(jnp.bfloat16)


def contract_kernel(blocks_ref, out_ref, held_ref):
    shards, block_rows, cols = blocks_ref.shape
    total = held_ref.shape[0] // 8
    held_ref[...] = blocks_ref[...].reshape(shards * block_rows, cols).astype(jnp.float32)
    products = []
    for c in range(4):
        left = held_ref[pl.ds(c, total, stride=8), :].astype(jnp.bfloat16)
        right = held_ref[pl.ds(4 + c, total, stride=8), :].astype(jnp.bfloat16)
        products.append(
            lax.dot_general(
                left, right, (((1,), (1,)), ((), ())), preferred_element_type=jnp.float32
            )
        )
    for row in range(0, total, 8):
        pieces = [product[row : row + 8] for product in products]
        low, high = swap_halves(pieces[0], pieces[1]), swap_halves(pieces[2], pieces[3])
        for half in range(2):
            rows = jnp.concatenate([low[half], high[half]], axis=0)
            out_ref[row // 4 + half] = rows.astype(jnp.bfloat16)


def gate_kernel(normed_ref, w_ref, out_ref):
    chan_count = normed_ref.shape[1]
    projected = jnp.dot(
        normed_ref[...], w_ref[:, 4 * chan_count :], preferred_element_type=jnp.float32
    )
    out_ref[...] = jax.nn.sigmoid(projected).astype(jnp.bfloat16)


def finish_kernel(blocks_ref, gate_ref, gain_ref, bias_ref, w_ref, out_ref, held_ref):
    row_count, col_count, chan_count = out_ref.shape
    held_ref[...] = blocks_ref[...].reshape(held_ref.shape).astype(jnp.float32)
    gain = jnp.transpose(jnp.broadcast_to(gain_ref[...], (col_count, chan_count)))
    bias = jnp.transpose(jnp.broadcast_to(bias_ref[...], (col_count, chan_count)))
    for r in range(row_count):
        triangle = held_ref[pl.ds(r, chan_count, stride=row_count), :]
        normed = layer_norm(triangle, gain, bias, 0).astype(jnp.bfloat16)
        result = lax.dot_general(
            normed, w_ref[...], (((0,), (0,)), ((), ())), preferred_element_type=jnp.float32
        )
        gate = gate_ref[r * col_count : (r + 1) * col_count, :].astype(jnp.float32)
        out_ref[r] = (gate * result).astype(jnp.bfloat16)


def local_blocks(pair, valid, norm_gain, norm_bias, w_proj, out_gain, out_bias, w_out):
    row_count, col_count, chan_count = pair.shape
    shards = lax.axis_size(axes)
    tokens = row_count * col_count
    vmem = pl.BlockSpec(memory_space=pltpu.VMEM)
    smem = pl.BlockSpec(memory_space=pltpu.SMEM)

    def line(vector):
        return vector.reshape(1, -1)

    def shaped(*dims):
        return jax.ShapeDtypeStruct(dims, jnp.bfloat16)

    sides, normed = pl.pallas_call(
        project_kernel,
        out_shape=(shaped(shards, 8 * row_count, col_count), shaped(tokens, chan_count)),
        in_specs=[smem] + [vmem] * 5,
        out_specs=(vmem, vmem),
        name="project",
    )(valid, line(valid), pair, line(norm_gain), line(norm_bias), w_proj)
    sides = lax.all_to_all(sides, axes, split_axis=0, concat_axis=0, tiled=True)
    triangle = pl.pallas_call(
        contract_kernel,
        out_shape=shaped(shards, 4 * row_count, col_count),
        in_specs=[vmem],
        out_specs=vmem,
        scratch_shapes=[pltpu.VMEM((8 * col_count, col_count), jnp.float32)],
        name="contract",
    )(sides)
    triangle = lax.all_to_all(triangle, axes, split_axis=0, concat_axis=0, tiled=True)
    gate_values = pl.pallas_call(
        gate_kernel,
        out_shape=shaped(tokens, chan_count),
        in_specs=[vmem] * 2,
        out_specs=vmem,
        name="gate",
    )(normed, w_proj)
    return pl.pallas_call(
        finish_kernel,
        out_shape=shaped(row_count, col_count, chan_count),
        in_specs=[vmem] * 5,
        out_specs=vmem,
        scratch_shapes=[pltpu.VMEM((tokens, chan_count), jnp.float32)],
        name="finish",
    )(triangle, gate_values, line(out_gain), line(out_bias), w_out)


def local_arrays(pair, valid, norm_gain, norm_bias, w_proj, out_gain, out_bias, w_out):
    row_count, col_count, chan_count = pair.shape
    row_start = lax.axis_index(("wide", "narrow")) * row_count
    col_start = lax.axis_index("sub") * col_count
    row_flags = lax.dynamic_slice_in_dim(valid, row_start, row_count, 0).astype(jnp.float32)
    col_flags = lax.dynamic_slice_in_dim(valid, col_start, col_count, 0).astype(jnp.float32)
    pair_flags = row_flags[:, None] * col_flags[None, :]
    normed = layer_norm(pair.astype(jnp.float32), norm_gain, norm_bias, 2).astype(jnp.bfloat16)
    projected = jnp.einsum(
        "rkc,cd->drk", normed, w_proj[:, : 4 * chan_count], preferred_element_type=jnp.float32
    )
    left_side = (
        jax.nn.sigmoid(projected[:chan_count]) * projected[chan_count : 2 * chan_count] * pair_flags
    ).astype(jnp.bfloat16)
    right_side = (
        jax.nn.sigmoid(projected[2 * chan_count : 3 * chan_count])
        * projected[3 * chan_count :]
        * pair_flags
    ).astype(jnp.bfloat16)
    gate_values = jax.nn.sigmoid(
        jnp.einsum(
            "rkc,cd->rkd", normed, w_proj[:, 4 * chan_count :], preferred_element_type=jnp.float32
        )
    ).astype(jnp.bfloat16)
    both_sides = jnp.stack([left_side, right_side], axis=1)
    both_group = lax.all_to_all(
        both_sides, ("wide", "narrow"), split_axis=0, concat_axis=2, tiled=True
    )
    left_group, right_group = both_group[:, 0], both_group[:, 1]
    partial_sums = jnp.einsum(
        "cik,cjk->cij", left_group, right_group, preferred_element_type=jnp.float32
    )
    summed = lax.psum_scatter(partial_sums, "sub", scatter_dimension=2, tiled=True).astype(
        jnp.bfloat16
    )
    returned = lax.all_to_all(summed, ("wide", "narrow"), split_axis=1, concat_axis=0, tiled=True)
    normed_out = layer_norm(
        returned.astype(jnp.float32), out_gain[:, None, None], out_bias[:, None, None], 0
    ).astype(jnp.bfloat16)
    result_out = jnp.einsum("crj,cd->rjd", normed_out, w_out, preferred_element_type=jnp.float32)
    return (gate_values.astype(jnp.float32) * result_out).astype(jnp.bfloat16)


def local(pair, *rest):
    row_count, col_count, chan_count = pair.shape
    shards = lax.axis_size(axes)
    fits = (
        lax.axis_size("sub") == 1
        and (row_count, col_count, chan_count) == (4, 128, 128)
        and shards * row_count == col_count
        and shards * 4 == chan_count
    )
    return (local_blocks if fits else local_arrays)(pair, *rest)


def solution(mesh):
    in_specs = (
        P(("parts", "wide", "narrow"), "sub", None),
        P("parts"),
        P(),
        P(),
        P(),
        P(),
        P(),
        P(),
    )
    out_specs = P(("parts", "wide", "narrow"), "sub", None)
    return jax.shard_map(local, mesh=mesh, in_specs=in_specs, out_specs=out_specs, check_vma=False)
```

```python
import functools

import jax
import jax.numpy as jnp
from jax import lax
from jax.experimental import pallas as pl
from jax.experimental.pallas import tpu as pltpu
from jax.sharding import PartitionSpec as P

epsilon = 1e-05
axes = ("wide", "narrow")


def layer_norm(values, gain_vec, bias_vec, axis_dim):
    average = jnp.mean(values, axis=axis_dim, keepdims=True)
    centered = values - average
    variance = jnp.mean(centered * centered, axis=axis_dim, keepdims=True)
    return centered * lax.rsqrt(variance + epsilon) * gain_vec + bias_vec


def swap_halves(low, high):
    first = lax.broadcasted_iota(jnp.int32, low.shape, 0) < 4
    return (
        jnp.where(first, low, pltpu.roll(high, 4, 0)),
        jnp.where(first, pltpu.roll(low, 4, 0), high),
    )


def send_blocks(held_ref, out_refs):
    me = lax.axis_index(axes)
    for s, out_ref in enumerate(out_refs):
        out_ref[...] = held_ref[me ^ s]


def receive_blocks(block_refs, held_ref):
    me = lax.axis_index(axes)
    rows = block_refs[0].shape[0]
    for s, block_ref in enumerate(block_refs):
        held_ref[pl.ds(pl.multiple_of((me ^ s) * rows, rows), rows), :] = block_ref[...].astype(
            jnp.float32
        )


def project_kernel(flags_ref, valid_ref, pair_ref, gain_ref, bias_ref, w_ref, normed_ref, *rest):
    out_refs, out_ref = rest[:-1], rest[-1]
    row_count, col_count, chan_count = pair_ref.shape
    row_start = lax.axis_index(axes) * row_count
    tokens = pair_ref[...].reshape(row_count * col_count, chan_count).astype(jnp.float32)
    normed = layer_norm(tokens, gain_ref[...], bias_ref[...], 1).astype(jnp.bfloat16)
    normed_ref[...] = normed
    projected = lax.dot_general(
        w_ref[:, : 4 * chan_count], normed, (((0,), (1,)), ((), ())),
        preferred_element_type=jnp.float32,
    )
    col_flags = valid_ref[...].astype(jnp.float32)
    flags = jnp.concatenate(
        [col_flags * flags_ref[row_start + r].astype(jnp.float32) for r in range(row_count)], axis=1
    )
    for chan in range(0, chan_count, 8):
        a_gate, a, b_gate, b = (
            projected[i * chan_count + chan : i * chan_count + chan + 8] for i in range(4)
        )
        left = jax.nn.sigmoid(a_gate) * a * flags
        right = jax.nn.sigmoid(b_gate) * b * flags
        for half, block in enumerate(swap_halves(left, right)):
            for r in range(0, row_count, 2):
                rows = jnp.concatenate(
                    [block[:, (r + i) * col_count : (r + i + 1) * col_count] for i in range(2)], axis=0
                )
                out_ref[chan // 4 + half, r * 8 : (r + 2) * 8, :] = rows.astype(jnp.bfloat16)
    send_blocks(out_ref, out_refs)


def contract_kernel(shards, *refs):
    block_refs, out_refs, (held_ref, out_ref) = refs[:shards], refs[shards : 2 * shards], refs[2 * shards :]
    total = held_ref.shape[0] // 8
    receive_blocks(block_refs, held_ref)
    products = []
    for c in range(4):
        left = held_ref[pl.ds(c, total, stride=8), :].astype(jnp.bfloat16)
        right = held_ref[pl.ds(4 + c, total, stride=8), :].astype(jnp.bfloat16)
        products.append(
            lax.dot_general(
                left, right, (((1,), (1,)), ((), ())), preferred_element_type=jnp.float32
            )
        )
    for row in range(0, total, 8):
        pieces = [product[row : row + 8] for product in products]
        low, high = swap_halves(pieces[0], pieces[1]), swap_halves(pieces[2], pieces[3])
        for half in range(2):
            rows = jnp.concatenate([low[half], high[half]], axis=0)
            out_ref[row // 4 + half] = rows.astype(jnp.bfloat16)
    send_blocks(out_ref, out_refs)


def gate_kernel(normed_ref, w_ref, out_ref):
    chan_count = normed_ref.shape[1]
    projected = jnp.dot(
        normed_ref[...], w_ref[:, 4 * chan_count :], preferred_element_type=jnp.float32
    )
    out_ref[...] = jax.nn.sigmoid(projected).astype(jnp.bfloat16)


def finish_kernel(gate_ref, gain_ref, bias_ref, w_ref, *rest):
    block_refs, out_ref, held_ref = rest[:-2], rest[-2], rest[-1]
    row_count, col_count, chan_count = out_ref.shape
    receive_blocks(block_refs, held_ref)
    gain = jnp.transpose(jnp.broadcast_to(gain_ref[...], (col_count, chan_count)))
    bias = jnp.transpose(jnp.broadcast_to(bias_ref[...], (col_count, chan_count)))
    for r in range(row_count):
        triangle = held_ref[pl.ds(r, chan_count, stride=row_count), :]
        normed = layer_norm(triangle, gain, bias, 0).astype(jnp.bfloat16)
        result = lax.dot_general(
            normed, w_ref[...], (((0,), (0,)), ((), ())), preferred_element_type=jnp.float32
        )
        gate = gate_ref[r * col_count : (r + 1) * col_count, :].astype(jnp.float32)
        out_ref[r] = (gate * result).astype(jnp.bfloat16)


def exchange(blocks):
    shards = len(blocks)
    return [
        lax.ppermute(block, axes, [(i, i ^ s) for i in range(shards)]) if s else block
        for s, block in enumerate(blocks)
    ]


def local_blocks(pair, valid, norm_gain, norm_bias, w_proj, out_gain, out_bias, w_out):
    row_count, col_count, chan_count = pair.shape
    shards = lax.axis_size(axes)
    tokens = row_count * col_count
    vmem = pl.BlockSpec(memory_space=pltpu.VMEM)
    smem = pl.BlockSpec(memory_space=pltpu.SMEM)

    def line(vector):
        return vector.reshape(1, -1)

    def shaped(*dims):
        return jax.ShapeDtypeStruct(dims, jnp.bfloat16)

    side_block = shaped(8 * row_count, col_count)
    triangle_block = shaped(4 * row_count, col_count)

    def held(block, dtype):
        dims = block.shape if dtype == jnp.bfloat16 else (shards * block.shape[0],) + block.shape[1:]
        return pltpu.VMEM((shards,) + dims if dtype == jnp.bfloat16 else dims, dtype)

    normed, *sides = pl.pallas_call(
        project_kernel,
        out_shape=[shaped(tokens, chan_count)] + [side_block] * shards,
        in_specs=[smem] + [vmem] * 5,
        out_specs=[vmem] * (shards + 1),
        scratch_shapes=[held(side_block, jnp.bfloat16)],
        name="project",
    )(valid, line(valid), pair, line(norm_gain), line(norm_bias), w_proj)
    triangle = pl.pallas_call(
        functools.partial(contract_kernel, shards),
        out_shape=[triangle_block] * shards,
        in_specs=[vmem] * shards,
        out_specs=[vmem] * shards,
        scratch_shapes=[held(side_block, jnp.float32), held(triangle_block, jnp.bfloat16)],
        name="contract",
    )(*exchange(sides))
    triangle = exchange(triangle)
    gate_values = pl.pallas_call(
        gate_kernel,
        out_shape=shaped(tokens, chan_count),
        in_specs=[vmem] * 2,
        out_specs=vmem,
        name="gate",
    )(normed, w_proj)
    return pl.pallas_call(
        finish_kernel,
        out_shape=shaped(row_count, col_count, chan_count),
        in_specs=[vmem] * (4 + shards),
        out_specs=vmem,
        scratch_shapes=[held(triangle_block, jnp.float32)],
        name="finish",
    )(gate_values, line(out_gain), line(out_bias), w_out, *triangle)


def local_arrays(pair, valid, norm_gain, norm_bias, w_proj, out_gain, out_bias, w_out):
    row_count, col_count, chan_count = pair.shape
    row_start = lax.axis_index(("wide", "narrow")) * row_count
    col_start = lax.axis_index("sub") * col_count
    row_flags = lax.dynamic_slice_in_dim(valid, row_start, row_count, 0).astype(jnp.float32)
    col_flags = lax.dynamic_slice_in_dim(valid, col_start, col_count, 0).astype(jnp.float32)
    pair_flags = row_flags[:, None] * col_flags[None, :]
    normed = layer_norm(pair.astype(jnp.float32), norm_gain, norm_bias, 2).astype(jnp.bfloat16)
    projected = jnp.einsum(
        "rkc,cd->drk", normed, w_proj[:, : 4 * chan_count], preferred_element_type=jnp.float32
    )
    left_side = (
        jax.nn.sigmoid(projected[:chan_count]) * projected[chan_count : 2 * chan_count] * pair_flags
    ).astype(jnp.bfloat16)
    right_side = (
        jax.nn.sigmoid(projected[2 * chan_count : 3 * chan_count])
        * projected[3 * chan_count :]
        * pair_flags
    ).astype(jnp.bfloat16)
    gate_values = jax.nn.sigmoid(
        jnp.einsum(
            "rkc,cd->rkd", normed, w_proj[:, 4 * chan_count :], preferred_element_type=jnp.float32
        )
    ).astype(jnp.bfloat16)
    both_sides = jnp.stack([left_side, right_side], axis=1)
    both_group = lax.all_to_all(
        both_sides, ("wide", "narrow"), split_axis=0, concat_axis=2, tiled=True
    )
    left_group, right_group = both_group[:, 0], both_group[:, 1]
    partial_sums = jnp.einsum(
        "cik,cjk->cij", left_group, right_group, preferred_element_type=jnp.float32
    )
    summed = lax.psum_scatter(partial_sums, "sub", scatter_dimension=2, tiled=True).astype(
        jnp.bfloat16
    )
    returned = lax.all_to_all(summed, ("wide", "narrow"), split_axis=1, concat_axis=0, tiled=True)
    normed_out = layer_norm(
        returned.astype(jnp.float32), out_gain[:, None, None], out_bias[:, None, None], 0
    ).astype(jnp.bfloat16)
    result_out = jnp.einsum("crj,cd->rjd", normed_out, w_out, preferred_element_type=jnp.float32)
    return (gate_values.astype(jnp.float32) * result_out).astype(jnp.bfloat16)


def local(pair, *rest):
    row_count, col_count, chan_count = pair.shape
    shards = lax.axis_size(axes)
    fits = (
        lax.axis_size("sub") == 1
        and (row_count, col_count, chan_count) == (4, 128, 128)
        and shards * row_count == col_count
        and shards * 4 == chan_count
        and shards & (shards - 1) == 0
    )
    return (local_blocks if fits else local_arrays)(pair, *rest)


def solution(mesh):
    in_specs = (
        P(("parts", "wide", "narrow"), "sub", None),
        P("parts"),
        P(),
        P(),
        P(),
        P(),
        P(),
        P(),
    )
    out_specs = P(("parts", "wide", "narrow"), "sub", None)
    return jax.shard_map(local, mesh=mesh, in_specs=in_specs, out_specs=out_specs, check_vma=False)
```

```python
import functools

import jax
import jax.numpy as jnp
from jax import lax
from jax.experimental import pallas as pl
from jax.experimental.pallas import tpu as pltpu
from jax.sharding import PartitionSpec as P

epsilon = 1e-05
axes = ("wide", "narrow")
kernel_vmem = 8 * 2**20


def layer_norm(values, gain_vec, bias_vec, axis_dim):
    average = jnp.mean(values, axis=axis_dim, keepdims=True)
    centered = values - average
    variance = jnp.mean(centered * centered, axis=axis_dim, keepdims=True)
    return centered * lax.rsqrt(variance + epsilon) * gain_vec + bias_vec


def swap_halves(low, high):
    first = lax.broadcasted_iota(jnp.int32, low.shape, 0) < 4
    return (
        jnp.where(first, low, pltpu.roll(high, 4, 0)),
        jnp.where(first, pltpu.roll(low, 4, 0), high),
    )


def project_kernel(flags_ref, valid_ref, pair_ref, gain_ref, bias_ref, w_ref, out_ref, normed_ref):
    row_count, col_count, chan_count = pair_ref.shape
    row_start = lax.axis_index(axes) * row_count
    tokens = pair_ref[...].reshape(row_count * col_count, chan_count).astype(jnp.float32)
    normed = layer_norm(tokens, gain_ref[...], bias_ref[...], 1).astype(jnp.bfloat16)
    normed_ref[...] = normed
    projected = lax.dot_general(
        w_ref[:, : 4 * chan_count], normed, (((0,), (1,)), ((), ())),
        preferred_element_type=jnp.float32,
    )
    col_flags = valid_ref[...].astype(jnp.float32)
    flags = jnp.concatenate(
        [col_flags * flags_ref[row_start + r].astype(jnp.float32) for r in range(row_count)], axis=1
    )
    for chan in range(0, chan_count, 8):
        a_gate, a, b_gate, b = (
            projected[i * chan_count + chan : i * chan_count + chan + 8] for i in range(4)
        )
        left = jax.nn.sigmoid(a_gate) * a * flags
        right = jax.nn.sigmoid(b_gate) * b * flags
        for half, block in enumerate(swap_halves(left, right)):
            for r in range(0, row_count, 2):
                rows = jnp.concatenate(
                    [block[:, (r + i) * col_count : (r + i + 1) * col_count] for i in range(2)], axis=0
                )
                out_ref[chan // 4 + half, r * 8 : (r + 2) * 8, :] = rows.astype(jnp.bfloat16)


def contract_kernel(blocks_ref, out_ref, held_ref):
    shards, block_rows, cols = blocks_ref.shape
    total = held_ref.shape[0] // 8
    held_ref[...] = blocks_ref[...].reshape(shards * block_rows, cols).astype(jnp.float32)
    products = []
    for c in range(4):
        left = held_ref[pl.ds(c, total, stride=8), :].astype(jnp.bfloat16)
        right = held_ref[pl.ds(4 + c, total, stride=8), :].astype(jnp.bfloat16)
        products.append(
            lax.dot_general(
                left, right, (((1,), (1,)), ((), ())), preferred_element_type=jnp.float32
            )
        )
    for row in range(0, total, 8):
        pieces = [product[row : row + 8] for product in products]
        low, high = swap_halves(pieces[0], pieces[1]), swap_halves(pieces[2], pieces[3])
        for half in range(2):
            rows = jnp.concatenate([low[half], high[half]], axis=0)
            out_ref[row // 4 + half] = rows.astype(jnp.bfloat16)


def gate_kernel(normed_ref, w_ref, out_ref):
    chan_count = normed_ref.shape[1]
    projected = jnp.dot(
        normed_ref[...], w_ref[:, 4 * chan_count :], preferred_element_type=jnp.float32
    )
    out_ref[...] = jax.nn.sigmoid(projected).astype(jnp.bfloat16)


def finish_kernel(blocks_ref, gate_ref, gain_ref, bias_ref, w_ref, out_ref, held_ref):
    row_count, col_count, chan_count = out_ref.shape
    held_ref[...] = blocks_ref[...].reshape(held_ref.shape).astype(jnp.float32)
    gain = jnp.transpose(jnp.broadcast_to(gain_ref[...], (col_count, chan_count)))
    bias = jnp.transpose(jnp.broadcast_to(bias_ref[...], (col_count, chan_count)))
    for r in range(row_count):
        triangle = held_ref[pl.ds(r, chan_count, stride=row_count), :]
        normed = layer_norm(triangle, gain, bias, 0).astype(jnp.bfloat16)
        result = lax.dot_general(
            normed, w_ref[...], (((0,), (0,)), ((), ())), preferred_element_type=jnp.float32
        )
        gate = gate_ref[r * col_count : (r + 1) * col_count, :].astype(jnp.float32)
        out_ref[r] = (gate * result).astype(jnp.bfloat16)


def local_blocks(pair, valid, norm_gain, norm_bias, w_proj, out_gain, out_bias, w_out):
    row_count, col_count, chan_count = pair.shape
    shards = lax.axis_size(axes)
    tokens = row_count * col_count
    vmem = pl.BlockSpec(memory_space=pltpu.VMEM)
    smem = pl.BlockSpec(memory_space=pltpu.SMEM)

    def line(vector):
        return vector.reshape(1, -1)

    def shaped(*dims):
        return jax.ShapeDtypeStruct(dims, jnp.bfloat16)

    sides, normed = pl.pallas_call(
        project_kernel,
        out_shape=(shaped(shards, 8 * row_count, col_count), shaped(tokens, chan_count)),
        in_specs=[smem] + [vmem] * 5,
        out_specs=(vmem, vmem),
        compiler_params=pltpu.CompilerParams(vmem_limit_bytes=kernel_vmem),
        name="project",
    )(valid, line(valid), pair, line(norm_gain), line(norm_bias), w_proj)
    sides = lax.all_to_all(sides, axes, split_axis=0, concat_axis=0, tiled=True)
    triangle = pl.pallas_call(
        contract_kernel,
        out_shape=shaped(shards, 4 * row_count, col_count),
        in_specs=[vmem],
        out_specs=vmem,
        scratch_shapes=[pltpu.VMEM((8 * col_count, col_count), jnp.float32)],
        compiler_params=pltpu.CompilerParams(vmem_limit_bytes=kernel_vmem),
        name="contract",
    )(sides)
    triangle = lax.all_to_all(triangle, axes, split_axis=0, concat_axis=0, tiled=True)
    gate_values = pl.pallas_call(
        gate_kernel,
        out_shape=shaped(tokens, chan_count),
        in_specs=[vmem] * 2,
        out_specs=vmem,
        compiler_params=pltpu.CompilerParams(vmem_limit_bytes=kernel_vmem),
        name="gate",
    )(normed, w_proj)
    return pl.pallas_call(
        finish_kernel,
        out_shape=shaped(row_count, col_count, chan_count),
        in_specs=[vmem] * 5,
        out_specs=vmem,
        scratch_shapes=[pltpu.VMEM((tokens, chan_count), jnp.float32)],
        compiler_params=pltpu.CompilerParams(vmem_limit_bytes=kernel_vmem),
        name="finish",
    )(triangle, gate_values, line(out_gain), line(out_bias), w_out)


def local_arrays(pair, valid, norm_gain, norm_bias, w_proj, out_gain, out_bias, w_out):
    row_count, col_count, chan_count = pair.shape
    row_start = lax.axis_index(("wide", "narrow")) * row_count
    col_start = lax.axis_index("sub") * col_count
    row_flags = lax.dynamic_slice_in_dim(valid, row_start, row_count, 0).astype(jnp.float32)
    col_flags = lax.dynamic_slice_in_dim(valid, col_start, col_count, 0).astype(jnp.float32)
    pair_flags = row_flags[:, None] * col_flags[None, :]
    normed = layer_norm(pair.astype(jnp.float32), norm_gain, norm_bias, 2).astype(jnp.bfloat16)
    projected = jnp.einsum(
        "rkc,cd->drk", normed, w_proj[:, : 4 * chan_count], preferred_element_type=jnp.float32
    )
    left_side = (
        jax.nn.sigmoid(projected[:chan_count]) * projected[chan_count : 2 * chan_count] * pair_flags
    ).astype(jnp.bfloat16)
    right_side = (
        jax.nn.sigmoid(projected[2 * chan_count : 3 * chan_count])
        * projected[3 * chan_count :]
        * pair_flags
    ).astype(jnp.bfloat16)
    gate_values = jax.nn.sigmoid(
        jnp.einsum(
            "rkc,cd->rkd", normed, w_proj[:, 4 * chan_count :], preferred_element_type=jnp.float32
        )
    ).astype(jnp.bfloat16)
    both_sides = jnp.stack([left_side, right_side], axis=1)
    both_group = lax.all_to_all(
        both_sides, ("wide", "narrow"), split_axis=0, concat_axis=2, tiled=True
    )
    left_group, right_group = both_group[:, 0], both_group[:, 1]
    partial_sums = jnp.einsum(
        "cik,cjk->cij", left_group, right_group, preferred_element_type=jnp.float32
    )
    summed = lax.psum_scatter(partial_sums, "sub", scatter_dimension=2, tiled=True).astype(
        jnp.bfloat16
    )
    returned = lax.all_to_all(summed, ("wide", "narrow"), split_axis=1, concat_axis=0, tiled=True)
    normed_out = layer_norm(
        returned.astype(jnp.float32), out_gain[:, None, None], out_bias[:, None, None], 0
    ).astype(jnp.bfloat16)
    result_out = jnp.einsum("crj,cd->rjd", normed_out, w_out, preferred_element_type=jnp.float32)
    return (gate_values.astype(jnp.float32) * result_out).astype(jnp.bfloat16)


def local(pair, *rest):
    row_count, col_count, chan_count = pair.shape
    shards = lax.axis_size(axes)
    fits = (
        lax.axis_size("sub") == 1
        and (row_count, col_count, chan_count) == (4, 128, 128)
        and shards * row_count == col_count
        and shards * 4 == chan_count
    )
    return (local_blocks if fits else local_arrays)(pair, *rest)


def solution(mesh):
    in_specs = (
        P(("parts", "wide", "narrow"), "sub", None),
        P("parts"),
        P(),
        P(),
        P(),
        P(),
        P(),
        P(),
    )
    out_specs = P(("parts", "wide", "narrow"), "sub", None)
    return jax.shard_map(local, mesh=mesh, in_specs=in_specs, out_specs=out_specs, check_vma=False)
```

```python
import functools

import jax
import jax.numpy as jnp
from jax import lax
from jax.experimental import pallas as pl
from jax.experimental.pallas import tpu as pltpu
from jax.sharding import PartitionSpec as P

epsilon = 1e-05
axes = ("wide", "narrow")
kernel_vmem = 8 * 2**20


def layer_norm(values, gain_vec, bias_vec, axis_dim):
    average = jnp.mean(values, axis=axis_dim, keepdims=True)
    centered = values - average
    variance = jnp.mean(centered * centered, axis=axis_dim, keepdims=True)
    return centered * lax.rsqrt(variance + epsilon) * gain_vec + bias_vec


def swap_halves(low, high):
    first = lax.broadcasted_iota(jnp.int32, low.shape, 0) < 4
    return (
        jnp.where(first, low, pltpu.roll(high, 4, 0)),
        jnp.where(first, pltpu.roll(low, 4, 0), high),
    )


def project_kernel(
    pair_hbm, valid_hbm, gain_hbm, bias_hbm, w_hbm, out_ref, normed_ref,
    pair_ref, valid_ref, gain_ref, bias_ref, w_ref, sems,
):
    row_count, col_count, chan_count = pair_ref.shape
    fetches = [
        pltpu.make_async_copy(source, held, sems.at[i])
        for i, (source, held) in enumerate((
            (pair_hbm, pair_ref), (gain_hbm, gain_ref), (bias_hbm, bias_ref),
            (w_hbm.at[:, : 4 * chan_count], w_ref), (valid_hbm, valid_ref),
        ))
    ]
    for fetch in fetches:
        fetch.start()
    row_start = lax.axis_index(axes) * row_count
    for fetch in fetches[:3]:
        fetch.wait()
    tokens = pair_ref[...].reshape(row_count * col_count, chan_count).astype(jnp.float32)
    normed = layer_norm(tokens, gain_ref[...], bias_ref[...], 1).astype(jnp.bfloat16)
    normed_ref[...] = normed
    for fetch in fetches[3:]:
        fetch.wait()
    projected = lax.dot_general(
        w_ref[...], normed, (((0,), (1,)), ((), ())),
        preferred_element_type=jnp.float32,
    )
    col_flags = valid_ref[...].astype(jnp.float32)
    places = lax.broadcasted_iota(jnp.int32, col_flags.shape, 1)
    row_flags = [
        jnp.sum(jnp.where(places == row_start + r, col_flags, 0.0), axis=1, keepdims=True)
        for r in range(row_count)
    ]
    flags = jnp.concatenate([col_flags * row_flag for row_flag in row_flags], axis=1)
    for chan in range(0, chan_count, 8):
        a_gate, a, b_gate, b = (
            projected[i * chan_count + chan : i * chan_count + chan + 8] for i in range(4)
        )
        left = jax.nn.sigmoid(a_gate) * a * flags
        right = jax.nn.sigmoid(b_gate) * b * flags
        for half, block in enumerate(swap_halves(left, right)):
            for r in range(0, row_count, 2):
                rows = jnp.concatenate(
                    [block[:, (r + i) * col_count : (r + i + 1) * col_count] for i in range(2)], axis=0
                )
                out_ref[chan // 4 + half, r * 8 : (r + 2) * 8, :] = rows.astype(jnp.bfloat16)


def contract_kernel(blocks_ref, out_ref, held_ref):
    shards, block_rows, cols = blocks_ref.shape
    total = held_ref.shape[0] // 8
    held_ref[...] = blocks_ref[...].reshape(shards * block_rows, cols).astype(jnp.float32)
    products = []
    for c in range(4):
        left = held_ref[pl.ds(c, total, stride=8), :].astype(jnp.bfloat16)
        right = held_ref[pl.ds(4 + c, total, stride=8), :].astype(jnp.bfloat16)
        products.append(
            lax.dot_general(
                left, right, (((1,), (1,)), ((), ())), preferred_element_type=jnp.float32
            )
        )
    for row in range(0, total, 8):
        pieces = [product[row : row + 8] for product in products]
        low, high = swap_halves(pieces[0], pieces[1]), swap_halves(pieces[2], pieces[3])
        for half in range(2):
            rows = jnp.concatenate([low[half], high[half]], axis=0)
            out_ref[row // 4 + half] = rows.astype(jnp.bfloat16)


def gate_kernel(normed_ref, w_ref, gain_ref, bias_ref, w_out_ref, out_ref, scales_ref, weights_ref):
    chan_count = normed_ref.shape[1]
    projected = jnp.dot(
        normed_ref[...], w_ref[:, 4 * chan_count :], preferred_element_type=jnp.float32
    )
    out_ref[...] = jax.nn.sigmoid(projected).astype(jnp.bfloat16)
    for i, vector_ref in enumerate((gain_ref, bias_ref)):
        scales_ref[i] = jnp.transpose(jnp.broadcast_to(vector_ref[...], scales_ref.shape[1:]))
    weights_ref[...] = w_out_ref[...]


def finish_kernel(blocks_ref, gate_ref, scales_ref, w_ref, out_ref, held_ref):
    row_count, col_count, chan_count = out_ref.shape
    held_ref[...] = blocks_ref[...].reshape(held_ref.shape).astype(jnp.float32)
    for r in range(row_count):
        triangle = held_ref[pl.ds(r, chan_count, stride=row_count), :]
        normed = layer_norm(triangle, scales_ref[0], scales_ref[1], 0).astype(jnp.bfloat16)
        result = lax.dot_general(
            normed, w_ref[...], (((0,), (0,)), ((), ())), preferred_element_type=jnp.float32
        )
        gate = gate_ref[r * col_count : (r + 1) * col_count, :].astype(jnp.float32)
        out_ref[r] = (gate * result).astype(jnp.bfloat16)


def local_blocks(pair, valid, norm_gain, norm_bias, w_proj, out_gain, out_bias, w_out):
    row_count, col_count, chan_count = pair.shape
    shards = lax.axis_size(axes)
    tokens = row_count * col_count
    vmem = pl.BlockSpec(memory_space=pltpu.VMEM)
    hbm = pl.BlockSpec(memory_space=pltpu.HBM)

    def line(vector):
        return vector.reshape(1, -1)

    def shaped(*dims):
        return jax.ShapeDtypeStruct(dims, jnp.bfloat16)

    sides, normed = pl.pallas_call(
        project_kernel,
        out_shape=(shaped(shards, 8 * row_count, col_count), shaped(tokens, chan_count)),
        in_specs=[hbm] * 5,
        out_specs=(vmem, vmem),
        scratch_shapes=[
            pltpu.VMEM(pair.shape, jnp.bfloat16),
            pltpu.VMEM((1, col_count), jnp.int32),
            pltpu.VMEM((1, chan_count), jnp.float32),
            pltpu.VMEM((1, chan_count), jnp.float32),
            pltpu.VMEM((chan_count, 4 * chan_count), jnp.bfloat16),
            pltpu.SemaphoreType.DMA((5,)),
        ],
        compiler_params=pltpu.CompilerParams(vmem_limit_bytes=kernel_vmem),
        name="project",
    )(pair, line(valid), line(norm_gain), line(norm_bias), w_proj)
    sides = lax.all_to_all(sides, axes, split_axis=0, concat_axis=0, tiled=True)
    triangle = pl.pallas_call(
        contract_kernel,
        out_shape=shaped(shards, 4 * row_count, col_count),
        in_specs=[vmem],
        out_specs=vmem,
        scratch_shapes=[pltpu.VMEM((8 * col_count, col_count), jnp.float32)],
        compiler_params=pltpu.CompilerParams(vmem_limit_bytes=kernel_vmem),
        name="contract",
    )(sides)
    triangle = lax.all_to_all(triangle, axes, split_axis=0, concat_axis=0, tiled=True)
    gate_values, scales, weights = pl.pallas_call(
        gate_kernel,
        out_shape=(
            shaped(tokens, chan_count),
            jax.ShapeDtypeStruct((2, chan_count, col_count), jnp.float32),
            shaped(chan_count, chan_count),
        ),
        in_specs=[vmem] * 5,
        out_specs=(vmem,) * 3,
        compiler_params=pltpu.CompilerParams(vmem_limit_bytes=kernel_vmem),
        name="gate",
    )(normed, w_proj, line(out_gain), line(out_bias), w_out)
    return pl.pallas_call(
        finish_kernel,
        out_shape=shaped(row_count, col_count, chan_count),
        in_specs=[vmem] * 4,
        out_specs=vmem,
        scratch_shapes=[pltpu.VMEM((tokens, chan_count), jnp.float32)],
        compiler_params=pltpu.CompilerParams(vmem_limit_bytes=kernel_vmem),
        name="finish",
    )(triangle, gate_values, scales, weights)


def local_arrays(pair, valid, norm_gain, norm_bias, w_proj, out_gain, out_bias, w_out):
    row_count, col_count, chan_count = pair.shape
    row_start = lax.axis_index(("wide", "narrow")) * row_count
    col_start = lax.axis_index("sub") * col_count
    row_flags = lax.dynamic_slice_in_dim(valid, row_start, row_count, 0).astype(jnp.float32)
    col_flags = lax.dynamic_slice_in_dim(valid, col_start, col_count, 0).astype(jnp.float32)
    pair_flags = row_flags[:, None] * col_flags[None, :]
    normed = layer_norm(pair.astype(jnp.float32), norm_gain, norm_bias, 2).astype(jnp.bfloat16)
    projected = jnp.einsum(
        "rkc,cd->drk", normed, w_proj[:, : 4 * chan_count], preferred_element_type=jnp.float32
    )
    left_side = (
        jax.nn.sigmoid(projected[:chan_count]) * projected[chan_count : 2 * chan_count] * pair_flags
    ).astype(jnp.bfloat16)
    right_side = (
        jax.nn.sigmoid(projected[2 * chan_count : 3 * chan_count])
        * projected[3 * chan_count :]
        * pair_flags
    ).astype(jnp.bfloat16)
    gate_values = jax.nn.sigmoid(
        jnp.einsum(
            "rkc,cd->rkd", normed, w_proj[:, 4 * chan_count :], preferred_element_type=jnp.float32
        )
    ).astype(jnp.bfloat16)
    both_sides = jnp.stack([left_side, right_side], axis=1)
    both_group = lax.all_to_all(
        both_sides, ("wide", "narrow"), split_axis=0, concat_axis=2, tiled=True
    )
    left_group, right_group = both_group[:, 0], both_group[:, 1]
    partial_sums = jnp.einsum(
        "cik,cjk->cij", left_group, right_group, preferred_element_type=jnp.float32
    )
    summed = lax.psum_scatter(partial_sums, "sub", scatter_dimension=2, tiled=True).astype(
        jnp.bfloat16
    )
    returned = lax.all_to_all(summed, ("wide", "narrow"), split_axis=1, concat_axis=0, tiled=True)
    normed_out = layer_norm(
        returned.astype(jnp.float32), out_gain[:, None, None], out_bias[:, None, None], 0
    ).astype(jnp.bfloat16)
    result_out = jnp.einsum("crj,cd->rjd", normed_out, w_out, preferred_element_type=jnp.float32)
    return (gate_values.astype(jnp.float32) * result_out).astype(jnp.bfloat16)


def local(pair, *rest):
    row_count, col_count, chan_count = pair.shape
    shards = lax.axis_size(axes)
    fits = (
        lax.axis_size("sub") == 1
        and (row_count, col_count, chan_count) == (4, 128, 128)
        and shards * row_count == col_count
        and shards * 4 == chan_count
    )
    return (local_blocks if fits else local_arrays)(pair, *rest)


def solution(mesh):
    in_specs = (
        P(("parts", "wide", "narrow"), "sub", None),
        P("parts"),
        P(),
        P(),
        P(),
        P(),
        P(),
        P(),
    )
    out_specs = P(("parts", "wide", "narrow"), "sub", None)
    return jax.shard_map(local, mesh=mesh, in_specs=in_specs, out_specs=out_specs, check_vma=False)
```

```python
import functools

import jax
import jax.numpy as jnp
from jax import lax
from jax.experimental import pallas as pl
from jax.experimental.pallas import tpu as pltpu
from jax.sharding import PartitionSpec as P

epsilon = 1e-05
axes = ("wide", "narrow")
kernel_vmem = 8 * 2**20


def layer_norm(values, gain_vec, bias_vec, axis_dim):
    average = jnp.mean(values, axis=axis_dim, keepdims=True)
    centered = values - average
    variance = jnp.mean(centered * centered, axis=axis_dim, keepdims=True)
    return centered * lax.rsqrt(variance + epsilon) * gain_vec + bias_vec


def swap_halves(low, high):
    first = lax.broadcasted_iota(jnp.int32, low.shape, 0) < 4
    return (
        jnp.where(first, low, pltpu.roll(high, 4, 0)),
        jnp.where(first, pltpu.roll(low, 4, 0), high),
    )


def project_kernel(
    pair_hbm, valid_hbm, gain_hbm, bias_hbm, w_hbm, out_ref, normed_ref,
    pair_ref, valid_ref, gain_ref, bias_ref, w_ref, sems,
):
    row_count, col_count, chan_count = pair_ref.shape
    fetches = [
        pltpu.make_async_copy(source, held, sems.at[i])
        for i, (source, held) in enumerate((
            (pair_hbm, pair_ref), (gain_hbm, gain_ref), (bias_hbm, bias_ref),
            (w_hbm.at[:, : 4 * chan_count], w_ref), (valid_hbm, valid_ref),
        ))
    ]
    for fetch in fetches:
        fetch.start()
    row_start = lax.axis_index(axes) * row_count
    for fetch in fetches[:3]:
        fetch.wait()
    tokens = pair_ref[...].reshape(row_count * col_count, chan_count).astype(jnp.float32)
    normed = layer_norm(tokens, gain_ref[...], bias_ref[...], 1).astype(jnp.bfloat16)
    normed_ref[...] = normed
    for fetch in fetches[3:]:
        fetch.wait()
    projected = lax.dot_general(
        w_ref[...], normed, (((0,), (1,)), ((), ())),
        preferred_element_type=jnp.float32,
    )
    col_flags = valid_ref[...].astype(jnp.float32)
    places = lax.broadcasted_iota(jnp.int32, col_flags.shape, 1)
    row_flags = [
        jnp.sum(jnp.where(places == row_start + r, col_flags, 0.0), axis=1, keepdims=True)
        for r in range(row_count)
    ]
    flags = jnp.concatenate([col_flags * row_flag for row_flag in row_flags], axis=1)
    for chan in range(0, chan_count, 8):
        a_gate, a, b_gate, b = (
            projected[i * chan_count + chan : i * chan_count + chan + 8] for i in range(4)
        )
        left = jax.nn.sigmoid(a_gate) * a * flags
        right = jax.nn.sigmoid(b_gate) * b * flags
        for half, block in enumerate(swap_halves(left, right)):
            for r in range(0, row_count, 2):
                rows = jnp.concatenate(
                    [block[:, (r + i) * col_count : (r + i + 1) * col_count] for i in range(2)], axis=0
                )
                out_ref[chan // 4 + half, r * 8 : (r + 2) * 8, :] = rows.astype(jnp.bfloat16)


def contract_kernel(blocks_ref, out_ref, held_ref):
    shards, block_rows, cols = blocks_ref.shape
    total = held_ref.shape[0] // 8
    held_ref[...] = blocks_ref[...].reshape(shards * block_rows, cols).astype(jnp.float32)
    products = []
    for c in range(4):
        left = held_ref[pl.ds(c, total, stride=8), :].astype(jnp.bfloat16)
        right = held_ref[pl.ds(4 + c, total, stride=8), :].astype(jnp.bfloat16)
        products.append(
            lax.dot_general(
                left, right, (((1,), (1,)), ((), ())), preferred_element_type=jnp.float32
            )
        )
    for row in range(0, total, 8):
        pieces = [product[row : row + 8] for product in products]
        low, high = swap_halves(pieces[0], pieces[1]), swap_halves(pieces[2], pieces[3])
        for half in range(2):
            rows = jnp.concatenate([low[half], high[half]], axis=0)
            out_ref[row // 4 + half] = rows.astype(jnp.bfloat16)


def gate_kernel(normed_ref, w_ref, gain_ref, bias_ref, w_out_ref, out_ref, scales_ref, weights_ref):
    chan_count = normed_ref.shape[1]
    projected = jnp.dot(
        normed_ref[...], w_ref[:, 4 * chan_count :], preferred_element_type=jnp.float32
    )
    out_ref[...] = jax.nn.sigmoid(projected).astype(jnp.bfloat16)
    for i, vector_ref in enumerate((gain_ref, bias_ref)):
        scales_ref[i] = jnp.transpose(jnp.broadcast_to(vector_ref[...], scales_ref.shape[1:]))
    weights_ref[...] = w_out_ref[...]


def finish_kernel(blocks_ref, gate_ref, scales_ref, w_ref, out_ref, held_ref):
    row_count, col_count, chan_count = out_ref.shape
    held_ref[...] = blocks_ref[...].reshape(held_ref.shape).astype(jnp.float32)
    for r in range(row_count):
        triangle = held_ref[pl.ds(r, chan_count, stride=row_count), :]
        normed = layer_norm(triangle, scales_ref[0], scales_ref[1], 0).astype(jnp.bfloat16)
        result = lax.dot_general(
            normed, w_ref[...], (((0,), (0,)), ((), ())), preferred_element_type=jnp.float32
        )
        gate = gate_ref[r * col_count : (r + 1) * col_count, :].astype(jnp.float32)
        out_ref[r] = (gate * result).astype(jnp.bfloat16)


def local_blocks(pair, valid, norm_gain, norm_bias, w_proj, out_gain, out_bias, w_out):
    row_count, col_count, chan_count = pair.shape
    shards = lax.axis_size(axes)
    tokens = row_count * col_count
    vmem = pl.BlockSpec(memory_space=pltpu.VMEM)
    hbm = pl.BlockSpec(memory_space=pltpu.HBM)

    def line(vector):
        return vector.reshape(1, -1)

    def shaped(*dims):
        return jax.ShapeDtypeStruct(dims, jnp.bfloat16)

    sides, normed = pl.pallas_call(
        project_kernel,
        out_shape=(shaped(shards, 8 * row_count, col_count), shaped(tokens, chan_count)),
        in_specs=[hbm] * 5,
        out_specs=(vmem, vmem),
        scratch_shapes=[
            pltpu.VMEM(pair.shape, jnp.bfloat16),
            pltpu.VMEM((1, col_count), jnp.int32),
            pltpu.VMEM((1, chan_count), jnp.float32),
            pltpu.VMEM((1, chan_count), jnp.float32),
            pltpu.VMEM((chan_count, 4 * chan_count), jnp.bfloat16),
            pltpu.SemaphoreType.DMA((5,)),
        ],
        name="project",
    )(pair, line(valid), line(norm_gain), line(norm_bias), w_proj)
    sides = lax.all_to_all(sides, axes, split_axis=0, concat_axis=0, tiled=True)
    triangle = pl.pallas_call(
        contract_kernel,
        out_shape=shaped(shards, 4 * row_count, col_count),
        in_specs=[vmem],
        out_specs=vmem,
        scratch_shapes=[pltpu.VMEM((8 * col_count, col_count), jnp.float32)],
        compiler_params=pltpu.CompilerParams(vmem_limit_bytes=kernel_vmem),
        name="contract",
    )(sides)
    triangle = lax.all_to_all(triangle, axes, split_axis=0, concat_axis=0, tiled=True)
    gate_values, scales, weights = pl.pallas_call(
        gate_kernel,
        out_shape=(
            shaped(tokens, chan_count),
            jax.ShapeDtypeStruct((2, chan_count, col_count), jnp.float32),
            shaped(chan_count, chan_count),
        ),
        in_specs=[vmem] * 5,
        out_specs=(vmem,) * 3,
        compiler_params=pltpu.CompilerParams(vmem_limit_bytes=kernel_vmem),
        name="gate",
    )(normed, w_proj, line(out_gain), line(out_bias), w_out)
    return pl.pallas_call(
        finish_kernel,
        out_shape=shaped(row_count, col_count, chan_count),
        in_specs=[vmem] * 4,
        out_specs=vmem,
        scratch_shapes=[pltpu.VMEM((tokens, chan_count), jnp.float32)],
        compiler_params=pltpu.CompilerParams(vmem_limit_bytes=kernel_vmem),
        name="finish",
    )(triangle, gate_values, scales, weights)


def local_arrays(pair, valid, norm_gain, norm_bias, w_proj, out_gain, out_bias, w_out):
    row_count, col_count, chan_count = pair.shape
    row_start = lax.axis_index(("wide", "narrow")) * row_count
    col_start = lax.axis_index("sub") * col_count
    row_flags = lax.dynamic_slice_in_dim(valid, row_start, row_count, 0).astype(jnp.float32)
    col_flags = lax.dynamic_slice_in_dim(valid, col_start, col_count, 0).astype(jnp.float32)
    pair_flags = row_flags[:, None] * col_flags[None, :]
    normed = layer_norm(pair.astype(jnp.float32), norm_gain, norm_bias, 2).astype(jnp.bfloat16)
    projected = jnp.einsum(
        "rkc,cd->drk", normed, w_proj[:, : 4 * chan_count], preferred_element_type=jnp.float32
    )
    left_side = (
        jax.nn.sigmoid(projected[:chan_count]) * projected[chan_count : 2 * chan_count] * pair_flags
    ).astype(jnp.bfloat16)
    right_side = (
        jax.nn.sigmoid(projected[2 * chan_count : 3 * chan_count])
        * projected[3 * chan_count :]
        * pair_flags
    ).astype(jnp.bfloat16)
    gate_values = jax.nn.sigmoid(
        jnp.einsum(
            "rkc,cd->rkd", normed, w_proj[:, 4 * chan_count :], preferred_element_type=jnp.float32
        )
    ).astype(jnp.bfloat16)
    both_sides = jnp.stack([left_side, right_side], axis=1)
    both_group = lax.all_to_all(
        both_sides, ("wide", "narrow"), split_axis=0, concat_axis=2, tiled=True
    )
    left_group, right_group = both_group[:, 0], both_group[:, 1]
    partial_sums = jnp.einsum(
        "cik,cjk->cij", left_group, right_group, preferred_element_type=jnp.float32
    )
    summed = lax.psum_scatter(partial_sums, "sub", scatter_dimension=2, tiled=True).astype(
        jnp.bfloat16
    )
    returned = lax.all_to_all(summed, ("wide", "narrow"), split_axis=1, concat_axis=0, tiled=True)
    normed_out = layer_norm(
        returned.astype(jnp.float32), out_gain[:, None, None], out_bias[:, None, None], 0
    ).astype(jnp.bfloat16)
    result_out = jnp.einsum("crj,cd->rjd", normed_out, w_out, preferred_element_type=jnp.float32)
    return (gate_values.astype(jnp.float32) * result_out).astype(jnp.bfloat16)


def local(pair, *rest):
    row_count, col_count, chan_count = pair.shape
    shards = lax.axis_size(axes)
    fits = (
        lax.axis_size("sub") == 1
        and (row_count, col_count, chan_count) == (4, 128, 128)
        and shards * row_count == col_count
        and shards * 4 == chan_count
    )
    return (local_blocks if fits else local_arrays)(pair, *rest)


def solution(mesh):
    in_specs = (
        P(("parts", "wide", "narrow"), "sub", None),
        P("parts"),
        P(),
        P(),
        P(),
        P(),
        P(),
        P(),
    )
    out_specs = P(("parts", "wide", "narrow"), "sub", None)
    return jax.shard_map(local, mesh=mesh, in_specs=in_specs, out_specs=out_specs, check_vma=False)
```

```python
import functools

import jax
import jax.numpy as jnp
from jax import lax
from jax.experimental import pallas as pl
from jax.experimental.pallas import tpu as pltpu
from jax.sharding import PartitionSpec as P

epsilon = 1e-05
axes = ("wide", "narrow")
kernel_vmem = 8 * 2**20
places = 4


def layer_norm(values, gain_vec, bias_vec, axis_dim):
    average = jnp.mean(values, axis=axis_dim, keepdims=True)
    centered = values - average
    variance = jnp.mean(centered * centered, axis=axis_dim, keepdims=True)
    return centered * lax.rsqrt(variance + epsilon) * gain_vec + bias_vec


def swap_halves(low, high):
    first = lax.broadcasted_iota(jnp.int32, low.shape, 0) < 4
    return (
        jnp.where(first, low, pltpu.roll(high, 4, 0)),
        jnp.where(first, pltpu.roll(low, 4, 0), high),
    )


def plane_place():
    return lax.rem(lax.axis_index("wide"), 2) * 2 + lax.axis_index("narrow") // 2


def ring_place(position):
    return position ^ (position >> 1)


def send_blocks(held_ref, out_refs):
    for s, out_ref in enumerate(out_refs):
        out_ref[...] = held_ref[plane_place() ^ s]


def receive_blocks(block_refs, held_ref):
    rows = block_refs[0].shape[0]
    for s, block_ref in enumerate(block_refs):
        start = pl.multiple_of((plane_place() ^ s) * rows, rows)
        held_ref[pl.ds(start, rows), :] = block_ref[...].astype(jnp.float32)


def pack_rows(held_ref, out_ref):
    chans, rows, _ = out_ref.shape
    for c in range(chans):
        out_ref[c] = held_ref[pl.ds(c, rows, stride=chans), :].astype(jnp.bfloat16)


def project_kernel(
    pair_hbm, valid_hbm, gain_hbm, bias_hbm, w_hbm, normed_ref, left_ref, *rest
):
    right_refs, rest = rest[:places], rest[places:]
    right_ref, pair_ref, valid_ref, gain_ref, bias_ref, w_ref, sems = rest
    row_count, col_count, chan_count = pair_ref.shape
    group = chan_count // places
    fetches = [
        pltpu.make_async_copy(source, held, sems.at[i])
        for i, (source, held) in enumerate((
            (pair_hbm, pair_ref), (gain_hbm, gain_ref), (bias_hbm, bias_ref),
            (w_hbm.at[:, : 4 * chan_count], w_ref), (valid_hbm, valid_ref),
        ))
    ]
    for fetch in fetches:
        fetch.start()
    row_start = lax.axis_index(axes) * row_count
    for fetch in fetches[:3]:
        fetch.wait()
    tokens = pair_ref[...].reshape(row_count * col_count, chan_count).astype(jnp.float32)
    normed = layer_norm(tokens, gain_ref[...], bias_ref[...], 1).astype(jnp.bfloat16)
    normed_ref[...] = normed
    for fetch in fetches[3:]:
        fetch.wait()
    col_flags = valid_ref[...].astype(jnp.float32)
    columns = lax.broadcasted_iota(jnp.int32, col_flags.shape, 1)
    row_flags = [
        jnp.sum(jnp.where(columns == row_start + r, col_flags, 0.0), axis=1, keepdims=True)
        for r in range(row_count)
    ]
    flags = jnp.concatenate([col_flags * row_flag for row_flag in row_flags], axis=1)
    for first, out_ref in ((2, right_ref), (0, left_ref)):
        projected = lax.dot_general(
            w_ref[:, first * chan_count : (first + 2) * chan_count], normed,
            (((0,), (1,)), ((), ())), preferred_element_type=jnp.float32,
        )
        side = jax.nn.sigmoid(projected[:chan_count]) * projected[chan_count:] * flags
        side = side.astype(jnp.bfloat16)
        for place in range(places):
            for r in range(row_count):
                out_ref[place, r * group : (r + 1) * group, :] = side[
                    place * group : (place + 1) * group, r * col_count : (r + 1) * col_count
                ]
    send_blocks(right_ref, right_refs)


def pack_kernel(left_ref, *refs):
    right_refs, (packed_ref, *left_refs), held_ref = refs[:places], refs[places:-1], refs[-1]
    receive_blocks(right_refs, held_ref)
    pack_rows(held_ref, packed_ref)
    send_blocks(left_ref, left_refs)


def contract_kernel(*refs):
    left_refs, right_refs = refs[:places], refs[places : 2 * places + places]
    out_refs, (left_held, packed_ref, out_ref) = refs[3 * places : 4 * places], refs[4 * places :]
    receive_blocks(left_refs, left_held)
    pack_rows(left_held, packed_ref)
    for chan in range(0, packed_ref.shape[0], 4):
        products = [
            lax.dot_general(
                packed_ref[c],
                jnp.concatenate([right_ref[c] for right_ref in right_refs], axis=0),
                (((1,), (1,)), ((), ())),
                preferred_element_type=jnp.float32,
            )
            for c in range(chan, chan + 4)
        ]
        for row in range(0, packed_ref.shape[1], 8):
            pieces = [product[row : row + 8] for product in products]
            low, high = swap_halves(pieces[0], pieces[1]), swap_halves(pieces[2], pieces[3])
            for half in range(2):
                rows = jnp.concatenate([low[half], high[half]], axis=0).astype(jnp.bfloat16)
                out_ref[row // 4 + half, chan * 4 : (chan + 4) * 4, :] = rows
    send_blocks(out_ref, out_refs)


def gate_kernel(normed_ref, w_ref, gain_ref, bias_ref, w_out_ref, out_ref, scales_ref, weights_ref):
    chan_count = normed_ref.shape[1]
    projected = jnp.dot(
        normed_ref[...], w_ref[:, 4 * chan_count :], preferred_element_type=jnp.float32
    )
    out_ref[...] = jax.nn.sigmoid(projected).astype(jnp.bfloat16)
    for i, vector_ref in enumerate((gain_ref, bias_ref)):
        scales_ref[i] = jnp.transpose(jnp.broadcast_to(vector_ref[...], scales_ref.shape[1:]))
    weights_ref[...] = w_out_ref[...]


def finish_kernel(gate_ref, scales_ref, w_ref, *refs):
    block_refs, out_ref, held_ref = refs[:places], refs[places], refs[places + 1]
    row_count, col_count, chan_count = out_ref.shape
    receive_blocks(block_refs, held_ref)
    plane_rows = 2 * places * row_count
    planes = col_count // plane_rows
    position = ring_place(lax.axis_index("wide") // 2)
    even_core = lax.rem(lax.axis_index("narrow"), 2) == 0
    for r in range(row_count):
        triangle = held_ref[pl.ds(r, chan_count, stride=row_count), :]
        normed = layer_norm(triangle, scales_ref[0], scales_ref[1], 0).astype(jnp.bfloat16)
        result = lax.dot_general(
            normed, w_ref[...], (((0,), (0,)), ((), ())), preferred_element_type=jnp.float32
        )
        for step in range(planes):
            own, other = (
                result[step * plane_rows + i * plane_rows // 2 :][: plane_rows // 2] for i in range(2)
            )
            low, high = jnp.where(even_core, own, other), jnp.where(even_core, other, own)
            rows = []
            for row in range(0, plane_rows // 2, 8):
                rows.extend(swap_halves(low[row : row + 8], high[row : row + 8]))
            rows = jnp.concatenate(rows, axis=0)
            plane = ring_place(lax.rem(position + planes - step, planes))
            start = pl.multiple_of(plane * plane_rows, plane_rows)
            gate = gate_ref[r, pl.ds(start, plane_rows), :].astype(jnp.float32)
            out_ref[r, pl.ds(start, plane_rows), :] = (gate * rows).astype(jnp.bfloat16)


def exchange(blocks, shards):
    return [
        lax.ppermute(block, axes, [(i, i ^ (2 * s)) for i in range(shards)]) if s else block
        for s, block in enumerate(blocks)
    ]


def to_other_core(block, shards):
    return lax.ppermute(block, axes, [(i, i ^ 1) for i in range(shards)])


def to_next_plane(block, shards):
    size = 2 * places
    planes = shards // size
    perm = []
    for position in range(planes):
        here, there = ring_place(position), ring_place((position + 1) % planes)
        perm.extend((here * size + q, there * size + q) for q in range(size))
    return lax.ppermute(block, axes, perm)


def local_blocks(pair, valid, norm_gain, norm_bias, w_proj, out_gain, out_bias, w_out):
    row_count, col_count, chan_count = pair.shape
    shards = lax.axis_size(axes)
    tokens = row_count * col_count
    vmem = pl.BlockSpec(memory_space=pltpu.VMEM)
    hbm = pl.BlockSpec(memory_space=pltpu.HBM)

    def line(vector):
        return vector.reshape(1, -1)

    def shaped(*dims):
        return jax.ShapeDtypeStruct(dims, jnp.bfloat16)

    group = chan_count // places
    block = shaped(row_count * group, col_count)
    packed = shaped(group, places * row_count, col_count)
    limit = pltpu.CompilerParams(vmem_limit_bytes=kernel_vmem)
    held_blocks = pltpu.VMEM((places,) + block.shape, jnp.bfloat16)
    held_rows = pltpu.VMEM((places * block.shape[0], col_count), jnp.float32)

    normed, left, *right = pl.pallas_call(
        project_kernel,
        out_shape=[shaped(tokens, chan_count), shaped(places, *block.shape)] + [block] * places,
        in_specs=[hbm] * 5,
        out_specs=[vmem] * (2 + places),
        scratch_shapes=[
            held_blocks,
            pltpu.VMEM(pair.shape, jnp.bfloat16),
            pltpu.VMEM((1, col_count), jnp.int32),
            pltpu.VMEM((1, chan_count), jnp.float32),
            pltpu.VMEM((1, chan_count), jnp.float32),
            pltpu.VMEM((chan_count, 4 * chan_count), jnp.bfloat16),
            pltpu.SemaphoreType.DMA((5,)),
        ],
        name="project",
    )(pair, line(valid), line(norm_gain), line(norm_bias), w_proj)
    right, *left = pl.pallas_call(
        pack_kernel,
        out_shape=[packed] + [block] * places,
        in_specs=[vmem] * (1 + places),
        out_specs=[vmem] * (1 + places),
        scratch_shapes=[held_rows],
        compiler_params=limit,
        name="pack",
    )(left, *exchange(right, shards))
    rights = []
    for step in range(shards // (2 * places)):
        if step:
            right = to_next_plane(right, shards)
        rights += [right, to_other_core(right, shards)]
    left = exchange(left, shards)
    triangle = pl.pallas_call(
        contract_kernel,
        out_shape=[block] * places,
        in_specs=[vmem] * (places + len(rights)),
        out_specs=[vmem] * places,
        scratch_shapes=[held_rows, pltpu.VMEM(packed.shape, jnp.bfloat16), held_blocks],
        compiler_params=limit,
        name="contract",
    )(*left, *rights)
    triangle = exchange(triangle, shards)
    gate_values, scales, weights = pl.pallas_call(
        gate_kernel,
        out_shape=(
            shaped(tokens, chan_count),
            jax.ShapeDtypeStruct((2, chan_count, col_count), jnp.float32),
            shaped(chan_count, chan_count),
        ),
        in_specs=[vmem] * 5,
        out_specs=(vmem,) * 3,
        compiler_params=limit,
        name="gate",
    )(normed, w_proj, line(out_gain), line(out_bias), w_out)
    return pl.pallas_call(
        finish_kernel,
        out_shape=shaped(row_count, col_count, chan_count),
        in_specs=[vmem] * (3 + places),
        out_specs=vmem,
        scratch_shapes=[held_rows],
        compiler_params=limit,
        name="finish",
    )(gate_values.reshape(pair.shape), scales, weights, *triangle)


def local_arrays(pair, valid, norm_gain, norm_bias, w_proj, out_gain, out_bias, w_out):
    row_count, col_count, chan_count = pair.shape
    row_start = lax.axis_index(("wide", "narrow")) * row_count
    col_start = lax.axis_index("sub") * col_count
    row_flags = lax.dynamic_slice_in_dim(valid, row_start, row_count, 0).astype(jnp.float32)
    col_flags = lax.dynamic_slice_in_dim(valid, col_start, col_count, 0).astype(jnp.float32)
    pair_flags = row_flags[:, None] * col_flags[None, :]
    normed = layer_norm(pair.astype(jnp.float32), norm_gain, norm_bias, 2).astype(jnp.bfloat16)
    projected = jnp.einsum(
        "rkc,cd->drk", normed, w_proj[:, : 4 * chan_count], preferred_element_type=jnp.float32
    )
    left_side = (
        jax.nn.sigmoid(projected[:chan_count]) * projected[chan_count : 2 * chan_count] * pair_flags
    ).astype(jnp.bfloat16)
    right_side = (
        jax.nn.sigmoid(projected[2 * chan_count : 3 * chan_count])
        * projected[3 * chan_count :]
        * pair_flags
    ).astype(jnp.bfloat16)
    gate_values = jax.nn.sigmoid(
        jnp.einsum(
            "rkc,cd->rkd", normed, w_proj[:, 4 * chan_count :], preferred_element_type=jnp.float32
        )
    ).astype(jnp.bfloat16)
    both_sides = jnp.stack([left_side, right_side], axis=1)
    both_group = lax.all_to_all(
        both_sides, ("wide", "narrow"), split_axis=0, concat_axis=2, tiled=True
    )
    left_group, right_group = both_group[:, 0], both_group[:, 1]
    partial_sums = jnp.einsum(
        "cik,cjk->cij", left_group, right_group, preferred_element_type=jnp.float32
    )
    summed = lax.psum_scatter(partial_sums, "sub", scatter_dimension=2, tiled=True).astype(
        jnp.bfloat16
    )
    returned = lax.all_to_all(summed, ("wide", "narrow"), split_axis=1, concat_axis=0, tiled=True)
    normed_out = layer_norm(
        returned.astype(jnp.float32), out_gain[:, None, None], out_bias[:, None, None], 0
    ).astype(jnp.bfloat16)
    result_out = jnp.einsum("crj,cd->rjd", normed_out, w_out, preferred_element_type=jnp.float32)
    return (gate_values.astype(jnp.float32) * result_out).astype(jnp.bfloat16)


def local(pair, *rest):
    row_count, col_count, chan_count = pair.shape
    fits = (
        lax.axis_size("sub") == 1
        and (lax.axis_size("wide"), lax.axis_size("narrow")) == (8, 4)
        and (row_count, col_count, chan_count) == (4, 128, 128)
    )
    return (local_blocks if fits else local_arrays)(pair, *rest)


def solution(mesh):
    in_specs = (
        P(("parts", "wide", "narrow"), "sub", None),
        P("parts"),
        P(),
        P(),
        P(),
        P(),
        P(),
        P(),
    )
    out_specs = P(("parts", "wide", "narrow"), "sub", None)
    return jax.shard_map(local, mesh=mesh, in_specs=in_specs, out_specs=out_specs, check_vma=False)
```

```python
import functools

import jax
import jax.numpy as jnp
from jax import lax
from jax.experimental import pallas as pl
from jax.experimental.pallas import tpu as pltpu
from jax.sharding import PartitionSpec as P

epsilon = 1e-05
axes = ("wide", "narrow")
kernel_vmem = 8 * 2**20
hub = 8


def layer_norm(values, gain_vec, bias_vec, axis_dim):
    average = jnp.mean(values, axis=axis_dim, keepdims=True)
    centered = values - average
    variance = jnp.mean(centered * centered, axis=axis_dim, keepdims=True)
    return centered * lax.rsqrt(variance + epsilon) * gain_vec + bias_vec


def swap_halves(low, high):
    first = lax.broadcasted_iota(jnp.int32, low.shape, 0) < 4
    return (
        jnp.where(first, low, pltpu.roll(high, 4, 0)),
        jnp.where(first, pltpu.roll(low, 4, 0), high),
    )


def project_kernel(
    pair_hbm, valid_hbm, gain_hbm, bias_hbm, w_hbm, out_ref, normed_ref,
    pair_ref, valid_ref, gain_ref, bias_ref, w_ref, sems,
):
    row_count, col_count, chan_count = pair_ref.shape
    fetches = [
        pltpu.make_async_copy(source, held, sems.at[i])
        for i, (source, held) in enumerate((
            (pair_hbm, pair_ref), (gain_hbm, gain_ref), (bias_hbm, bias_ref),
            (w_hbm.at[:, : 4 * chan_count], w_ref), (valid_hbm, valid_ref),
        ))
    ]
    for fetch in fetches:
        fetch.start()
    row_start = lax.axis_index(axes) * row_count
    for fetch in fetches[:3]:
        fetch.wait()
    tokens = pair_ref[...].reshape(row_count * col_count, chan_count).astype(jnp.float32)
    normed = layer_norm(tokens, gain_ref[...], bias_ref[...], 1).astype(jnp.bfloat16)
    normed_ref[...] = normed
    for fetch in fetches[3:]:
        fetch.wait()
    projected = lax.dot_general(
        w_ref[...], normed, (((0,), (1,)), ((), ())),
        preferred_element_type=jnp.float32,
    )
    col_flags = valid_ref[...].astype(jnp.float32)
    places = lax.broadcasted_iota(jnp.int32, col_flags.shape, 1)
    row_flags = [
        jnp.sum(jnp.where(places == row_start + r, col_flags, 0.0), axis=1, keepdims=True)
        for r in range(row_count)
    ]
    flags = jnp.concatenate([col_flags * row_flag for row_flag in row_flags], axis=1)
    for chan in range(0, chan_count, 8):
        a_gate, a, b_gate, b = (
            projected[i * chan_count + chan : i * chan_count + chan + 8] for i in range(4)
        )
        left = jax.nn.sigmoid(a_gate) * a * flags
        right = jax.nn.sigmoid(b_gate) * b * flags
        for half, block in enumerate(swap_halves(left, right)):
            for r in range(0, row_count, 2):
                rows = jnp.concatenate(
                    [block[:, (r + i) * col_count : (r + i + 1) * col_count] for i in range(2)], axis=0
                )
                out_ref[(chan // 4 + half) ^ hub, r * 8 : (r + 2) * 8, :] = rows.astype(jnp.bfloat16)


def receive_blocks(blocks_ref, held_ref):
    shards, rows, _ = blocks_ref.shape
    for i in range(shards):
        held_ref[(i ^ hub) * rows : ((i ^ hub) + 1) * rows, :] = blocks_ref[i].astype(jnp.float32)


def exchange(blocks):
    groups = [[i ^ hub for i in range(blocks.shape[0])]]
    return lax.all_to_all(
        blocks, axes, split_axis=0, concat_axis=0, axis_index_groups=groups, tiled=True
    )


def contract_kernel(blocks_ref, out_ref, held_ref):
    total = held_ref.shape[0] // 8
    receive_blocks(blocks_ref, held_ref)
    products = []
    for c in range(4):
        left = held_ref[pl.ds(c, total, stride=8), :].astype(jnp.bfloat16)
        right = held_ref[pl.ds(4 + c, total, stride=8), :].astype(jnp.bfloat16)
        products.append(
            lax.dot_general(
                left, right, (((1,), (1,)), ((), ())), preferred_element_type=jnp.float32
            )
        )
    for row in range(0, total, 8):
        pieces = [product[row : row + 8] for product in products]
        low, high = swap_halves(pieces[0], pieces[1]), swap_halves(pieces[2], pieces[3])
        for half in range(2):
            rows = jnp.concatenate([low[half], high[half]], axis=0)
            out_ref[(row // 4 + half) ^ hub] = rows.astype(jnp.bfloat16)


def gate_kernel(normed_ref, w_ref, gain_ref, bias_ref, w_out_ref, out_ref, scales_ref, weights_ref):
    chan_count = normed_ref.shape[1]
    projected = jnp.dot(
        normed_ref[...], w_ref[:, 4 * chan_count :], preferred_element_type=jnp.float32
    )
    out_ref[...] = jax.nn.sigmoid(projected).astype(jnp.bfloat16)
    for i, vector_ref in enumerate((gain_ref, bias_ref)):
        scales_ref[i] = jnp.transpose(jnp.broadcast_to(vector_ref[...], scales_ref.shape[1:]))
    weights_ref[...] = w_out_ref[...]


def finish_kernel(blocks_ref, gate_ref, scales_ref, w_ref, out_ref, held_ref):
    row_count, col_count, chan_count = out_ref.shape
    receive_blocks(blocks_ref, held_ref)
    for r in range(row_count):
        triangle = held_ref[pl.ds(r, chan_count, stride=row_count), :]
        normed = layer_norm(triangle, scales_ref[0], scales_ref[1], 0).astype(jnp.bfloat16)
        result = lax.dot_general(
            normed, w_ref[...], (((0,), (0,)), ((), ())), preferred_element_type=jnp.float32
        )
        gate = gate_ref[r * col_count : (r + 1) * col_count, :].astype(jnp.float32)
        out_ref[r] = (gate * result).astype(jnp.bfloat16)


def local_blocks(pair, valid, norm_gain, norm_bias, w_proj, out_gain, out_bias, w_out):
    row_count, col_count, chan_count = pair.shape
    shards = lax.axis_size(axes)
    tokens = row_count * col_count
    vmem = pl.BlockSpec(memory_space=pltpu.VMEM)
    hbm = pl.BlockSpec(memory_space=pltpu.HBM)

    def line(vector):
        return vector.reshape(1, -1)

    def shaped(*dims):
        return jax.ShapeDtypeStruct(dims, jnp.bfloat16)

    sides, normed = pl.pallas_call(
        project_kernel,
        out_shape=(shaped(shards, 8 * row_count, col_count), shaped(tokens, chan_count)),
        in_specs=[hbm] * 5,
        out_specs=(vmem, vmem),
        scratch_shapes=[
            pltpu.VMEM(pair.shape, jnp.bfloat16),
            pltpu.VMEM((1, col_count), jnp.int32),
            pltpu.VMEM((1, chan_count), jnp.float32),
            pltpu.VMEM((1, chan_count), jnp.float32),
            pltpu.VMEM((chan_count, 4 * chan_count), jnp.bfloat16),
            pltpu.SemaphoreType.DMA((5,)),
        ],
        name="project",
    )(pair, line(valid), line(norm_gain), line(norm_bias), w_proj)
    sides = exchange(sides)
    triangle = pl.pallas_call(
        contract_kernel,
        out_shape=shaped(shards, 4 * row_count, col_count),
        in_specs=[vmem],
        out_specs=vmem,
        scratch_shapes=[pltpu.VMEM((8 * col_count, col_count), jnp.float32)],
        compiler_params=pltpu.CompilerParams(vmem_limit_bytes=kernel_vmem),
        name="contract",
    )(sides)
    triangle = exchange(triangle)
    gate_values, scales, weights = pl.pallas_call(
        gate_kernel,
        out_shape=(
            shaped(tokens, chan_count),
            jax.ShapeDtypeStruct((2, chan_count, col_count), jnp.float32),
            shaped(chan_count, chan_count),
        ),
        in_specs=[vmem] * 5,
        out_specs=(vmem,) * 3,
        compiler_params=pltpu.CompilerParams(vmem_limit_bytes=kernel_vmem),
        name="gate",
    )(normed, w_proj, line(out_gain), line(out_bias), w_out)
    return pl.pallas_call(
        finish_kernel,
        out_shape=shaped(row_count, col_count, chan_count),
        in_specs=[vmem] * 4,
        out_specs=vmem,
        scratch_shapes=[pltpu.VMEM((tokens, chan_count), jnp.float32)],
        compiler_params=pltpu.CompilerParams(vmem_limit_bytes=kernel_vmem),
        name="finish",
    )(triangle, gate_values, scales, weights)


def local_arrays(pair, valid, norm_gain, norm_bias, w_proj, out_gain, out_bias, w_out):
    row_count, col_count, chan_count = pair.shape
    row_start = lax.axis_index(("wide", "narrow")) * row_count
    col_start = lax.axis_index("sub") * col_count
    row_flags = lax.dynamic_slice_in_dim(valid, row_start, row_count, 0).astype(jnp.float32)
    col_flags = lax.dynamic_slice_in_dim(valid, col_start, col_count, 0).astype(jnp.float32)
    pair_flags = row_flags[:, None] * col_flags[None, :]
    normed = layer_norm(pair.astype(jnp.float32), norm_gain, norm_bias, 2).astype(jnp.bfloat16)
    projected = jnp.einsum(
        "rkc,cd->drk", normed, w_proj[:, : 4 * chan_count], preferred_element_type=jnp.float32
    )
    left_side = (
        jax.nn.sigmoid(projected[:chan_count]) * projected[chan_count : 2 * chan_count] * pair_flags
    ).astype(jnp.bfloat16)
    right_side = (
        jax.nn.sigmoid(projected[2 * chan_count : 3 * chan_count])
        * projected[3 * chan_count :]
        * pair_flags
    ).astype(jnp.bfloat16)
    gate_values = jax.nn.sigmoid(
        jnp.einsum(
            "rkc,cd->rkd", normed, w_proj[:, 4 * chan_count :], preferred_element_type=jnp.float32
        )
    ).astype(jnp.bfloat16)
    both_sides = jnp.stack([left_side, right_side], axis=1)
    both_group = lax.all_to_all(
        both_sides, ("wide", "narrow"), split_axis=0, concat_axis=2, tiled=True
    )
    left_group, right_group = both_group[:, 0], both_group[:, 1]
    partial_sums = jnp.einsum(
        "cik,cjk->cij", left_group, right_group, preferred_element_type=jnp.float32
    )
    summed = lax.psum_scatter(partial_sums, "sub", scatter_dimension=2, tiled=True).astype(
        jnp.bfloat16
    )
    returned = lax.all_to_all(summed, ("wide", "narrow"), split_axis=1, concat_axis=0, tiled=True)
    normed_out = layer_norm(
        returned.astype(jnp.float32), out_gain[:, None, None], out_bias[:, None, None], 0
    ).astype(jnp.bfloat16)
    result_out = jnp.einsum("crj,cd->rjd", normed_out, w_out, preferred_element_type=jnp.float32)
    return (gate_values.astype(jnp.float32) * result_out).astype(jnp.bfloat16)


def local(pair, *rest):
    row_count, col_count, chan_count = pair.shape
    shards = lax.axis_size(axes)
    fits = (
        lax.axis_size("sub") == 1
        and (row_count, col_count, chan_count) == (4, 128, 128)
        and shards * row_count == col_count
        and shards * 4 == chan_count
        and shards % (2 * hub) == 0
    )
    return (local_blocks if fits else local_arrays)(pair, *rest)


def solution(mesh):
    in_specs = (
        P(("parts", "wide", "narrow"), "sub", None),
        P("parts"),
        P(),
        P(),
        P(),
        P(),
        P(),
        P(),
    )
    out_specs = P(("parts", "wide", "narrow"), "sub", None)
    return jax.shard_map(local, mesh=mesh, in_specs=in_specs, out_specs=out_specs, check_vma=False)
```

```python
import functools

import jax
import jax.numpy as jnp
from jax import lax
from jax.experimental import pallas as pl
from jax.experimental.pallas import tpu as pltpu
from jax.sharding import PartitionSpec as P

epsilon = 1e-05
axes = ("wide", "narrow")
kernel_vmem = 8 * 2**20
hub = 31


def layer_norm(values, gain_vec, bias_vec, axis_dim):
    average = jnp.mean(values, axis=axis_dim, keepdims=True)
    centered = values - average
    variance = jnp.mean(centered * centered, axis=axis_dim, keepdims=True)
    return centered * lax.rsqrt(variance + epsilon) * gain_vec + bias_vec


def swap_halves(low, high):
    first = lax.broadcasted_iota(jnp.int32, low.shape, 0) < 4
    return (
        jnp.where(first, low, pltpu.roll(high, 4, 0)),
        jnp.where(first, pltpu.roll(low, 4, 0), high),
    )


def project_kernel(
    pair_hbm, valid_hbm, gain_hbm, bias_hbm, w_hbm, out_ref, normed_ref,
    pair_ref, valid_ref, gain_ref, bias_ref, w_ref, sems,
):
    row_count, col_count, chan_count = pair_ref.shape
    fetches = [
        pltpu.make_async_copy(source, held, sems.at[i])
        for i, (source, held) in enumerate((
            (pair_hbm, pair_ref), (gain_hbm, gain_ref), (bias_hbm, bias_ref),
            (w_hbm.at[:, : 4 * chan_count], w_ref), (valid_hbm, valid_ref),
        ))
    ]
    for fetch in fetches:
        fetch.start()
    row_start = lax.axis_index(axes) * row_count
    for fetch in fetches[:3]:
        fetch.wait()
    tokens = pair_ref[...].reshape(row_count * col_count, chan_count).astype(jnp.float32)
    normed = layer_norm(tokens, gain_ref[...], bias_ref[...], 1).astype(jnp.bfloat16)
    normed_ref[...] = normed
    for fetch in fetches[3:]:
        fetch.wait()
    projected = lax.dot_general(
        w_ref[...], normed, (((0,), (1,)), ((), ())),
        preferred_element_type=jnp.float32,
    )
    col_flags = valid_ref[...].astype(jnp.float32)
    places = lax.broadcasted_iota(jnp.int32, col_flags.shape, 1)
    row_flags = [
        jnp.sum(jnp.where(places == row_start + r, col_flags, 0.0), axis=1, keepdims=True)
        for r in range(row_count)
    ]
    flags = jnp.concatenate([col_flags * row_flag for row_flag in row_flags], axis=1)
    for chan in range(0, chan_count, 8):
        a_gate, a, b_gate, b = (
            projected[i * chan_count + chan : i * chan_count + chan + 8] for i in range(4)
        )
        left = jax.nn.sigmoid(a_gate) * a * flags
        right = jax.nn.sigmoid(b_gate) * b * flags
        for half, block in enumerate(swap_halves(left, right)):
            for r in range(0, row_count, 2):
                rows = jnp.concatenate(
                    [block[:, (r + i) * col_count : (r + i + 1) * col_count] for i in range(2)], axis=0
                )
                out_ref[(chan // 4 + half) ^ hub, r * 8 : (r + 2) * 8, :] = rows.astype(jnp.bfloat16)


def receive_blocks(blocks_ref, held_ref):
    shards, rows, _ = blocks_ref.shape
    for i in range(shards):
        held_ref[(i ^ hub) * rows : ((i ^ hub) + 1) * rows, :] = blocks_ref[i].astype(jnp.float32)


def exchange(blocks):
    groups = [[i ^ hub for i in range(blocks.shape[0])]]
    return lax.all_to_all(
        blocks, axes, split_axis=0, concat_axis=0, axis_index_groups=groups, tiled=True
    )


def contract_kernel(blocks_ref, out_ref, held_ref):
    total = held_ref.shape[0] // 8
    receive_blocks(blocks_ref, held_ref)
    products = []
    for c in range(4):
        left = held_ref[pl.ds(c, total, stride=8), :].astype(jnp.bfloat16)
        right = held_ref[pl.ds(4 + c, total, stride=8), :].astype(jnp.bfloat16)
        products.append(
            lax.dot_general(
                left, right, (((1,), (1,)), ((), ())), preferred_element_type=jnp.float32
            )
        )
    for row in range(0, total, 8):
        pieces = [product[row : row + 8] for product in products]
        low, high = swap_halves(pieces[0], pieces[1]), swap_halves(pieces[2], pieces[3])
        for half in range(2):
            rows = jnp.concatenate([low[half], high[half]], axis=0)
            out_ref[(row // 4 + half) ^ hub] = rows.astype(jnp.bfloat16)


def gate_kernel(normed_ref, w_ref, gain_ref, bias_ref, w_out_ref, out_ref, scales_ref, weights_ref):
    chan_count = normed_ref.shape[1]
    projected = jnp.dot(
        normed_ref[...], w_ref[:, 4 * chan_count :], preferred_element_type=jnp.float32
    )
    out_ref[...] = jax.nn.sigmoid(projected).astype(jnp.bfloat16)
    for i, vector_ref in enumerate((gain_ref, bias_ref)):
        scales_ref[i] = jnp.transpose(jnp.broadcast_to(vector_ref[...], scales_ref.shape[1:]))
    weights_ref[...] = w_out_ref[...]


def finish_kernel(blocks_ref, gate_ref, scales_ref, w_ref, out_ref, held_ref):
    row_count, col_count, chan_count = out_ref.shape
    receive_blocks(blocks_ref, held_ref)
    for r in range(row_count):
        triangle = held_ref[pl.ds(r, chan_count, stride=row_count), :]
        normed = layer_norm(triangle, scales_ref[0], scales_ref[1], 0).astype(jnp.bfloat16)
        result = lax.dot_general(
            normed, w_ref[...], (((0,), (0,)), ((), ())), preferred_element_type=jnp.float32
        )
        gate = gate_ref[r * col_count : (r + 1) * col_count, :].astype(jnp.float32)
        out_ref[r] = (gate * result).astype(jnp.bfloat16)


def local_blocks(pair, valid, norm_gain, norm_bias, w_proj, out_gain, out_bias, w_out):
    row_count, col_count, chan_count = pair.shape
    shards = lax.axis_size(axes)
    tokens = row_count * col_count
    vmem = pl.BlockSpec(memory_space=pltpu.VMEM)
    hbm = pl.BlockSpec(memory_space=pltpu.HBM)

    def line(vector):
        return vector.reshape(1, -1)

    def shaped(*dims):
        return jax.ShapeDtypeStruct(dims, jnp.bfloat16)

    sides, normed = pl.pallas_call(
        project_kernel,
        out_shape=(shaped(shards, 8 * row_count, col_count), shaped(tokens, chan_count)),
        in_specs=[hbm] * 5,
        out_specs=(vmem, vmem),
        scratch_shapes=[
            pltpu.VMEM(pair.shape, jnp.bfloat16),
            pltpu.VMEM((1, col_count), jnp.int32),
            pltpu.VMEM((1, chan_count), jnp.float32),
            pltpu.VMEM((1, chan_count), jnp.float32),
            pltpu.VMEM((chan_count, 4 * chan_count), jnp.bfloat16),
            pltpu.SemaphoreType.DMA((5,)),
        ],
        name="project",
    )(pair, line(valid), line(norm_gain), line(norm_bias), w_proj)
    sides = exchange(sides)
    triangle = pl.pallas_call(
        contract_kernel,
        out_shape=shaped(shards, 4 * row_count, col_count),
        in_specs=[vmem],
        out_specs=vmem,
        scratch_shapes=[pltpu.VMEM((8 * col_count, col_count), jnp.float32)],
        compiler_params=pltpu.CompilerParams(vmem_limit_bytes=kernel_vmem),
        name="contract",
    )(sides)
    triangle = exchange(triangle)
    gate_values, scales, weights = pl.pallas_call(
        gate_kernel,
        out_shape=(
            shaped(tokens, chan_count),
            jax.ShapeDtypeStruct((2, chan_count, col_count), jnp.float32),
            shaped(chan_count, chan_count),
        ),
        in_specs=[vmem] * 5,
        out_specs=(vmem,) * 3,
        compiler_params=pltpu.CompilerParams(vmem_limit_bytes=kernel_vmem),
        name="gate",
    )(normed, w_proj, line(out_gain), line(out_bias), w_out)
    return pl.pallas_call(
        finish_kernel,
        out_shape=shaped(row_count, col_count, chan_count),
        in_specs=[vmem] * 4,
        out_specs=vmem,
        scratch_shapes=[pltpu.VMEM((tokens, chan_count), jnp.float32)],
        compiler_params=pltpu.CompilerParams(vmem_limit_bytes=kernel_vmem),
        name="finish",
    )(triangle, gate_values, scales, weights)


def local_arrays(pair, valid, norm_gain, norm_bias, w_proj, out_gain, out_bias, w_out):
    row_count, col_count, chan_count = pair.shape
    row_start = lax.axis_index(("wide", "narrow")) * row_count
    col_start = lax.axis_index("sub") * col_count
    row_flags = lax.dynamic_slice_in_dim(valid, row_start, row_count, 0).astype(jnp.float32)
    col_flags = lax.dynamic_slice_in_dim(valid, col_start, col_count, 0).astype(jnp.float32)
    pair_flags = row_flags[:, None] * col_flags[None, :]
    normed = layer_norm(pair.astype(jnp.float32), norm_gain, norm_bias, 2).astype(jnp.bfloat16)
    projected = jnp.einsum(
        "rkc,cd->drk", normed, w_proj[:, : 4 * chan_count], preferred_element_type=jnp.float32
    )
    left_side = (
        jax.nn.sigmoid(projected[:chan_count]) * projected[chan_count : 2 * chan_count] * pair_flags
    ).astype(jnp.bfloat16)
    right_side = (
        jax.nn.sigmoid(projected[2 * chan_count : 3 * chan_count])
        * projected[3 * chan_count :]
        * pair_flags
    ).astype(jnp.bfloat16)
    gate_values = jax.nn.sigmoid(
        jnp.einsum(
            "rkc,cd->rkd", normed, w_proj[:, 4 * chan_count :], preferred_element_type=jnp.float32
        )
    ).astype(jnp.bfloat16)
    both_sides = jnp.stack([left_side, right_side], axis=1)
    both_group = lax.all_to_all(
        both_sides, ("wide", "narrow"), split_axis=0, concat_axis=2, tiled=True
    )
    left_group, right_group = both_group[:, 0], both_group[:, 1]
    partial_sums = jnp.einsum(
        "cik,cjk->cij", left_group, right_group, preferred_element_type=jnp.float32
    )
    summed = lax.psum_scatter(partial_sums, "sub", scatter_dimension=2, tiled=True).astype(
        jnp.bfloat16
    )
    returned = lax.all_to_all(summed, ("wide", "narrow"), split_axis=1, concat_axis=0, tiled=True)
    normed_out = layer_norm(
        returned.astype(jnp.float32), out_gain[:, None, None], out_bias[:, None, None], 0
    ).astype(jnp.bfloat16)
    result_out = jnp.einsum("crj,cd->rjd", normed_out, w_out, preferred_element_type=jnp.float32)
    return (gate_values.astype(jnp.float32) * result_out).astype(jnp.bfloat16)


def local(pair, *rest):
    row_count, col_count, chan_count = pair.shape
    shards = lax.axis_size(axes)
    fits = (
        lax.axis_size("sub") == 1
        and (row_count, col_count, chan_count) == (4, 128, 128)
        and shards * row_count == col_count
        and shards * 4 == chan_count
        and shards == hub + 1
    )
    return (local_blocks if fits else local_arrays)(pair, *rest)


def solution(mesh):
    in_specs = (
        P(("parts", "wide", "narrow"), "sub", None),
        P("parts"),
        P(),
        P(),
        P(),
        P(),
        P(),
        P(),
    )
    out_specs = P(("parts", "wide", "narrow"), "sub", None)
    return jax.shard_map(local, mesh=mesh, in_specs=in_specs, out_specs=out_specs, check_vma=False)
```

```python
import functools

import jax
import jax.numpy as jnp
from jax import lax
from jax.experimental import pallas as pl
from jax.experimental.pallas import tpu as pltpu
from jax.sharding import PartitionSpec as P

epsilon = 1e-05
axes = ("wide", "narrow")
kernel_vmem = 8 * 2**20
planes = 4


def layer_norm(values, gain_vec, bias_vec, axis_dim):
    average = jnp.mean(values, axis=axis_dim, keepdims=True)
    centered = values - average
    variance = jnp.mean(centered * centered, axis=axis_dim, keepdims=True)
    return centered * lax.rsqrt(variance + epsilon) * gain_vec + bias_vec


def swap_halves(low, high):
    first = lax.broadcasted_iota(jnp.int32, low.shape, 0) < 4
    return (
        jnp.where(first, low, pltpu.roll(high, 4, 0)),
        jnp.where(first, pltpu.roll(low, 4, 0), high),
    )


def project_kernel(
    pair_hbm, valid_hbm, gain_hbm, bias_hbm, w_hbm, out_ref, normed_ref,
    pair_ref, valid_ref, gain_ref, bias_ref, w_ref, sems,
):
    row_count, col_count, chan_count = pair_ref.shape
    shards = out_ref.shape[0]
    fetches = [
        pltpu.make_async_copy(source, held, sems.at[i])
        for i, (source, held) in enumerate((
            (pair_hbm, pair_ref), (gain_hbm, gain_ref), (bias_hbm, bias_ref),
            (w_hbm.at[:, : 4 * chan_count], w_ref), (valid_hbm, valid_ref),
        ))
    ]
    for fetch in fetches:
        fetch.start()
    row_start = lax.axis_index(axes) * row_count
    for fetch in fetches[:3]:
        fetch.wait()
    tokens = pair_ref[...].reshape(row_count * col_count, chan_count).astype(jnp.float32)
    normed = layer_norm(tokens, gain_ref[...], bias_ref[...], 1).astype(jnp.bfloat16)
    normed_ref[...] = normed
    for fetch in fetches[3:]:
        fetch.wait()
    projected = lax.dot_general(
        w_ref[...], normed, (((0,), (1,)), ((), ())),
        preferred_element_type=jnp.float32,
    )
    col_flags = valid_ref[...].astype(jnp.float32)
    places = lax.broadcasted_iota(jnp.int32, col_flags.shape, 1)
    row_flags = [
        jnp.sum(jnp.where(places == row_start + r, col_flags, 0.0), axis=1, keepdims=True)
        for r in range(row_count)
    ]
    flags = jnp.concatenate([col_flags * row_flag for row_flag in row_flags], axis=1)
    for chan in range(0, chan_count, 8):
        a_gate, a, b_gate, b = (
            projected[i * chan_count + chan : i * chan_count + chan + 8] for i in range(4)
        )
        left = jax.nn.sigmoid(a_gate) * a * flags
        right = jax.nn.sigmoid(b_gate) * b * flags
        for half, block in enumerate(swap_halves(left, right)):
            for r in range(0, row_count, 2):
                rows = jnp.concatenate(
                    [block[:, (r + i) * col_count : (r + i + 1) * col_count] for i in range(2)], axis=0
                )
                out_ref[spot(chan // 4 + half, shards), r * 8 : (r + 2) * 8, :] = rows.astype(jnp.bfloat16)


def group_order(shards):
    size = shards // planes
    return [plane * size + place for place in range(size) for plane in range(planes)]


def spot(device, shards):
    return group_order(shards).index(device)


def receive_blocks(blocks_ref, held_ref):
    shards, rows, _ = blocks_ref.shape
    for i, device in enumerate(group_order(shards)):
        held_ref[device * rows : (device + 1) * rows, :] = blocks_ref[i].astype(jnp.float32)


def exchange(blocks):
    return lax.all_to_all(
        blocks, axes, split_axis=0, concat_axis=0,
        axis_index_groups=[group_order(blocks.shape[0])], tiled=True,
    )


def contract_kernel(blocks_ref, out_ref, held_ref):
    total = held_ref.shape[0] // 8
    receive_blocks(blocks_ref, held_ref)
    products = []
    for c in range(4):
        left = held_ref[pl.ds(c, total, stride=8), :].astype(jnp.bfloat16)
        right = held_ref[pl.ds(4 + c, total, stride=8), :].astype(jnp.bfloat16)
        products.append(
            lax.dot_general(
                left, right, (((1,), (1,)), ((), ())), preferred_element_type=jnp.float32
            )
        )
    for row in range(0, total, 8):
        pieces = [product[row : row + 8] for product in products]
        low, high = swap_halves(pieces[0], pieces[1]), swap_halves(pieces[2], pieces[3])
        for half in range(2):
            rows = jnp.concatenate([low[half], high[half]], axis=0)
            out_ref[spot(row // 4 + half, out_ref.shape[0])] = rows.astype(jnp.bfloat16)


def gate_kernel(normed_ref, w_ref, gain_ref, bias_ref, w_out_ref, out_ref, scales_ref, weights_ref):
    chan_count = normed_ref.shape[1]
    projected = jnp.dot(
        normed_ref[...], w_ref[:, 4 * chan_count :], preferred_element_type=jnp.float32
    )
    out_ref[...] = jax.nn.sigmoid(projected).astype(jnp.bfloat16)
    for i, vector_ref in enumerate((gain_ref, bias_ref)):
        scales_ref[i] = jnp.transpose(jnp.broadcast_to(vector_ref[...], scales_ref.shape[1:]))
    weights_ref[...] = w_out_ref[...]


def finish_kernel(blocks_ref, gate_ref, scales_ref, w_ref, out_ref, held_ref):
    row_count, col_count, chan_count = out_ref.shape
    receive_blocks(blocks_ref, held_ref)
    for r in range(row_count):
        triangle = held_ref[pl.ds(r, chan_count, stride=row_count), :]
        normed = layer_norm(triangle, scales_ref[0], scales_ref[1], 0).astype(jnp.bfloat16)
        result = lax.dot_general(
            normed, w_ref[...], (((0,), (0,)), ((), ())), preferred_element_type=jnp.float32
        )
        gate = gate_ref[r * col_count : (r + 1) * col_count, :].astype(jnp.float32)
        out_ref[r] = (gate * result).astype(jnp.bfloat16)


def local_blocks(pair, valid, norm_gain, norm_bias, w_proj, out_gain, out_bias, w_out):
    row_count, col_count, chan_count = pair.shape
    shards = lax.axis_size(axes)
    tokens = row_count * col_count
    vmem = pl.BlockSpec(memory_space=pltpu.VMEM)
    hbm = pl.BlockSpec(memory_space=pltpu.HBM)

    def line(vector):
        return vector.reshape(1, -1)

    def shaped(*dims):
        return jax.ShapeDtypeStruct(dims, jnp.bfloat16)

    sides, normed = pl.pallas_call(
        project_kernel,
        out_shape=(shaped(shards, 8 * row_count, col_count), shaped(tokens, chan_count)),
        in_specs=[hbm] * 5,
        out_specs=(vmem, vmem),
        scratch_shapes=[
            pltpu.VMEM(pair.shape, jnp.bfloat16),
            pltpu.VMEM((1, col_count), jnp.int32),
            pltpu.VMEM((1, chan_count), jnp.float32),
            pltpu.VMEM((1, chan_count), jnp.float32),
            pltpu.VMEM((chan_count, 4 * chan_count), jnp.bfloat16),
            pltpu.SemaphoreType.DMA((5,)),
        ],
        name="project",
    )(pair, line(valid), line(norm_gain), line(norm_bias), w_proj)
    sides = exchange(sides)
    triangle = pl.pallas_call(
        contract_kernel,
        out_shape=shaped(shards, 4 * row_count, col_count),
        in_specs=[vmem],
        out_specs=vmem,
        scratch_shapes=[pltpu.VMEM((8 * col_count, col_count), jnp.float32)],
        compiler_params=pltpu.CompilerParams(vmem_limit_bytes=kernel_vmem),
        name="contract",
    )(sides)
    triangle = exchange(triangle)
    gate_values, scales, weights = pl.pallas_call(
        gate_kernel,
        out_shape=(
            shaped(tokens, chan_count),
            jax.ShapeDtypeStruct((2, chan_count, col_count), jnp.float32),
            shaped(chan_count, chan_count),
        ),
        in_specs=[vmem] * 5,
        out_specs=(vmem,) * 3,
        compiler_params=pltpu.CompilerParams(vmem_limit_bytes=kernel_vmem),
        name="gate",
    )(normed, w_proj, line(out_gain), line(out_bias), w_out)
    return pl.pallas_call(
        finish_kernel,
        out_shape=shaped(row_count, col_count, chan_count),
        in_specs=[vmem] * 4,
        out_specs=vmem,
        scratch_shapes=[pltpu.VMEM((tokens, chan_count), jnp.float32)],
        compiler_params=pltpu.CompilerParams(vmem_limit_bytes=kernel_vmem),
        name="finish",
    )(triangle, gate_values, scales, weights)


def local_arrays(pair, valid, norm_gain, norm_bias, w_proj, out_gain, out_bias, w_out):
    row_count, col_count, chan_count = pair.shape
    row_start = lax.axis_index(("wide", "narrow")) * row_count
    col_start = lax.axis_index("sub") * col_count
    row_flags = lax.dynamic_slice_in_dim(valid, row_start, row_count, 0).astype(jnp.float32)
    col_flags = lax.dynamic_slice_in_dim(valid, col_start, col_count, 0).astype(jnp.float32)
    pair_flags = row_flags[:, None] * col_flags[None, :]
    normed = layer_norm(pair.astype(jnp.float32), norm_gain, norm_bias, 2).astype(jnp.bfloat16)
    projected = jnp.einsum(
        "rkc,cd->drk", normed, w_proj[:, : 4 * chan_count], preferred_element_type=jnp.float32
    )
    left_side = (
        jax.nn.sigmoid(projected[:chan_count]) * projected[chan_count : 2 * chan_count] * pair_flags
    ).astype(jnp.bfloat16)
    right_side = (
        jax.nn.sigmoid(projected[2 * chan_count : 3 * chan_count])
        * projected[3 * chan_count :]
        * pair_flags
    ).astype(jnp.bfloat16)
    gate_values = jax.nn.sigmoid(
        jnp.einsum(
            "rkc,cd->rkd", normed, w_proj[:, 4 * chan_count :], preferred_element_type=jnp.float32
        )
    ).astype(jnp.bfloat16)
    both_sides = jnp.stack([left_side, right_side], axis=1)
    both_group = lax.all_to_all(
        both_sides, ("wide", "narrow"), split_axis=0, concat_axis=2, tiled=True
    )
    left_group, right_group = both_group[:, 0], both_group[:, 1]
    partial_sums = jnp.einsum(
        "cik,cjk->cij", left_group, right_group, preferred_element_type=jnp.float32
    )
    summed = lax.psum_scatter(partial_sums, "sub", scatter_dimension=2, tiled=True).astype(
        jnp.bfloat16
    )
    returned = lax.all_to_all(summed, ("wide", "narrow"), split_axis=1, concat_axis=0, tiled=True)
    normed_out = layer_norm(
        returned.astype(jnp.float32), out_gain[:, None, None], out_bias[:, None, None], 0
    ).astype(jnp.bfloat16)
    result_out = jnp.einsum("crj,cd->rjd", normed_out, w_out, preferred_element_type=jnp.float32)
    return (gate_values.astype(jnp.float32) * result_out).astype(jnp.bfloat16)


def local(pair, *rest):
    row_count, col_count, chan_count = pair.shape
    shards = lax.axis_size(axes)
    fits = (
        lax.axis_size("sub") == 1
        and (row_count, col_count, chan_count) == (4, 128, 128)
        and shards * row_count == col_count
        and shards * 4 == chan_count
        and shards % planes == 0
    )
    return (local_blocks if fits else local_arrays)(pair, *rest)


def solution(mesh):
    in_specs = (
        P(("parts", "wide", "narrow"), "sub", None),
        P("parts"),
        P(),
        P(),
        P(),
        P(),
        P(),
        P(),
    )
    out_specs = P(("parts", "wide", "narrow"), "sub", None)
    return jax.shard_map(local, mesh=mesh, in_specs=in_specs, out_specs=out_specs, check_vma=False)
```

```python
import functools

import jax
import jax.numpy as jnp
from jax import lax
from jax.experimental import pallas as pl
from jax.experimental.pallas import tpu as pltpu
from jax.sharding import PartitionSpec as P

epsilon = 1e-05
axes = ("wide", "narrow")
kernel_vmem = 8 * 2**20
planes = 4


def layer_norm(values, gain_vec, bias_vec, axis_dim):
    average = jnp.mean(values, axis=axis_dim, keepdims=True)
    centered = values - average
    variance = jnp.mean(centered * centered, axis=axis_dim, keepdims=True)
    return centered * lax.rsqrt(variance + epsilon) * gain_vec + bias_vec


def swap_halves(low, high):
    first = lax.broadcasted_iota(jnp.int32, low.shape, 0) < 4
    return (
        jnp.where(first, low, pltpu.roll(high, 4, 0)),
        jnp.where(first, pltpu.roll(low, 4, 0), high),
    )


def project_kernel(
    pair_hbm, valid_hbm, gain_hbm, bias_hbm, w_hbm, out_ref, normed_ref,
    pair_ref, valid_ref, gain_ref, bias_ref, w_ref, sems,
):
    row_count, col_count, chan_count = pair_ref.shape
    shards = out_ref.shape[0]
    fetches = [
        pltpu.make_async_copy(source, held, sems.at[i])
        for i, (source, held) in enumerate((
            (pair_hbm, pair_ref), (gain_hbm, gain_ref), (bias_hbm, bias_ref),
            (w_hbm.at[:, : 4 * chan_count], w_ref), (valid_hbm, valid_ref),
        ))
    ]
    for fetch in fetches:
        fetch.start()
    row_start = lax.axis_index(axes) * row_count
    for fetch in fetches[:3]:
        fetch.wait()
    tokens = pair_ref[...].reshape(row_count * col_count, chan_count).astype(jnp.float32)
    normed = layer_norm(tokens, gain_ref[...], bias_ref[...], 1).astype(jnp.bfloat16)
    normed_ref[...] = normed
    for fetch in fetches[3:]:
        fetch.wait()
    projected = lax.dot_general(
        w_ref[...], normed, (((0,), (1,)), ((), ())),
        preferred_element_type=jnp.float32,
    )
    col_flags = valid_ref[...].astype(jnp.float32)
    places = lax.broadcasted_iota(jnp.int32, col_flags.shape, 1)
    row_flags = [
        jnp.sum(jnp.where(places == row_start + r, col_flags, 0.0), axis=1, keepdims=True)
        for r in range(row_count)
    ]
    flags = jnp.concatenate([col_flags * row_flag for row_flag in row_flags], axis=1)
    for chan in range(0, chan_count, 8):
        a_gate, a, b_gate, b = (
            projected[i * chan_count + chan : i * chan_count + chan + 8] for i in range(4)
        )
        left = jax.nn.sigmoid(a_gate) * a * flags
        right = jax.nn.sigmoid(b_gate) * b * flags
        for half, block in enumerate(swap_halves(left, right)):
            for r in range(0, row_count, 2):
                rows = jnp.concatenate(
                    [block[:, (r + i) * col_count : (r + i + 1) * col_count] for i in range(2)], axis=0
                )
                out_ref[spot(chan // 4 + half, shards), r * 8 : (r + 2) * 8, :] = rows.astype(jnp.bfloat16)


def group_order(shards):
    size = shards // planes
    return [plane * size + place for place in range(size) for plane in range(planes)][::-1]


def spot(device, shards):
    return group_order(shards).index(device)


def receive_blocks(blocks_ref, held_ref):
    shards, rows, _ = blocks_ref.shape
    for i, device in enumerate(group_order(shards)):
        held_ref[device * rows : (device + 1) * rows, :] = blocks_ref[i].astype(jnp.float32)


def exchange(blocks):
    return lax.all_to_all(
        blocks, axes, split_axis=0, concat_axis=0,
        axis_index_groups=[group_order(blocks.shape[0])], tiled=True,
    )


def contract_kernel(blocks_ref, out_ref, held_ref):
    total = held_ref.shape[0] // 8
    receive_blocks(blocks_ref, held_ref)
    products = []
    for c in range(4):
        left = held_ref[pl.ds(c, total, stride=8), :].astype(jnp.bfloat16)
        right = held_ref[pl.ds(4 + c, total, stride=8), :].astype(jnp.bfloat16)
        products.append(
            lax.dot_general(
                left, right, (((1,), (1,)), ((), ())), preferred_element_type=jnp.float32
            )
        )
    for row in range(0, total, 8):
        pieces = [product[row : row + 8] for product in products]
        low, high = swap_halves(pieces[0], pieces[1]), swap_halves(pieces[2], pieces[3])
        for half in range(2):
            rows = jnp.concatenate([low[half], high[half]], axis=0)
            out_ref[spot(row // 4 + half, out_ref.shape[0])] = rows.astype(jnp.bfloat16)


def gate_kernel(normed_ref, w_ref, gain_ref, bias_ref, w_out_ref, out_ref, scales_ref, weights_ref):
    chan_count = normed_ref.shape[1]
    projected = jnp.dot(
        normed_ref[...], w_ref[:, 4 * chan_count :], preferred_element_type=jnp.float32
    )
    out_ref[...] = jax.nn.sigmoid(projected).astype(jnp.bfloat16)
    for i, vector_ref in enumerate((gain_ref, bias_ref)):
        scales_ref[i] = jnp.transpose(jnp.broadcast_to(vector_ref[...], scales_ref.shape[1:]))
    weights_ref[...] = w_out_ref[...]


def finish_kernel(blocks_ref, gate_ref, scales_ref, w_ref, out_ref, held_ref):
    row_count, col_count, chan_count = out_ref.shape
    receive_blocks(blocks_ref, held_ref)
    for r in range(row_count):
        triangle = held_ref[pl.ds(r, chan_count, stride=row_count), :]
        normed = layer_norm(triangle, scales_ref[0], scales_ref[1], 0).astype(jnp.bfloat16)
        result = lax.dot_general(
            normed, w_ref[...], (((0,), (0,)), ((), ())), preferred_element_type=jnp.float32
        )
        gate = gate_ref[r * col_count : (r + 1) * col_count, :].astype(jnp.float32)
        out_ref[r] = (gate * result).astype(jnp.bfloat16)


def local_blocks(pair, valid, norm_gain, norm_bias, w_proj, out_gain, out_bias, w_out):
    row_count, col_count, chan_count = pair.shape
    shards = lax.axis_size(axes)
    tokens = row_count * col_count
    vmem = pl.BlockSpec(memory_space=pltpu.VMEM)
    hbm = pl.BlockSpec(memory_space=pltpu.HBM)

    def line(vector):
        return vector.reshape(1, -1)

    def shaped(*dims):
        return jax.ShapeDtypeStruct(dims, jnp.bfloat16)

    sides, normed = pl.pallas_call(
        project_kernel,
        out_shape=(shaped(shards, 8 * row_count, col_count), shaped(tokens, chan_count)),
        in_specs=[hbm] * 5,
        out_specs=(vmem, vmem),
        scratch_shapes=[
            pltpu.VMEM(pair.shape, jnp.bfloat16),
            pltpu.VMEM((1, col_count), jnp.int32),
            pltpu.VMEM((1, chan_count), jnp.float32),
            pltpu.VMEM((1, chan_count), jnp.float32),
            pltpu.VMEM((chan_count, 4 * chan_count), jnp.bfloat16),
            pltpu.SemaphoreType.DMA((5,)),
        ],
        name="project",
    )(pair, line(valid), line(norm_gain), line(norm_bias), w_proj)
    sides = exchange(sides)
    triangle = pl.pallas_call(
        contract_kernel,
        out_shape=shaped(shards, 4 * row_count, col_count),
        in_specs=[vmem],
        out_specs=vmem,
        scratch_shapes=[pltpu.VMEM((8 * col_count, col_count), jnp.float32)],
        compiler_params=pltpu.CompilerParams(vmem_limit_bytes=kernel_vmem),
        name="contract",
    )(sides)
    triangle = exchange(triangle)
    gate_values, scales, weights = pl.pallas_call(
        gate_kernel,
        out_shape=(
            shaped(tokens, chan_count),
            jax.ShapeDtypeStruct((2, chan_count, col_count), jnp.float32),
            shaped(chan_count, chan_count),
        ),
        in_specs=[vmem] * 5,
        out_specs=(vmem,) * 3,
        compiler_params=pltpu.CompilerParams(vmem_limit_bytes=kernel_vmem),
        name="gate",
    )(normed, w_proj, line(out_gain), line(out_bias), w_out)
    return pl.pallas_call(
        finish_kernel,
        out_shape=shaped(row_count, col_count, chan_count),
        in_specs=[vmem] * 4,
        out_specs=vmem,
        scratch_shapes=[pltpu.VMEM((tokens, chan_count), jnp.float32)],
        compiler_params=pltpu.CompilerParams(vmem_limit_bytes=kernel_vmem),
        name="finish",
    )(triangle, gate_values, scales, weights)


def local_arrays(pair, valid, norm_gain, norm_bias, w_proj, out_gain, out_bias, w_out):
    row_count, col_count, chan_count = pair.shape
    row_start = lax.axis_index(("wide", "narrow")) * row_count
    col_start = lax.axis_index("sub") * col_count
    row_flags = lax.dynamic_slice_in_dim(valid, row_start, row_count, 0).astype(jnp.float32)
    col_flags = lax.dynamic_slice_in_dim(valid, col_start, col_count, 0).astype(jnp.float32)
    pair_flags = row_flags[:, None] * col_flags[None, :]
    normed = layer_norm(pair.astype(jnp.float32), norm_gain, norm_bias, 2).astype(jnp.bfloat16)
    projected = jnp.einsum(
        "rkc,cd->drk", normed, w_proj[:, : 4 * chan_count], preferred_element_type=jnp.float32
    )
    left_side = (
        jax.nn.sigmoid(projected[:chan_count]) * projected[chan_count : 2 * chan_count] * pair_flags
    ).astype(jnp.bfloat16)
    right_side = (
        jax.nn.sigmoid(projected[2 * chan_count : 3 * chan_count])
        * projected[3 * chan_count :]
        * pair_flags
    ).astype(jnp.bfloat16)
    gate_values = jax.nn.sigmoid(
        jnp.einsum(
            "rkc,cd->rkd", normed, w_proj[:, 4 * chan_count :], preferred_element_type=jnp.float32
        )
    ).astype(jnp.bfloat16)
    both_sides = jnp.stack([left_side, right_side], axis=1)
    both_group = lax.all_to_all(
        both_sides, ("wide", "narrow"), split_axis=0, concat_axis=2, tiled=True
    )
    left_group, right_group = both_group[:, 0], both_group[:, 1]
    partial_sums = jnp.einsum(
        "cik,cjk->cij", left_group, right_group, preferred_element_type=jnp.float32
    )
    summed = lax.psum_scatter(partial_sums, "sub", scatter_dimension=2, tiled=True).astype(
        jnp.bfloat16
    )
    returned = lax.all_to_all(summed, ("wide", "narrow"), split_axis=1, concat_axis=0, tiled=True)
    normed_out = layer_norm(
        returned.astype(jnp.float32), out_gain[:, None, None], out_bias[:, None, None], 0
    ).astype(jnp.bfloat16)
    result_out = jnp.einsum("crj,cd->rjd", normed_out, w_out, preferred_element_type=jnp.float32)
    return (gate_values.astype(jnp.float32) * result_out).astype(jnp.bfloat16)


def local(pair, *rest):
    row_count, col_count, chan_count = pair.shape
    shards = lax.axis_size(axes)
    fits = (
        lax.axis_size("sub") == 1
        and (row_count, col_count, chan_count) == (4, 128, 128)
        and shards * row_count == col_count
        and shards * 4 == chan_count
        and shards % planes == 0
    )
    return (local_blocks if fits else local_arrays)(pair, *rest)


def solution(mesh):
    in_specs = (
        P(("parts", "wide", "narrow"), "sub", None),
        P("parts"),
        P(),
        P(),
        P(),
        P(),
        P(),
        P(),
    )
    out_specs = P(("parts", "wide", "narrow"), "sub", None)
    return jax.shard_map(local, mesh=mesh, in_specs=in_specs, out_specs=out_specs, check_vma=False)
```

```python
import functools

import jax
import jax.numpy as jnp
from jax import lax
from jax.experimental import pallas as pl
from jax.experimental.pallas import tpu as pltpu
from jax.sharding import PartitionSpec as P

epsilon = 1e-05
axes = ("wide", "narrow")
kernel_vmem = 8 * 2**20
hub = 31


def layer_norm(values, gain_vec, bias_vec, axis_dim):
    average = jnp.mean(values, axis=axis_dim, keepdims=True)
    centered = values - average
    variance = jnp.mean(centered * centered, axis=axis_dim, keepdims=True)
    return centered * lax.rsqrt(variance + epsilon) * gain_vec + bias_vec


def swap_halves(low, high):
    first = lax.broadcasted_iota(jnp.int32, low.shape, 0) < 4
    return (
        jnp.where(first, low, pltpu.roll(high, 4, 0)),
        jnp.where(first, pltpu.roll(low, 4, 0), high),
    )


def start_copies(pairs, sems, first):
    copies = [
        pltpu.make_async_copy(source, target, sems.at[first + i])
        for i, (source, target) in enumerate(pairs)
    ]
    for copy in copies:
        copy.start()
    return copies


def send_piece(held_ref, out_hbm, done, sems):
    count = held_ref.shape[0] // 4
    if done % count:
        return []
    blocks = pl.ds((done - count) ^ (hub - count + 1), count)
    last = sems.shape[0] - 4 + done // count - 1
    return start_copies([(held_ref.at[blocks], out_hbm.at[blocks])], sems, last)


def project_kernel(
    pair_hbm, valid_hbm, gain_hbm, bias_hbm, w_hbm, out_hbm,
    pair_ref, valid_ref, gain_ref, bias_ref, w_ref, out_ref, sems,
):
    row_count, col_count, chan_count = pair_ref.shape
    shards = out_ref.shape[0]
    small = start_copies(
        [(gain_hbm, gain_ref), (bias_hbm, bias_ref), (valid_hbm, valid_ref)], sems, 0
    )
    rows = start_copies([(pair_hbm.at[r], pair_ref.at[r]) for r in range(row_count)], sems, 3)
    weights = start_copies([(w_hbm.at[:, : 4 * chan_count], w_ref)], sems, 3 + row_count)
    row_start = lax.axis_index(axes) * row_count
    for copy in small:
        copy.wait()
    normed = []
    for r in range(row_count):
        rows[r].wait()
        tokens = pair_ref[r].astype(jnp.float32)
        normed.append(layer_norm(tokens, gain_ref[...], bias_ref[...], 1).astype(jnp.bfloat16))
    normed = jnp.concatenate(normed, axis=0)
    weights[0].wait()
    projected = lax.dot_general(
        w_ref[...], normed, (((0,), (1,)), ((), ())), preferred_element_type=jnp.float32
    )
    col_flags = valid_ref[...].astype(jnp.float32)
    places = lax.broadcasted_iota(jnp.int32, col_flags.shape, 1)
    row_flags = [
        jnp.sum(jnp.where(places == row_start + r, col_flags, 0.0), axis=1, keepdims=True)
        for r in range(row_count)
    ]
    flags = jnp.concatenate([col_flags * row_flag for row_flag in row_flags], axis=1)
    sent = []
    for chan in range(0, chan_count, 8):
        a_gate, a, b_gate, b = (
            projected[i * chan_count + chan : i * chan_count + chan + 8] for i in range(4)
        )
        left = jax.nn.sigmoid(a_gate) * a * flags
        right = jax.nn.sigmoid(b_gate) * b * flags
        for half, block in enumerate(swap_halves(left, right)):
            for r in range(0, row_count, 2):
                rows = jnp.concatenate(
                    [block[:, (r + i) * col_count : (r + i + 1) * col_count] for i in range(2)], axis=0
                )
                out_ref[(chan // 4 + half) ^ hub, r * 8 : (r + 2) * 8, :] = rows.astype(jnp.bfloat16)
        sent += send_piece(out_ref, out_hbm, chan // 4 + 2, sems)
    for copy in sent:
        copy.wait()


def receive_blocks(blocks_ref, held_ref):
    shards, rows, _ = blocks_ref.shape
    for i in range(shards):
        held_ref[(i ^ hub) * rows : ((i ^ hub) + 1) * rows, :] = blocks_ref[i].astype(jnp.float32)


def exchange(blocks):
    groups = [[i ^ hub for i in range(blocks.shape[0])]]
    return lax.all_to_all(
        blocks, axes, split_axis=0, concat_axis=0, axis_index_groups=groups, tiled=True
    )


def contract_kernel(blocks_ref, out_hbm, held_ref, out_ref, sems):
    total = held_ref.shape[0] // 8
    receive_blocks(blocks_ref, held_ref)
    products = []
    for c in range(4):
        left = held_ref[pl.ds(c, total, stride=8), :].astype(jnp.bfloat16)
        right = held_ref[pl.ds(4 + c, total, stride=8), :].astype(jnp.bfloat16)
        products.append(
            lax.dot_general(
                left, right, (((1,), (1,)), ((), ())), preferred_element_type=jnp.float32
            )
        )
    sent = []
    for row in range(0, total, 8):
        pieces = [product[row : row + 8] for product in products]
        low, high = swap_halves(pieces[0], pieces[1]), swap_halves(pieces[2], pieces[3])
        for half in range(2):
            rows = jnp.concatenate([low[half], high[half]], axis=0)
            out_ref[(row // 4 + half) ^ hub] = rows.astype(jnp.bfloat16)
        sent += send_piece(out_ref, out_hbm, row // 4 + 2, sems)
    for copy in sent:
        copy.wait()


def gate_kernel(
    pair_ref, norm_gain_ref, norm_bias_ref, w_ref, gain_ref, bias_ref, w_out_ref, out_ref, scales_ref, weights_ref
):
    chan_count = pair_ref.shape[2]
    tokens = pair_ref[...].reshape(-1, chan_count).astype(jnp.float32)
    normed = layer_norm(tokens, norm_gain_ref[...], norm_bias_ref[...], 1).astype(jnp.bfloat16)
    projected = jnp.dot(
        normed, w_ref[:, 4 * chan_count :], preferred_element_type=jnp.float32
    )
    out_ref[...] = jax.nn.sigmoid(projected).astype(jnp.bfloat16)
    for i, vector_ref in enumerate((gain_ref, bias_ref)):
        scales_ref[i] = jnp.transpose(jnp.broadcast_to(vector_ref[...], scales_ref.shape[1:]))
    weights_ref[...] = w_out_ref[...]


def finish_kernel(blocks_ref, gate_ref, scales_ref, w_ref, out_hbm, held_ref, out_ref, sems):
    row_count, col_count, chan_count = out_ref.shape
    receive_blocks(blocks_ref, held_ref)
    sent = []
    for r in range(row_count):
        triangle = held_ref[pl.ds(r, chan_count, stride=row_count), :]
        normed = layer_norm(triangle, scales_ref[0], scales_ref[1], 0).astype(jnp.bfloat16)
        result = lax.dot_general(
            normed, w_ref[...], (((0,), (0,)), ((), ())), preferred_element_type=jnp.float32
        )
        gate = gate_ref[r * col_count : (r + 1) * col_count, :].astype(jnp.float32)
        out_ref[r] = (gate * result).astype(jnp.bfloat16)
        sent += start_copies([(out_ref.at[r], out_hbm.at[r])], sems, r)
    for copy in sent:
        copy.wait()


def local_blocks(pair, valid, norm_gain, norm_bias, w_proj, out_gain, out_bias, w_out):
    row_count, col_count, chan_count = pair.shape
    shards = lax.axis_size(axes)
    tokens = row_count * col_count
    vmem = pl.BlockSpec(memory_space=pltpu.VMEM)
    hbm = pl.BlockSpec(memory_space=pltpu.HBM)

    def line(vector):
        return vector.reshape(1, -1)

    def shaped(*dims):
        return jax.ShapeDtypeStruct(dims, jnp.bfloat16)

    sides = pl.pallas_call(
        project_kernel,
        out_shape=shaped(shards, 8 * row_count, col_count),
        in_specs=[hbm] * 5,
        out_specs=hbm,
        scratch_shapes=[
            pltpu.VMEM(pair.shape, jnp.bfloat16),
            pltpu.VMEM((1, col_count), jnp.int32),
            pltpu.VMEM((1, chan_count), jnp.float32),
            pltpu.VMEM((1, chan_count), jnp.float32),
            pltpu.VMEM((chan_count, 4 * chan_count), jnp.bfloat16),
            pltpu.VMEM((shards, 8 * row_count, col_count), jnp.bfloat16),
            pltpu.SemaphoreType.DMA((8 + row_count,)),
        ],
        name="project",
    )(pair, line(valid), line(norm_gain), line(norm_bias), w_proj)
    sides = exchange(sides)
    triangle = pl.pallas_call(
        contract_kernel,
        out_shape=shaped(shards, 4 * row_count, col_count),
        in_specs=[vmem],
        out_specs=hbm,
        scratch_shapes=[
            pltpu.VMEM((8 * col_count, col_count), jnp.float32),
            pltpu.VMEM((shards, 4 * row_count, col_count), jnp.bfloat16),
            pltpu.SemaphoreType.DMA((4,)),
        ],
        compiler_params=pltpu.CompilerParams(vmem_limit_bytes=kernel_vmem),
        name="contract",
    )(sides)
    triangle = exchange(triangle)
    gate_values, scales, weights = pl.pallas_call(
        gate_kernel,
        out_shape=(
            shaped(tokens, chan_count),
            jax.ShapeDtypeStruct((2, chan_count, col_count), jnp.float32),
            shaped(chan_count, chan_count),
        ),
        in_specs=[vmem] * 7,
        out_specs=(vmem,) * 3,
        compiler_params=pltpu.CompilerParams(vmem_limit_bytes=kernel_vmem),
        name="gate",
    )(
        pair, line(norm_gain), line(norm_bias), w_proj, line(out_gain), line(out_bias), w_out
    )
    return pl.pallas_call(
        finish_kernel,
        out_shape=shaped(row_count, col_count, chan_count),
        in_specs=[vmem] * 4,
        out_specs=hbm,
        scratch_shapes=[
            pltpu.VMEM((tokens, chan_count), jnp.float32),
            pltpu.VMEM(pair.shape, jnp.bfloat16),
            pltpu.SemaphoreType.DMA((row_count,)),
        ],
        compiler_params=pltpu.CompilerParams(vmem_limit_bytes=kernel_vmem),
        name="finish",
    )(triangle, gate_values, scales, weights)


def local_arrays(pair, valid, norm_gain, norm_bias, w_proj, out_gain, out_bias, w_out):
    row_count, col_count, chan_count = pair.shape
    row_start = lax.axis_index(("wide", "narrow")) * row_count
    col_start = lax.axis_index("sub") * col_count
    row_flags = lax.dynamic_slice_in_dim(valid, row_start, row_count, 0).astype(jnp.float32)
    col_flags = lax.dynamic_slice_in_dim(valid, col_start, col_count, 0).astype(jnp.float32)
    pair_flags = row_flags[:, None] * col_flags[None, :]
    normed = layer_norm(pair.astype(jnp.float32), norm_gain, norm_bias, 2).astype(jnp.bfloat16)
    projected = jnp.einsum(
        "rkc,cd->drk", normed, w_proj[:, : 4 * chan_count], preferred_element_type=jnp.float32
    )
    left_side = (
        jax.nn.sigmoid(projected[:chan_count]) * projected[chan_count : 2 * chan_count] * pair_flags
    ).astype(jnp.bfloat16)
    right_side = (
        jax.nn.sigmoid(projected[2 * chan_count : 3 * chan_count])
        * projected[3 * chan_count :]
        * pair_flags
    ).astype(jnp.bfloat16)
    gate_values = jax.nn.sigmoid(
        jnp.einsum(
            "rkc,cd->rkd", normed, w_proj[:, 4 * chan_count :], preferred_element_type=jnp.float32
        )
    ).astype(jnp.bfloat16)
    both_sides = jnp.stack([left_side, right_side], axis=1)
    both_group = lax.all_to_all(
        both_sides, ("wide", "narrow"), split_axis=0, concat_axis=2, tiled=True
    )
    left_group, right_group = both_group[:, 0], both_group[:, 1]
    partial_sums = jnp.einsum(
        "cik,cjk->cij", left_group, right_group, preferred_element_type=jnp.float32
    )
    summed = lax.psum_scatter(partial_sums, "sub", scatter_dimension=2, tiled=True).astype(
        jnp.bfloat16
    )
    returned = lax.all_to_all(summed, ("wide", "narrow"), split_axis=1, concat_axis=0, tiled=True)
    normed_out = layer_norm(
        returned.astype(jnp.float32), out_gain[:, None, None], out_bias[:, None, None], 0
    ).astype(jnp.bfloat16)
    result_out = jnp.einsum("crj,cd->rjd", normed_out, w_out, preferred_element_type=jnp.float32)
    return (gate_values.astype(jnp.float32) * result_out).astype(jnp.bfloat16)


def local(pair, *rest):
    row_count, col_count, chan_count = pair.shape
    shards = lax.axis_size(axes)
    fits = (
        lax.axis_size("sub") == 1
        and (row_count, col_count, chan_count) == (4, 128, 128)
        and shards * row_count == col_count
        and shards * 4 == chan_count
        and shards == hub + 1
    )
    return (local_blocks if fits else local_arrays)(pair, *rest)


def solution(mesh):
    in_specs = (
        P(("parts", "wide", "narrow"), "sub", None),
        P("parts"),
        P(),
        P(),
        P(),
        P(),
        P(),
        P(),
    )
    out_specs = P(("parts", "wide", "narrow"), "sub", None)
    return jax.shard_map(local, mesh=mesh, in_specs=in_specs, out_specs=out_specs, check_vma=False)
```

```python
import functools

import jax
import jax.numpy as jnp
from jax import lax
from jax.experimental import pallas as pl
from jax.experimental.pallas import tpu as pltpu
from jax.sharding import PartitionSpec as P

epsilon = 1e-05
axes = ("wide", "narrow")
kernel_vmem = 8 * 2**20


def layer_norm(values, gain_vec, bias_vec, axis_dim):
    average = jnp.mean(values, axis=axis_dim, keepdims=True)
    centered = values - average
    variance = jnp.mean(centered * centered, axis=axis_dim, keepdims=True)
    return centered * lax.rsqrt(variance + epsilon) * gain_vec + bias_vec


def swap_halves(low, high):
    first = lax.broadcasted_iota(jnp.int32, low.shape, 0) < 4
    return (
        jnp.where(first, low, pltpu.roll(high, 4, 0)),
        jnp.where(first, pltpu.roll(low, 4, 0), high),
    )


def project_kernel(
    pair_hbm, valid_hbm, gain_hbm, bias_hbm, w_hbm, near_ref, far_ref,
    out_ref, pair_ref, valid_ref, gain_ref, bias_ref, w_ref, sems,
):
    row_count, col_count, chan_count = pair_ref.shape
    fetches = [
        pltpu.make_async_copy(source, held, sems.at[i])
        for i, (source, held) in enumerate((
            (pair_hbm, pair_ref), (gain_hbm, gain_ref), (bias_hbm, bias_ref),
            (w_hbm.at[:, : 4 * chan_count], w_ref), (valid_hbm, valid_ref),
        ))
    ]
    for fetch in fetches:
        fetch.start()
    row_start = lax.axis_index(axes) * row_count
    for fetch in fetches[:3]:
        fetch.wait()
    tokens = pair_ref[...].reshape(row_count * col_count, chan_count).astype(jnp.float32)
    normed = layer_norm(tokens, gain_ref[...], bias_ref[...], 1).astype(jnp.bfloat16)
    for fetch in fetches[3:]:
        fetch.wait()
    projected = lax.dot_general(
        w_ref[...], normed, (((0,), (1,)), ((), ())),
        preferred_element_type=jnp.float32,
    )
    col_flags = valid_ref[...].astype(jnp.float32)
    places = lax.broadcasted_iota(jnp.int32, col_flags.shape, 1)
    row_flags = [
        jnp.sum(jnp.where(places == row_start + r, col_flags, 0.0), axis=1, keepdims=True)
        for r in range(row_count)
    ]
    flags = jnp.concatenate([col_flags * row_flag for row_flag in row_flags], axis=1)
    for chan in range(0, chan_count, 8):
        a_gate, a, b_gate, b = (
            projected[i * chan_count + chan : i * chan_count + chan + 8] for i in range(4)
        )
        left = jax.nn.sigmoid(a_gate) * a * flags
        right = jax.nn.sigmoid(b_gate) * b * flags
        for half, block in enumerate(swap_halves(left, right)):
            for r in range(0, row_count, 2):
                rows = jnp.concatenate(
                    [block[:, (r + i) * col_count : (r + i + 1) * col_count] for i in range(2)], axis=0
                )
                out_ref[chan // 4 + half, r * 8 : (r + 2) * 8, :] = rows.astype(jnp.bfloat16)
    send_halves(out_ref, near_ref, far_ref)


def first_of_half(shards):
    return lax.axis_index(axes) // (shards // 2) * (shards // 2)


def send_halves(held_ref, near_ref, far_ref):
    shards = held_ref.shape[0]
    first = first_of_half(shards)
    near_ref[...] = held_ref[pl.ds(first, shards // 2)]
    far_ref[...] = held_ref[pl.ds(shards // 2 - first, shards // 2)]


def receive_halves(near_ref, far_ref, held_ref):
    count, rows, _ = near_ref.shape
    first = first_of_half(2 * count)
    for start, block_ref in ((first, near_ref), (count - first, far_ref)):
        start = pl.multiple_of(start * rows, count * rows)
        held_ref[pl.ds(start, count * rows), :] = (
            block_ref[...].reshape(count * rows, -1).astype(jnp.float32)
        )


def exchange(near, far):
    count = near.shape[0]
    far = lax.ppermute(far, axes, [(i, (i + count) % (2 * count)) for i in range(2 * count)])
    groups = [list(range(count)), list(range(count, 2 * count))]
    return tuple(
        lax.all_to_all(
            blocks, axes, split_axis=0, concat_axis=0, axis_index_groups=groups, tiled=True
        )
        for blocks in (near, far)
    )


def contract_kernel(near_ref, far_ref, near_out_ref, far_out_ref, held_ref, out_ref):
    total = held_ref.shape[0] // 8
    receive_halves(near_ref, far_ref, held_ref)
    products = []
    for c in range(4):
        left = held_ref[pl.ds(c, total, stride=8), :].astype(jnp.bfloat16)
        right = held_ref[pl.ds(4 + c, total, stride=8), :].astype(jnp.bfloat16)
        products.append(
            lax.dot_general(
                left, right, (((1,), (1,)), ((), ())), preferred_element_type=jnp.float32
            )
        )
    for row in range(0, total, 8):
        pieces = [product[row : row + 8] for product in products]
        low, high = swap_halves(pieces[0], pieces[1]), swap_halves(pieces[2], pieces[3])
        for half in range(2):
            rows = jnp.concatenate([low[half], high[half]], axis=0)
            out_ref[row // 4 + half] = rows.astype(jnp.bfloat16)
    send_halves(out_ref, near_out_ref, far_out_ref)


def gate_kernel(
    pair_ref, norm_gain_ref, norm_bias_ref, w_ref, gain_ref, bias_ref, w_out_ref, out_ref, scales_ref, weights_ref
):
    chan_count = pair_ref.shape[2]
    tokens = pair_ref[...].reshape(-1, chan_count).astype(jnp.float32)
    normed = layer_norm(tokens, norm_gain_ref[...], norm_bias_ref[...], 1).astype(jnp.bfloat16)
    projected = jnp.dot(
        normed, w_ref[:, 4 * chan_count :], preferred_element_type=jnp.float32
    )
    out_ref[...] = jax.nn.sigmoid(projected).astype(jnp.bfloat16)
    for i, vector_ref in enumerate((gain_ref, bias_ref)):
        scales_ref[i] = jnp.transpose(jnp.broadcast_to(vector_ref[...], scales_ref.shape[1:]))
    weights_ref[...] = w_out_ref[...]


def finish_kernel(near_ref, far_ref, gate_ref, scales_ref, w_ref, out_ref, held_ref):
    row_count, col_count, chan_count = out_ref.shape
    receive_halves(near_ref, far_ref, held_ref)
    for r in range(row_count):
        triangle = held_ref[pl.ds(r, chan_count, stride=row_count), :]
        normed = layer_norm(triangle, scales_ref[0], scales_ref[1], 0).astype(jnp.bfloat16)
        result = lax.dot_general(
            normed, w_ref[...], (((0,), (0,)), ((), ())), preferred_element_type=jnp.float32
        )
        gate = gate_ref[r * col_count : (r + 1) * col_count, :].astype(jnp.float32)
        out_ref[r] = (gate * result).astype(jnp.bfloat16)


def local_blocks(pair, valid, norm_gain, norm_bias, w_proj, out_gain, out_bias, w_out):
    row_count, col_count, chan_count = pair.shape
    shards = lax.axis_size(axes)
    tokens = row_count * col_count
    vmem = pl.BlockSpec(memory_space=pltpu.VMEM)
    hbm = pl.BlockSpec(memory_space=pltpu.HBM)

    def line(vector):
        return vector.reshape(1, -1)

    def shaped(*dims):
        return jax.ShapeDtypeStruct(dims, jnp.bfloat16)

    sides = pl.pallas_call(
        project_kernel,
        out_shape=(shaped(shards // 2, 8 * row_count, col_count),) * 2,
        in_specs=[hbm] * 5,
        out_specs=(vmem,) * 2,
        scratch_shapes=[
            pltpu.VMEM((shards, 8 * row_count, col_count), jnp.bfloat16),
            pltpu.VMEM(pair.shape, jnp.bfloat16),
            pltpu.VMEM((1, col_count), jnp.int32),
            pltpu.VMEM((1, chan_count), jnp.float32),
            pltpu.VMEM((1, chan_count), jnp.float32),
            pltpu.VMEM((chan_count, 4 * chan_count), jnp.bfloat16),
            pltpu.SemaphoreType.DMA((5,)),
        ],
        name="project",
    )(pair, line(valid), line(norm_gain), line(norm_bias), w_proj)
    triangle = pl.pallas_call(
        contract_kernel,
        out_shape=(shaped(shards // 2, 4 * row_count, col_count),) * 2,
        in_specs=[vmem] * 2,
        out_specs=(vmem,) * 2,
        scratch_shapes=[
            pltpu.VMEM((8 * col_count, col_count), jnp.float32),
            pltpu.VMEM((shards, 4 * row_count, col_count), jnp.bfloat16),
        ],
        compiler_params=pltpu.CompilerParams(vmem_limit_bytes=kernel_vmem),
        name="contract",
    )(*exchange(*sides))
    triangle = exchange(*triangle)
    gate_values, scales, weights = pl.pallas_call(
        gate_kernel,
        out_shape=(
            shaped(tokens, chan_count),
            jax.ShapeDtypeStruct((2, chan_count, col_count), jnp.float32),
            shaped(chan_count, chan_count),
        ),
        in_specs=[vmem] * 7,
        out_specs=(vmem,) * 3,
        compiler_params=pltpu.CompilerParams(vmem_limit_bytes=kernel_vmem),
        name="gate",
    )(
        pair, line(norm_gain), line(norm_bias), w_proj, line(out_gain), line(out_bias), w_out
    )
    return pl.pallas_call(
        finish_kernel,
        out_shape=shaped(row_count, col_count, chan_count),
        in_specs=[vmem] * 5,
        out_specs=vmem,
        scratch_shapes=[pltpu.VMEM((tokens, chan_count), jnp.float32)],
        compiler_params=pltpu.CompilerParams(vmem_limit_bytes=kernel_vmem),
        name="finish",
    )(*triangle, gate_values, scales, weights)


def local_arrays(pair, valid, norm_gain, norm_bias, w_proj, out_gain, out_bias, w_out):
    row_count, col_count, chan_count = pair.shape
    row_start = lax.axis_index(("wide", "narrow")) * row_count
    col_start = lax.axis_index("sub") * col_count
    row_flags = lax.dynamic_slice_in_dim(valid, row_start, row_count, 0).astype(jnp.float32)
    col_flags = lax.dynamic_slice_in_dim(valid, col_start, col_count, 0).astype(jnp.float32)
    pair_flags = row_flags[:, None] * col_flags[None, :]
    normed = layer_norm(pair.astype(jnp.float32), norm_gain, norm_bias, 2).astype(jnp.bfloat16)
    projected = jnp.einsum(
        "rkc,cd->drk", normed, w_proj[:, : 4 * chan_count], preferred_element_type=jnp.float32
    )
    left_side = (
        jax.nn.sigmoid(projected[:chan_count]) * projected[chan_count : 2 * chan_count] * pair_flags
    ).astype(jnp.bfloat16)
    right_side = (
        jax.nn.sigmoid(projected[2 * chan_count : 3 * chan_count])
        * projected[3 * chan_count :]
        * pair_flags
    ).astype(jnp.bfloat16)
    gate_values = jax.nn.sigmoid(
        jnp.einsum(
            "rkc,cd->rkd", normed, w_proj[:, 4 * chan_count :], preferred_element_type=jnp.float32
        )
    ).astype(jnp.bfloat16)
    both_sides = jnp.stack([left_side, right_side], axis=1)
    both_group = lax.all_to_all(
        both_sides, ("wide", "narrow"), split_axis=0, concat_axis=2, tiled=True
    )
    left_group, right_group = both_group[:, 0], both_group[:, 1]
    partial_sums = jnp.einsum(
        "cik,cjk->cij", left_group, right_group, preferred_element_type=jnp.float32
    )
    summed = lax.psum_scatter(partial_sums, "sub", scatter_dimension=2, tiled=True).astype(
        jnp.bfloat16
    )
    returned = lax.all_to_all(summed, ("wide", "narrow"), split_axis=1, concat_axis=0, tiled=True)
    normed_out = layer_norm(
        returned.astype(jnp.float32), out_gain[:, None, None], out_bias[:, None, None], 0
    ).astype(jnp.bfloat16)
    result_out = jnp.einsum("crj,cd->rjd", normed_out, w_out, preferred_element_type=jnp.float32)
    return (gate_values.astype(jnp.float32) * result_out).astype(jnp.bfloat16)


def local(pair, *rest):
    row_count, col_count, chan_count = pair.shape
    shards = lax.axis_size(axes)
    fits = (
        lax.axis_size("sub") == 1
        and (row_count, col_count, chan_count) == (4, 128, 128)
        and shards * row_count == col_count
        and shards * 4 == chan_count
        and shards % 2 == 0
    )
    return (local_blocks if fits else local_arrays)(pair, *rest)


def solution(mesh):
    in_specs = (
        P(("parts", "wide", "narrow"), "sub", None),
        P("parts"),
        P(),
        P(),
        P(),
        P(),
        P(),
        P(),
    )
    out_specs = P(("parts", "wide", "narrow"), "sub", None)
    return jax.shard_map(local, mesh=mesh, in_specs=in_specs, out_specs=out_specs, check_vma=False)
```

```python
import functools

import jax
import jax.numpy as jnp
from jax import lax
from jax.experimental import pallas as pl
from jax.experimental.pallas import tpu as pltpu
from jax.sharding import PartitionSpec as P

epsilon = 1e-05
axes = ("wide", "narrow")
kernel_vmem = 8 * 2**20
hub = 31


def layer_norm(values, gain_vec, bias_vec, axis_dim):
    average = jnp.mean(values, axis=axis_dim, keepdims=True)
    centered = values - average
    variance = jnp.mean(centered * centered, axis=axis_dim, keepdims=True)
    return centered * lax.rsqrt(variance + epsilon) * gain_vec + bias_vec


def swap_halves(low, high):
    first = lax.broadcasted_iota(jnp.int32, low.shape, 0) < 4
    return (
        jnp.where(first, low, pltpu.roll(high, 4, 0)),
        jnp.where(first, pltpu.roll(low, 4, 0), high),
    )


def project_kernel(
    pair_hbm, valid_hbm, gain_hbm, bias_hbm, w_hbm, out_ref,
    pair_ref, valid_ref, gain_ref, bias_ref, w_ref, sems,
):
    row_count, col_count, chan_count = pair_ref.shape
    fetches = [
        pltpu.make_async_copy(source, held, sems.at[i])
        for i, (source, held) in enumerate((
            (pair_hbm, pair_ref), (gain_hbm, gain_ref), (bias_hbm, bias_ref),
            (w_hbm.at[:, : 4 * chan_count], w_ref), (valid_hbm, valid_ref),
        ))
    ]
    for fetch in fetches:
        fetch.start()
    row_start = lax.axis_index(axes) * row_count
    for fetch in fetches[:3]:
        fetch.wait()
    tokens = pair_ref[...].reshape(row_count * col_count, chan_count).astype(jnp.float32)
    normed = layer_norm(tokens, gain_ref[...], bias_ref[...], 1).astype(jnp.bfloat16)
    for fetch in fetches[3:]:
        fetch.wait()
    projected = lax.dot_general(
        w_ref[...], normed, (((0,), (1,)), ((), ())),
        preferred_element_type=jnp.float32,
    )
    col_flags = valid_ref[...].astype(jnp.float32)
    places = lax.broadcasted_iota(jnp.int32, col_flags.shape, 1)
    row_flags = [
        jnp.sum(jnp.where(places == row_start + r, col_flags, 0.0), axis=1, keepdims=True)
        for r in range(row_count)
    ]
    flags = jnp.concatenate([col_flags * row_flag for row_flag in row_flags], axis=1)
    for chan in range(0, chan_count, 8):
        a_gate, a, b_gate, b = (
            projected[i * chan_count + chan : i * chan_count + chan + 8] for i in range(4)
        )
        left = jax.nn.sigmoid(a_gate) * a * flags
        right = jax.nn.sigmoid(b_gate) * b * flags
        for half, block in enumerate(swap_halves(left, right)):
            for r in range(0, row_count, 2):
                rows = jnp.concatenate(
                    [block[:, (r + i) * col_count : (r + i + 1) * col_count] for i in range(2)], axis=0
                )
                out_ref[(chan // 4 + half) ^ hub, r * 8 : (r + 2) * 8, :] = rows.astype(jnp.bfloat16)


def receive_blocks(blocks_ref, held_ref):
    shards, rows, _ = blocks_ref.shape
    for i in range(shards):
        held_ref[(i ^ hub) * rows : ((i ^ hub) + 1) * rows, :] = blocks_ref[i].astype(jnp.float32)


def exchange(blocks):
    groups = [[i ^ hub for i in range(blocks.shape[0])]]
    return lax.all_to_all(
        blocks, axes, split_axis=0, concat_axis=0, axis_index_groups=groups, tiled=True
    )


def contract_kernel(blocks_ref, gate_ref, out_ref, held_ref):
    del gate_ref
    total = held_ref.shape[0] // 8
    receive_blocks(blocks_ref, held_ref)
    products = []
    for c in range(4):
        left = held_ref[pl.ds(c, total, stride=8), :].astype(jnp.bfloat16)
        right = held_ref[pl.ds(4 + c, total, stride=8), :].astype(jnp.bfloat16)
        products.append(
            lax.dot_general(
                left, right, (((1,), (1,)), ((), ())), preferred_element_type=jnp.float32
            )
        )
    for row in range(0, total, 8):
        pieces = [product[row : row + 8] for product in products]
        low, high = swap_halves(pieces[0], pieces[1]), swap_halves(pieces[2], pieces[3])
        for half in range(2):
            rows = jnp.concatenate([low[half], high[half]], axis=0)
            out_ref[(row // 4 + half) ^ hub] = rows.astype(jnp.bfloat16)


def gate_kernel(
    pair_ref, norm_gain_ref, norm_bias_ref, w_ref, gain_ref, bias_ref, w_out_ref, out_ref, scales_ref, weights_ref
):
    chan_count = pair_ref.shape[2]
    tokens = pair_ref[...].reshape(-1, chan_count).astype(jnp.float32)
    normed = layer_norm(tokens, norm_gain_ref[...], norm_bias_ref[...], 1).astype(jnp.bfloat16)
    projected = jnp.dot(
        normed, w_ref[:, 4 * chan_count :], preferred_element_type=jnp.float32
    )
    out_ref[...] = jax.nn.sigmoid(projected).astype(jnp.bfloat16)
    for i, vector_ref in enumerate((gain_ref, bias_ref)):
        scales_ref[i] = jnp.transpose(jnp.broadcast_to(vector_ref[...], scales_ref.shape[1:]))
    weights_ref[...] = w_out_ref[...]


def finish_kernel(blocks_ref, gate_ref, scales_ref, w_ref, out_ref, held_ref):
    row_count, col_count, chan_count = out_ref.shape
    receive_blocks(blocks_ref, held_ref)
    for r in range(row_count):
        triangle = held_ref[pl.ds(r, chan_count, stride=row_count), :]
        normed = layer_norm(triangle, scales_ref[0], scales_ref[1], 0).astype(jnp.bfloat16)
        result = lax.dot_general(
            normed, w_ref[...], (((0,), (0,)), ((), ())), preferred_element_type=jnp.float32
        )
        gate = gate_ref[r * col_count : (r + 1) * col_count, :].astype(jnp.float32)
        out_ref[r] = (gate * result).astype(jnp.bfloat16)


def local_blocks(pair, valid, norm_gain, norm_bias, w_proj, out_gain, out_bias, w_out):
    row_count, col_count, chan_count = pair.shape
    shards = lax.axis_size(axes)
    tokens = row_count * col_count
    vmem = pl.BlockSpec(memory_space=pltpu.VMEM)
    hbm = pl.BlockSpec(memory_space=pltpu.HBM)

    def line(vector):
        return vector.reshape(1, -1)

    def shaped(*dims):
        return jax.ShapeDtypeStruct(dims, jnp.bfloat16)

    sides = pl.pallas_call(
        project_kernel,
        out_shape=shaped(shards, 8 * row_count, col_count),
        in_specs=[hbm] * 5,
        out_specs=vmem,
        scratch_shapes=[
            pltpu.VMEM(pair.shape, jnp.bfloat16),
            pltpu.VMEM((1, col_count), jnp.int32),
            pltpu.VMEM((1, chan_count), jnp.float32),
            pltpu.VMEM((1, chan_count), jnp.float32),
            pltpu.VMEM((chan_count, 4 * chan_count), jnp.bfloat16),
            pltpu.SemaphoreType.DMA((5,)),
        ],
        name="project",
    )(pair, line(valid), line(norm_gain), line(norm_bias), w_proj)
    sides = exchange(sides)
    gate_values, scales, weights = pl.pallas_call(
        gate_kernel,
        out_shape=(
            shaped(tokens, chan_count),
            jax.ShapeDtypeStruct((2, chan_count, col_count), jnp.float32),
            shaped(chan_count, chan_count),
        ),
        in_specs=[vmem] * 7,
        out_specs=(vmem,) * 3,
        compiler_params=pltpu.CompilerParams(vmem_limit_bytes=kernel_vmem),
        name="gate",
    )(
        pair, line(norm_gain), line(norm_bias), w_proj, line(out_gain), line(out_bias), w_out
    )
    triangle = pl.pallas_call(
        contract_kernel,
        out_shape=shaped(shards, 4 * row_count, col_count),
        in_specs=[vmem, pl.BlockSpec(memory_space=pl.ANY)],
        out_specs=vmem,
        scratch_shapes=[pltpu.VMEM((8 * col_count, col_count), jnp.float32)],
        compiler_params=pltpu.CompilerParams(vmem_limit_bytes=kernel_vmem),
        name="contract",
    )(sides, gate_values)
    triangle = exchange(triangle)
    return pl.pallas_call(
        finish_kernel,
        out_shape=shaped(row_count, col_count, chan_count),
        in_specs=[vmem] * 4,
        out_specs=vmem,
        scratch_shapes=[pltpu.VMEM((tokens, chan_count), jnp.float32)],
        compiler_params=pltpu.CompilerParams(vmem_limit_bytes=kernel_vmem),
        name="finish",
    )(triangle, gate_values, scales, weights)


def local_arrays(pair, valid, norm_gain, norm_bias, w_proj, out_gain, out_bias, w_out):
    row_count, col_count, chan_count = pair.shape
    row_start = lax.axis_index(("wide", "narrow")) * row_count
    col_start = lax.axis_index("sub") * col_count
    row_flags = lax.dynamic_slice_in_dim(valid, row_start, row_count, 0).astype(jnp.float32)
    col_flags = lax.dynamic_slice_in_dim(valid, col_start, col_count, 0).astype(jnp.float32)
    pair_flags = row_flags[:, None] * col_flags[None, :]
    normed = layer_norm(pair.astype(jnp.float32), norm_gain, norm_bias, 2).astype(jnp.bfloat16)
    projected = jnp.einsum(
        "rkc,cd->drk", normed, w_proj[:, : 4 * chan_count], preferred_element_type=jnp.float32
    )
    left_side = (
        jax.nn.sigmoid(projected[:chan_count]) * projected[chan_count : 2 * chan_count] * pair_flags
    ).astype(jnp.bfloat16)
    right_side = (
        jax.nn.sigmoid(projected[2 * chan_count : 3 * chan_count])
        * projected[3 * chan_count :]
        * pair_flags
    ).astype(jnp.bfloat16)
    gate_values = jax.nn.sigmoid(
        jnp.einsum(
            "rkc,cd->rkd", normed, w_proj[:, 4 * chan_count :], preferred_element_type=jnp.float32
        )
    ).astype(jnp.bfloat16)
    both_sides = jnp.stack([left_side, right_side], axis=1)
    both_group = lax.all_to_all(
        both_sides, ("wide", "narrow"), split_axis=0, concat_axis=2, tiled=True
    )
    left_group, right_group = both_group[:, 0], both_group[:, 1]
    partial_sums = jnp.einsum(
        "cik,cjk->cij", left_group, right_group, preferred_element_type=jnp.float32
    )
    summed = lax.psum_scatter(partial_sums, "sub", scatter_dimension=2, tiled=True).astype(
        jnp.bfloat16
    )
    returned = lax.all_to_all(summed, ("wide", "narrow"), split_axis=1, concat_axis=0, tiled=True)
    normed_out = layer_norm(
        returned.astype(jnp.float32), out_gain[:, None, None], out_bias[:, None, None], 0
    ).astype(jnp.bfloat16)
    result_out = jnp.einsum("crj,cd->rjd", normed_out, w_out, preferred_element_type=jnp.float32)
    return (gate_values.astype(jnp.float32) * result_out).astype(jnp.bfloat16)


def local(pair, *rest):
    row_count, col_count, chan_count = pair.shape
    shards = lax.axis_size(axes)
    fits = (
        lax.axis_size("sub") == 1
        and (row_count, col_count, chan_count) == (4, 128, 128)
        and shards * row_count == col_count
        and shards * 4 == chan_count
        and shards == hub + 1
    )
    return (local_blocks if fits else local_arrays)(pair, *rest)


def solution(mesh):
    in_specs = (
        P(("parts", "wide", "narrow"), "sub", None),
        P("parts"),
        P(),
        P(),
        P(),
        P(),
        P(),
        P(),
    )
    out_specs = P(("parts", "wide", "narrow"), "sub", None)
    return jax.shard_map(local, mesh=mesh, in_specs=in_specs, out_specs=out_specs, check_vma=False)
```

```python
import functools

import jax
import jax.numpy as jnp
from jax import lax
from jax.experimental import pallas as pl
from jax.experimental.pallas import tpu as pltpu
from jax.sharding import PartitionSpec as P

epsilon = 1e-05
axes = ("wide", "narrow")
kernel_vmem = 8 * 2**20
hub = 31


def layer_norm(values, gain_vec, bias_vec, axis_dim):
    average = jnp.mean(values, axis=axis_dim, keepdims=True)
    centered = values - average
    variance = jnp.mean(centered * centered, axis=axis_dim, keepdims=True)
    return centered * lax.rsqrt(variance + epsilon) * gain_vec + bias_vec


def swap_halves(low, high):
    first = lax.broadcasted_iota(jnp.int32, low.shape, 0) < 4
    return (
        jnp.where(first, low, pltpu.roll(high, 4, 0)),
        jnp.where(first, pltpu.roll(low, 4, 0), high),
    )


def project_kernel(
    pair_hbm, valid_hbm, gain_hbm, bias_hbm, w_hbm, out_ref, normed_ref,
    pair_ref, valid_ref, gain_ref, bias_ref, w_ref, sems,
):
    row_count, col_count, chan_count = pair_ref.shape
    fetches = [
        pltpu.make_async_copy(source, held, sems.at[i])
        for i, (source, held) in enumerate((
            (pair_hbm, pair_ref), (gain_hbm, gain_ref), (bias_hbm, bias_ref),
            (w_hbm.at[:, : 4 * chan_count], w_ref), (valid_hbm, valid_ref),
        ))
    ]
    for fetch in fetches:
        fetch.start()
    row_start = lax.axis_index(axes) * row_count
    for fetch in fetches[:3]:
        fetch.wait()
    tokens = pair_ref[...].reshape(row_count * col_count, chan_count).astype(jnp.float32)
    normed = layer_norm(tokens, gain_ref[...], bias_ref[...], 1).astype(jnp.bfloat16)
    normed_ref[...] = normed
    for fetch in fetches[3:]:
        fetch.wait()
    projected = lax.dot_general(
        w_ref[...], normed, (((0,), (1,)), ((), ())),
        preferred_element_type=jnp.float32,
    )
    col_flags = valid_ref[...].astype(jnp.float32)
    places = lax.broadcasted_iota(jnp.int32, col_flags.shape, 1)
    row_flags = [
        jnp.sum(jnp.where(places == row_start + r, col_flags, 0.0), axis=1, keepdims=True)
        for r in range(row_count)
    ]
    flags = jnp.concatenate([col_flags * row_flag for row_flag in row_flags], axis=1)
    for chan in range(0, chan_count, 8):
        a_gate, a, b_gate, b = (
            projected[i * chan_count + chan : i * chan_count + chan + 8] for i in range(4)
        )
        left = jax.nn.sigmoid(a_gate) * a * flags
        right = jax.nn.sigmoid(b_gate) * b * flags
        for half, block in enumerate(swap_halves(left, right)):
            for r in range(0, row_count, 2):
                rows = jnp.concatenate(
                    [block[:, (r + i) * col_count : (r + i + 1) * col_count] for i in range(2)], axis=0
                )
                out_ref[(chan // 4 + half) ^ hub, r * 8 : (r + 2) * 8, :] = rows.astype(jnp.bfloat16)


def receive_blocks(blocks_ref, held_ref):
    shards, rows, _ = blocks_ref.shape
    for i in range(shards):
        held_ref[(i ^ hub) * rows : ((i ^ hub) + 1) * rows, :] = blocks_ref[i].astype(jnp.float32)


def exchange(blocks):
    groups = [[i ^ hub for i in range(blocks.shape[0])]]
    return lax.all_to_all(
        blocks, axes, split_axis=0, concat_axis=0, axis_index_groups=groups, tiled=True
    )


def contract_kernel(
    blocks_ref, normed_ref, w_ref, gain_ref, bias_ref, w_out_ref,
    out_ref, gate_ref, scales_ref, weights_ref, held_ref,
):
    total = held_ref.shape[0] // 8
    receive_blocks(blocks_ref, held_ref)
    products = []
    for c in range(4):
        left = held_ref[pl.ds(c, total, stride=8), :].astype(jnp.bfloat16)
        right = held_ref[pl.ds(4 + c, total, stride=8), :].astype(jnp.bfloat16)
        products.append(
            lax.dot_general(
                left, right, (((1,), (1,)), ((), ())), preferred_element_type=jnp.float32
            )
        )
    for row in range(0, total, 8):
        pieces = [product[row : row + 8] for product in products]
        low, high = swap_halves(pieces[0], pieces[1]), swap_halves(pieces[2], pieces[3])
        for half in range(2):
            rows = jnp.concatenate([low[half], high[half]], axis=0)
            out_ref[(row // 4 + half) ^ hub] = rows.astype(jnp.bfloat16)
    chan_count = normed_ref.shape[1]
    gate = jnp.dot(normed_ref[...], w_ref[:, 4 * chan_count :], preferred_element_type=jnp.float32)
    gate_ref[...] = jax.nn.sigmoid(gate).astype(jnp.bfloat16)
    for i, vector_ref in enumerate((gain_ref, bias_ref)):
        scales_ref[i] = jnp.transpose(jnp.broadcast_to(vector_ref[...], scales_ref.shape[1:]))
    weights_ref[...] = w_out_ref[...]


def finish_kernel(blocks_ref, gate_ref, scales_ref, w_ref, out_ref, held_ref):
    row_count, col_count, chan_count = out_ref.shape
    receive_blocks(blocks_ref, held_ref)
    for r in range(row_count):
        triangle = held_ref[pl.ds(r, chan_count, stride=row_count), :]
        normed = layer_norm(triangle, scales_ref[0], scales_ref[1], 0).astype(jnp.bfloat16)
        result = lax.dot_general(
            normed, w_ref[...], (((0,), (0,)), ((), ())), preferred_element_type=jnp.float32
        )
        gate = gate_ref[r * col_count : (r + 1) * col_count, :].astype(jnp.float32)
        out_ref[r] = (gate * result).astype(jnp.bfloat16)


def local_blocks(pair, valid, norm_gain, norm_bias, w_proj, out_gain, out_bias, w_out):
    row_count, col_count, chan_count = pair.shape
    shards = lax.axis_size(axes)
    tokens = row_count * col_count
    vmem = pl.BlockSpec(memory_space=pltpu.VMEM)
    hbm = pl.BlockSpec(memory_space=pltpu.HBM)

    def line(vector):
        return vector.reshape(1, -1)

    def shaped(*dims):
        return jax.ShapeDtypeStruct(dims, jnp.bfloat16)

    def in_hbm(array):
        return pltpu.with_memory_space_constraint(array, pltpu.HBM)

    limit = pltpu.CompilerParams(vmem_limit_bytes=kernel_vmem)
    sides, normed = pl.pallas_call(
        project_kernel,
        out_shape=(shaped(shards, 8 * row_count, col_count), shaped(tokens, chan_count)),
        in_specs=[hbm] * 5,
        out_specs=(vmem,) * 2,
        scratch_shapes=[
            pltpu.VMEM(pair.shape, jnp.bfloat16),
            pltpu.VMEM((1, col_count), jnp.int32),
            pltpu.VMEM((1, chan_count), jnp.float32),
            pltpu.VMEM((1, chan_count), jnp.float32),
            pltpu.VMEM((chan_count, 4 * chan_count), jnp.bfloat16),
            pltpu.SemaphoreType.DMA((5,)),
        ],
        compiler_params=limit,
        name="project",
    )(*map(in_hbm, (pair, line(valid), line(norm_gain), line(norm_bias), w_proj)))
    sides = exchange(sides)
    triangle, gate_values, scales, weights = pl.pallas_call(
        contract_kernel,
        out_shape=(
            shaped(shards, 4 * row_count, col_count),
            shaped(tokens, chan_count),
            jax.ShapeDtypeStruct((2, chan_count, col_count), jnp.float32),
            shaped(chan_count, chan_count),
        ),
        in_specs=[vmem] * 6,
        out_specs=(vmem,) * 4,
        scratch_shapes=[pltpu.VMEM((8 * col_count, col_count), jnp.float32)],
        compiler_params=limit,
        name="contract",
    )(sides, normed, w_proj, line(out_gain), line(out_bias), w_out)
    triangle = exchange(triangle)
    return pl.pallas_call(
        finish_kernel,
        out_shape=shaped(row_count, col_count, chan_count),
        in_specs=[vmem] * 4,
        out_specs=vmem,
        scratch_shapes=[pltpu.VMEM((tokens, chan_count), jnp.float32)],
        compiler_params=limit,
        name="finish",
    )(triangle, gate_values, scales, weights)


def local_arrays(pair, valid, norm_gain, norm_bias, w_proj, out_gain, out_bias, w_out):
    row_count, col_count, chan_count = pair.shape
    row_start = lax.axis_index(("wide", "narrow")) * row_count
    col_start = lax.axis_index("sub") * col_count
    row_flags = lax.dynamic_slice_in_dim(valid, row_start, row_count, 0).astype(jnp.float32)
    col_flags = lax.dynamic_slice_in_dim(valid, col_start, col_count, 0).astype(jnp.float32)
    pair_flags = row_flags[:, None] * col_flags[None, :]
    normed = layer_norm(pair.astype(jnp.float32), norm_gain, norm_bias, 2).astype(jnp.bfloat16)
    projected = jnp.einsum(
        "rkc,cd->drk", normed, w_proj[:, : 4 * chan_count], preferred_element_type=jnp.float32
    )
    left_side = (
        jax.nn.sigmoid(projected[:chan_count]) * projected[chan_count : 2 * chan_count] * pair_flags
    ).astype(jnp.bfloat16)
    right_side = (
        jax.nn.sigmoid(projected[2 * chan_count : 3 * chan_count])
        * projected[3 * chan_count :]
        * pair_flags
    ).astype(jnp.bfloat16)
    gate_values = jax.nn.sigmoid(
        jnp.einsum(
            "rkc,cd->rkd", normed, w_proj[:, 4 * chan_count :], preferred_element_type=jnp.float32
        )
    ).astype(jnp.bfloat16)
    both_sides = jnp.stack([left_side, right_side], axis=1)
    both_group = lax.all_to_all(
        both_sides, ("wide", "narrow"), split_axis=0, concat_axis=2, tiled=True
    )
    left_group, right_group = both_group[:, 0], both_group[:, 1]
    partial_sums = jnp.einsum(
        "cik,cjk->cij", left_group, right_group, preferred_element_type=jnp.float32
    )
    summed = lax.psum_scatter(partial_sums, "sub", scatter_dimension=2, tiled=True).astype(
        jnp.bfloat16
    )
    returned = lax.all_to_all(summed, ("wide", "narrow"), split_axis=1, concat_axis=0, tiled=True)
    normed_out = layer_norm(
        returned.astype(jnp.float32), out_gain[:, None, None], out_bias[:, None, None], 0
    ).astype(jnp.bfloat16)
    result_out = jnp.einsum("crj,cd->rjd", normed_out, w_out, preferred_element_type=jnp.float32)
    return (gate_values.astype(jnp.float32) * result_out).astype(jnp.bfloat16)


def local(pair, *rest):
    row_count, col_count, chan_count = pair.shape
    shards = lax.axis_size(axes)
    fits = (
        lax.axis_size("sub") == 1
        and (row_count, col_count, chan_count) == (4, 128, 128)
        and shards * row_count == col_count
        and shards * 4 == chan_count
        and shards == hub + 1
    )
    return (local_blocks if fits else local_arrays)(pair, *rest)


def solution(mesh):
    in_specs = (
        P(("parts", "wide", "narrow"), "sub", None),
        P("parts"),
        P(),
        P(),
        P(),
        P(),
        P(),
        P(),
    )
    out_specs = P(("parts", "wide", "narrow"), "sub", None)
    return jax.shard_map(local, mesh=mesh, in_specs=in_specs, out_specs=out_specs, check_vma=False)
```

```python
import functools

import jax
import jax.numpy as jnp
from jax import lax
from jax.experimental import pallas as pl
from jax.experimental.pallas import tpu as pltpu
from jax.sharding import PartitionSpec as P

epsilon = 1e-05
axes = ("wide", "narrow")
kernel_vmem = 8 * 2**20
hub = 31


def layer_norm(values, gain_vec, bias_vec, axis_dim):
    average = jnp.mean(values, axis=axis_dim, keepdims=True)
    centered = values - average
    variance = jnp.mean(centered * centered, axis=axis_dim, keepdims=True)
    return centered * lax.rsqrt(variance + epsilon) * gain_vec + bias_vec


def swap_halves(low, high):
    first = lax.broadcasted_iota(jnp.int32, low.shape, 0) < 4
    return (
        jnp.where(first, low, pltpu.roll(high, 4, 0)),
        jnp.where(first, pltpu.roll(low, 4, 0), high),
    )


def project_kernel(
    pair_hbm, valid_hbm, gain_hbm, bias_hbm, w_hbm, out_gain_hbm, out_bias_hbm, w_out_hbm,
    out_ref, normed_ref, w_gate_ref, out_gain_ref, out_bias_ref, w_out_ref,
    pair_ref, valid_ref, gain_ref, bias_ref, w_ref, sems,
):
    row_count, col_count, chan_count = pair_ref.shape
    fetches = [
        pltpu.make_async_copy(source, held, sems.at[i])
        for i, (source, held) in enumerate((
            (pair_hbm, pair_ref), (gain_hbm, gain_ref), (bias_hbm, bias_ref),
            (w_hbm.at[:, : 4 * chan_count], w_ref), (valid_hbm, valid_ref),
            (w_hbm.at[:, 4 * chan_count :], w_gate_ref), (out_gain_hbm, out_gain_ref),
            (out_bias_hbm, out_bias_ref), (w_out_hbm, w_out_ref),
        ))
    ]
    for fetch in fetches:
        fetch.start()
    row_start = lax.axis_index(axes) * row_count
    for fetch in fetches[:3]:
        fetch.wait()
    tokens = pair_ref[...].reshape(row_count * col_count, chan_count).astype(jnp.float32)
    normed = layer_norm(tokens, gain_ref[...], bias_ref[...], 1).astype(jnp.bfloat16)
    normed_ref[...] = normed
    for fetch in fetches[3:5]:
        fetch.wait()
    projected = lax.dot_general(
        w_ref[...], normed, (((0,), (1,)), ((), ())),
        preferred_element_type=jnp.float32,
    )
    col_flags = valid_ref[...].astype(jnp.float32)
    places = lax.broadcasted_iota(jnp.int32, col_flags.shape, 1)
    row_flags = [
        jnp.sum(jnp.where(places == row_start + r, col_flags, 0.0), axis=1, keepdims=True)
        for r in range(row_count)
    ]
    flags = jnp.concatenate([col_flags * row_flag for row_flag in row_flags], axis=1)
    for chan in range(0, chan_count, 8):
        a_gate, a, b_gate, b = (
            projected[i * chan_count + chan : i * chan_count + chan + 8] for i in range(4)
        )
        left = jax.nn.sigmoid(a_gate) * a * flags
        right = jax.nn.sigmoid(b_gate) * b * flags
        for half, block in enumerate(swap_halves(left, right)):
            for r in range(0, row_count, 2):
                rows = jnp.concatenate(
                    [block[:, (r + i) * col_count : (r + i + 1) * col_count] for i in range(2)], axis=0
                )
                out_ref[(chan // 4 + half) ^ hub, r * 8 : (r + 2) * 8, :] = rows.astype(jnp.bfloat16)
    for fetch in fetches[5:]:
        fetch.wait()


def receive_blocks(blocks_ref, held_ref):
    shards, rows, _ = blocks_ref.shape
    for i in range(shards):
        held_ref[(i ^ hub) * rows : ((i ^ hub) + 1) * rows, :] = blocks_ref[i].astype(jnp.float32)


def exchange(blocks):
    groups = [[i ^ hub for i in range(blocks.shape[0])]]
    return lax.all_to_all(
        blocks, axes, split_axis=0, concat_axis=0, axis_index_groups=groups, tiled=True
    )


def contract_kernel(
    blocks_ref, normed_ref, w_gate_ref, gain_ref, bias_ref,
    out_ref, gate_ref, scales_ref, held_ref,
):
    total = held_ref.shape[0] // 8
    receive_blocks(blocks_ref, held_ref)
    products = []
    for c in range(4):
        left = held_ref[pl.ds(c, total, stride=8), :].astype(jnp.bfloat16)
        right = held_ref[pl.ds(4 + c, total, stride=8), :].astype(jnp.bfloat16)
        products.append(
            lax.dot_general(
                left, right, (((1,), (1,)), ((), ())), preferred_element_type=jnp.float32
            )
        )
    for row in range(0, total, 8):
        pieces = [product[row : row + 8] for product in products]
        low, high = swap_halves(pieces[0], pieces[1]), swap_halves(pieces[2], pieces[3])
        for half in range(2):
            rows = jnp.concatenate([low[half], high[half]], axis=0)
            out_ref[(row // 4 + half) ^ hub] = rows.astype(jnp.bfloat16)
    gate = jnp.dot(normed_ref[...], w_gate_ref[...], preferred_element_type=jnp.float32)
    gate_ref[...] = jax.nn.sigmoid(gate).astype(jnp.bfloat16)
    for i, vector_ref in enumerate((gain_ref, bias_ref)):
        scales_ref[i] = jnp.transpose(jnp.broadcast_to(vector_ref[...], scales_ref.shape[1:]))


def finish_kernel(blocks_ref, gate_ref, scales_ref, w_ref, out_ref, held_ref):
    row_count, col_count, chan_count = out_ref.shape
    receive_blocks(blocks_ref, held_ref)
    for r in range(row_count):
        triangle = held_ref[pl.ds(r, chan_count, stride=row_count), :]
        normed = layer_norm(triangle, scales_ref[0], scales_ref[1], 0).astype(jnp.bfloat16)
        result = lax.dot_general(
            normed, w_ref[...], (((0,), (0,)), ((), ())), preferred_element_type=jnp.float32
        )
        gate = gate_ref[r * col_count : (r + 1) * col_count, :].astype(jnp.float32)
        out_ref[r] = (gate * result).astype(jnp.bfloat16)


def local_blocks(pair, valid, norm_gain, norm_bias, w_proj, out_gain, out_bias, w_out):
    row_count, col_count, chan_count = pair.shape
    shards = lax.axis_size(axes)
    tokens = row_count * col_count
    vmem = pl.BlockSpec(memory_space=pltpu.VMEM)
    hbm = pl.BlockSpec(memory_space=pltpu.HBM)

    def line(vector):
        return vector.reshape(1, -1)

    def shaped(*dims):
        return jax.ShapeDtypeStruct(dims, jnp.bfloat16)

    def in_hbm(array):
        return pltpu.with_memory_space_constraint(array, pltpu.HBM)

    limit = pltpu.CompilerParams(vmem_limit_bytes=kernel_vmem)
    vector = jax.ShapeDtypeStruct((1, chan_count), jnp.float32)
    square = shaped(chan_count, chan_count)
    sides, normed, w_gate, out_gain, out_bias, w_out = pl.pallas_call(
        project_kernel,
        out_shape=(
            shaped(shards, 8 * row_count, col_count), shaped(tokens, chan_count),
            square, vector, vector, square,
        ),
        in_specs=[hbm] * 8,
        out_specs=(vmem,) * 6,
        scratch_shapes=[
            pltpu.VMEM(pair.shape, jnp.bfloat16),
            pltpu.VMEM((1, col_count), jnp.int32),
            pltpu.VMEM((1, chan_count), jnp.float32),
            pltpu.VMEM((1, chan_count), jnp.float32),
            pltpu.VMEM((chan_count, 4 * chan_count), jnp.bfloat16),
            pltpu.SemaphoreType.DMA((9,)),
        ],
        compiler_params=limit,
        name="project",
    )(*map(in_hbm, (
        pair, line(valid), line(norm_gain), line(norm_bias), w_proj,
        line(out_gain), line(out_bias), w_out,
    )))
    sides = exchange(sides)
    triangle, gate_values, scales = pl.pallas_call(
        contract_kernel,
        out_shape=(
            shaped(shards, 4 * row_count, col_count),
            shaped(tokens, chan_count),
            jax.ShapeDtypeStruct((2, chan_count, col_count), jnp.float32),
        ),
        in_specs=[vmem] * 5,
        out_specs=(vmem,) * 3,
        scratch_shapes=[pltpu.VMEM((8 * col_count, col_count), jnp.float32)],
        compiler_params=limit,
        name="contract",
    )(sides, normed, w_gate, out_gain, out_bias)
    triangle = exchange(triangle)
    return pl.pallas_call(
        finish_kernel,
        out_shape=shaped(row_count, col_count, chan_count),
        in_specs=[vmem] * 4,
        out_specs=vmem,
        scratch_shapes=[pltpu.VMEM((tokens, chan_count), jnp.float32)],
        compiler_params=limit,
        name="finish",
    )(triangle, gate_values, scales, w_out)


def local_arrays(pair, valid, norm_gain, norm_bias, w_proj, out_gain, out_bias, w_out):
    row_count, col_count, chan_count = pair.shape
    row_start = lax.axis_index(("wide", "narrow")) * row_count
    col_start = lax.axis_index("sub") * col_count
    row_flags = lax.dynamic_slice_in_dim(valid, row_start, row_count, 0).astype(jnp.float32)
    col_flags = lax.dynamic_slice_in_dim(valid, col_start, col_count, 0).astype(jnp.float32)
    pair_flags = row_flags[:, None] * col_flags[None, :]
    normed = layer_norm(pair.astype(jnp.float32), norm_gain, norm_bias, 2).astype(jnp.bfloat16)
    projected = jnp.einsum(
        "rkc,cd->drk", normed, w_proj[:, : 4 * chan_count], preferred_element_type=jnp.float32
    )
    left_side = (
        jax.nn.sigmoid(projected[:chan_count]) * projected[chan_count : 2 * chan_count] * pair_flags
    ).astype(jnp.bfloat16)
    right_side = (
        jax.nn.sigmoid(projected[2 * chan_count : 3 * chan_count])
        * projected[3 * chan_count :]
        * pair_flags
    ).astype(jnp.bfloat16)
    gate_values = jax.nn.sigmoid(
        jnp.einsum(
            "rkc,cd->rkd", normed, w_proj[:, 4 * chan_count :], preferred_element_type=jnp.float32
        )
    ).astype(jnp.bfloat16)
    both_sides = jnp.stack([left_side, right_side], axis=1)
    both_group = lax.all_to_all(
        both_sides, ("wide", "narrow"), split_axis=0, concat_axis=2, tiled=True
    )
    left_group, right_group = both_group[:, 0], both_group[:, 1]
    partial_sums = jnp.einsum(
        "cik,cjk->cij", left_group, right_group, preferred_element_type=jnp.float32
    )
    summed = lax.psum_scatter(partial_sums, "sub", scatter_dimension=2, tiled=True).astype(
        jnp.bfloat16
    )
    returned = lax.all_to_all(summed, ("wide", "narrow"), split_axis=1, concat_axis=0, tiled=True)
    normed_out = layer_norm(
        returned.astype(jnp.float32), out_gain[:, None, None], out_bias[:, None, None], 0
    ).astype(jnp.bfloat16)
    result_out = jnp.einsum("crj,cd->rjd", normed_out, w_out, preferred_element_type=jnp.float32)
    return (gate_values.astype(jnp.float32) * result_out).astype(jnp.bfloat16)


def local(pair, *rest):
    row_count, col_count, chan_count = pair.shape
    shards = lax.axis_size(axes)
    fits = (
        lax.axis_size("sub") == 1
        and (row_count, col_count, chan_count) == (4, 128, 128)
        and shards * row_count == col_count
        and shards * 4 == chan_count
        and shards == hub + 1
    )
    return (local_blocks if fits else local_arrays)(pair, *rest)


def solution(mesh):
    in_specs = (
        P(("parts", "wide", "narrow"), "sub", None),
        P("parts"),
        P(),
        P(),
        P(),
        P(),
        P(),
        P(),
    )
    out_specs = P(("parts", "wide", "narrow"), "sub", None)
    return jax.shard_map(local, mesh=mesh, in_specs=in_specs, out_specs=out_specs, check_vma=False)
```

```python
import functools

import jax
import jax.numpy as jnp
from jax import lax
from jax.experimental import pallas as pl
from jax.experimental.pallas import tpu as pltpu
from jax.sharding import PartitionSpec as P

epsilon = 1e-05
axes = ("wide", "narrow")
kernel_vmem = 8 * 2**20
hub = 31


def layer_norm(values, gain_vec, bias_vec, axis_dim):
    average = jnp.mean(values, axis=axis_dim, keepdims=True)
    centered = values - average
    variance = jnp.mean(centered * centered, axis=axis_dim, keepdims=True)
    return centered * lax.rsqrt(variance + epsilon) * gain_vec + bias_vec


def sigmoid(values):
    return 0.5 + 0.5 * jnp.tanh(0.5 * values)


def swap_halves(low, high):
    first = lax.broadcasted_iota(jnp.int32, low.shape, 0) < 4
    return (
        jnp.where(first, low, pltpu.roll(high, 4, 0)),
        jnp.where(first, pltpu.roll(low, 4, 0), high),
    )


def project_kernel(
    pair_hbm, valid_hbm, gain_hbm, bias_hbm, w_hbm, out_gain_hbm, out_bias_hbm, w_out_hbm,
    out_ref, normed_ref, w_gate_ref, out_gain_ref, out_bias_ref, w_out_ref,
    pair_ref, valid_ref, gain_ref, bias_ref, w_ref, sems,
):
    row_count, col_count, chan_count = pair_ref.shape
    quarter = chan_count // 4
    pairs = [(pair_hbm.at[r], pair_ref.at[r]) for r in range(row_count)]
    for i in range(0, chan_count, quarter):
        rows = pl.ds(i, quarter)
        pairs.append((w_hbm.at[rows, : 4 * chan_count], w_ref.at[rows]))
    pairs += [(gain_hbm, gain_ref), (bias_hbm, bias_ref), (valid_hbm, valid_ref)]
    needed = len(pairs)
    pairs += [
        (w_hbm.at[:, 4 * chan_count :], w_gate_ref), (out_gain_hbm, out_gain_ref),
        (out_bias_hbm, out_bias_ref), (w_out_hbm, w_out_ref),
    ]
    fetches = [
        pltpu.make_async_copy(source, held, sems.at[i]) for i, (source, held) in enumerate(pairs)
    ]
    for fetch in fetches:
        fetch.start()
    row_start = lax.axis_index(axes) * row_count
    for fetch in fetches[:needed]:
        fetch.wait()
    tokens = pair_ref[...].reshape(row_count * col_count, chan_count).astype(jnp.float32)
    normed = layer_norm(tokens, gain_ref[...], bias_ref[...], 1).astype(jnp.bfloat16)
    normed_ref[...] = normed
    projected = lax.dot_general(
        w_ref[...], normed, (((0,), (1,)), ((), ())),
        preferred_element_type=jnp.float32,
    )
    col_flags = valid_ref[...].astype(jnp.float32)
    places = lax.broadcasted_iota(jnp.int32, col_flags.shape, 1)
    row_flags = [
        jnp.sum(jnp.where(places == row_start + r, col_flags, 0.0), axis=1, keepdims=True)
        for r in range(row_count)
    ]
    flags = jnp.concatenate([col_flags * row_flag for row_flag in row_flags], axis=1)
    for chan in range(0, chan_count, 8):
        a_gate, a, b_gate, b = (
            projected[i * chan_count + chan : i * chan_count + chan + 8] for i in range(4)
        )
        left = sigmoid(a_gate) * a * flags
        right = sigmoid(b_gate) * b * flags
        for half, block in enumerate(swap_halves(left, right)):
            for r in range(0, row_count, 2):
                rows = jnp.concatenate(
                    [block[:, (r + i) * col_count : (r + i + 1) * col_count] for i in range(2)], axis=0
                )
                out_ref[(chan // 4 + half) ^ hub, r * 8 : (r + 2) * 8, :] = rows.astype(jnp.bfloat16)
    for fetch in fetches[needed:]:
        fetch.wait()


def receive_blocks(blocks_ref, held_ref):
    shards, rows, _ = blocks_ref.shape
    for i in range(shards):
        held_ref[(i ^ hub) * rows : ((i ^ hub) + 1) * rows, :] = blocks_ref[i].astype(jnp.float32)


def exchange(blocks):
    groups = [[i ^ hub for i in range(blocks.shape[0])]]
    return lax.all_to_all(
        blocks, axes, split_axis=0, concat_axis=0, axis_index_groups=groups, tiled=True
    )


def contract_kernel(
    blocks_ref, normed_ref, w_gate_ref, gain_ref, bias_ref,
    out_ref, gate_ref, scales_ref, held_ref,
):
    total = held_ref.shape[0] // 8
    receive_blocks(blocks_ref, held_ref)
    products = []
    for c in range(4):
        left = held_ref[pl.ds(c, total, stride=8), :].astype(jnp.bfloat16)
        right = held_ref[pl.ds(4 + c, total, stride=8), :].astype(jnp.bfloat16)
        products.append(
            lax.dot_general(
                left, right, (((1,), (1,)), ((), ())), preferred_element_type=jnp.float32
            )
        )
    for row in range(0, total, 8):
        pieces = [product[row : row + 8] for product in products]
        low, high = swap_halves(pieces[0], pieces[1]), swap_halves(pieces[2], pieces[3])
        for half in range(2):
            rows = jnp.concatenate([low[half], high[half]], axis=0)
            out_ref[(row // 4 + half) ^ hub] = rows.astype(jnp.bfloat16)
    gate = jnp.dot(normed_ref[...], w_gate_ref[...], preferred_element_type=jnp.float32)
    gate_ref[...] = sigmoid(gate).astype(jnp.bfloat16)
    for i, vector_ref in enumerate((gain_ref, bias_ref)):
        scales_ref[i] = jnp.transpose(jnp.broadcast_to(vector_ref[...], scales_ref.shape[1:]))


def finish_kernel(blocks_ref, gate_ref, scales_ref, w_ref, out_ref, held_ref):
    row_count, col_count, chan_count = out_ref.shape
    receive_blocks(blocks_ref, held_ref)
    for r in range(row_count):
        triangle = held_ref[pl.ds(r, chan_count, stride=row_count), :]
        normed = layer_norm(triangle, scales_ref[0], scales_ref[1], 0).astype(jnp.bfloat16)
        result = lax.dot_general(
            normed, w_ref[...], (((0,), (0,)), ((), ())), preferred_element_type=jnp.float32
        )
        gate = gate_ref[r * col_count : (r + 1) * col_count, :].astype(jnp.float32)
        out_ref[r] = (gate * result).astype(jnp.bfloat16)


def local_blocks(pair, valid, norm_gain, norm_bias, w_proj, out_gain, out_bias, w_out):
    row_count, col_count, chan_count = pair.shape
    shards = lax.axis_size(axes)
    tokens = row_count * col_count
    vmem = pl.BlockSpec(memory_space=pltpu.VMEM)
    hbm = pl.BlockSpec(memory_space=pltpu.HBM)

    def line(vector):
        return vector.reshape(1, -1)

    def shaped(*dims):
        return jax.ShapeDtypeStruct(dims, jnp.bfloat16)

    def in_hbm(array):
        return pltpu.with_memory_space_constraint(array, pltpu.HBM)

    limit = pltpu.CompilerParams(vmem_limit_bytes=kernel_vmem)
    vector = jax.ShapeDtypeStruct((1, chan_count), jnp.float32)
    square = shaped(chan_count, chan_count)
    sides, normed, w_gate, out_gain, out_bias, w_out = pl.pallas_call(
        project_kernel,
        out_shape=(
            shaped(shards, 8 * row_count, col_count), shaped(tokens, chan_count),
            square, vector, vector, square,
        ),
        in_specs=[hbm] * 8,
        out_specs=(vmem,) * 6,
        scratch_shapes=[
            pltpu.VMEM(pair.shape, jnp.bfloat16),
            pltpu.VMEM((1, col_count), jnp.int32),
            pltpu.VMEM((1, chan_count), jnp.float32),
            pltpu.VMEM((1, chan_count), jnp.float32),
            pltpu.VMEM((chan_count, 4 * chan_count), jnp.bfloat16),
            pltpu.SemaphoreType.DMA((row_count + 11,)),
        ],
        compiler_params=limit,
        name="project",
    )(*map(in_hbm, (
        pair, line(valid), line(norm_gain), line(norm_bias), w_proj,
        line(out_gain), line(out_bias), w_out,
    )))
    sides = exchange(sides)
    triangle, gate_values, scales = pl.pallas_call(
        contract_kernel,
        out_shape=(
            shaped(shards, 4 * row_count, col_count),
            shaped(tokens, chan_count),
            jax.ShapeDtypeStruct((2, chan_count, col_count), jnp.float32),
        ),
        in_specs=[vmem] * 5,
        out_specs=(vmem,) * 3,
        scratch_shapes=[pltpu.VMEM((8 * col_count, col_count), jnp.float32)],
        compiler_params=limit,
        name="contract",
    )(sides, normed, w_gate, out_gain, out_bias)
    triangle = exchange(triangle)
    return pl.pallas_call(
        finish_kernel,
        out_shape=shaped(row_count, col_count, chan_count),
        in_specs=[vmem] * 4,
        out_specs=vmem,
        scratch_shapes=[pltpu.VMEM((tokens, chan_count), jnp.float32)],
        compiler_params=limit,
        name="finish",
    )(triangle, gate_values, scales, w_out)


def local_arrays(pair, valid, norm_gain, norm_bias, w_proj, out_gain, out_bias, w_out):
    row_count, col_count, chan_count = pair.shape
    row_start = lax.axis_index(("wide", "narrow")) * row_count
    col_start = lax.axis_index("sub") * col_count
    row_flags = lax.dynamic_slice_in_dim(valid, row_start, row_count, 0).astype(jnp.float32)
    col_flags = lax.dynamic_slice_in_dim(valid, col_start, col_count, 0).astype(jnp.float32)
    pair_flags = row_flags[:, None] * col_flags[None, :]
    normed = layer_norm(pair.astype(jnp.float32), norm_gain, norm_bias, 2).astype(jnp.bfloat16)
    projected = jnp.einsum(
        "rkc,cd->drk", normed, w_proj[:, : 4 * chan_count], preferred_element_type=jnp.float32
    )
    left_side = (
        jax.nn.sigmoid(projected[:chan_count]) * projected[chan_count : 2 * chan_count] * pair_flags
    ).astype(jnp.bfloat16)
    right_side = (
        jax.nn.sigmoid(projected[2 * chan_count : 3 * chan_count])
        * projected[3 * chan_count :]
        * pair_flags
    ).astype(jnp.bfloat16)
    gate_values = jax.nn.sigmoid(
        jnp.einsum(
            "rkc,cd->rkd", normed, w_proj[:, 4 * chan_count :], preferred_element_type=jnp.float32
        )
    ).astype(jnp.bfloat16)
    both_sides = jnp.stack([left_side, right_side], axis=1)
    both_group = lax.all_to_all(
        both_sides, ("wide", "narrow"), split_axis=0, concat_axis=2, tiled=True
    )
    left_group, right_group = both_group[:, 0], both_group[:, 1]
    partial_sums = jnp.einsum(
        "cik,cjk->cij", left_group, right_group, preferred_element_type=jnp.float32
    )
    summed = lax.psum_scatter(partial_sums, "sub", scatter_dimension=2, tiled=True).astype(
        jnp.bfloat16
    )
    returned = lax.all_to_all(summed, ("wide", "narrow"), split_axis=1, concat_axis=0, tiled=True)
    normed_out = layer_norm(
        returned.astype(jnp.float32), out_gain[:, None, None], out_bias[:, None, None], 0
    ).astype(jnp.bfloat16)
    result_out = jnp.einsum("crj,cd->rjd", normed_out, w_out, preferred_element_type=jnp.float32)
    return (gate_values.astype(jnp.float32) * result_out).astype(jnp.bfloat16)


def local(pair, *rest):
    row_count, col_count, chan_count = pair.shape
    shards = lax.axis_size(axes)
    fits = (
        lax.axis_size("sub") == 1
        and (row_count, col_count, chan_count) == (4, 128, 128)
        and shards * row_count == col_count
        and shards * 4 == chan_count
        and shards == hub + 1
    )
    return (local_blocks if fits else local_arrays)(pair, *rest)


def solution(mesh):
    in_specs = (
        P(("parts", "wide", "narrow"), "sub", None),
        P("parts"),
        P(),
        P(),
        P(),
        P(),
        P(),
        P(),
    )
    out_specs = P(("parts", "wide", "narrow"), "sub", None)
    return jax.shard_map(local, mesh=mesh, in_specs=in_specs, out_specs=out_specs, check_vma=False)
```

```python
import functools

import jax
import jax.numpy as jnp
from jax import lax
from jax.experimental import pallas as pl
from jax.experimental.pallas import tpu as pltpu
from jax.sharding import PartitionSpec as P

epsilon = 1e-05
axes = ("wide", "narrow")
kernel_vmem = 8 * 2**20
hub = 24


def layer_norm(values, gain_vec, bias_vec, axis_dim):
    average = jnp.mean(values, axis=axis_dim, keepdims=True)
    centered = values - average
    variance = jnp.mean(centered * centered, axis=axis_dim, keepdims=True)
    return centered * lax.rsqrt(variance + epsilon) * gain_vec + bias_vec


def sigmoid(values):
    return 0.5 + 0.5 * jnp.tanh(0.5 * values)


def swap_halves(low, high):
    first = lax.broadcasted_iota(jnp.int32, low.shape, 0) < 4
    return (
        jnp.where(first, low, pltpu.roll(high, 4, 0)),
        jnp.where(first, pltpu.roll(low, 4, 0), high),
    )


def project_kernel(
    pair_hbm, valid_hbm, gain_hbm, bias_hbm, w_hbm, out_gain_hbm, out_bias_hbm, w_out_hbm,
    out_ref, normed_ref, w_gate_ref, out_gain_ref, out_bias_ref, w_out_ref,
    pair_ref, valid_ref, gain_ref, bias_ref, w_ref, sems,
):
    row_count, col_count, chan_count = pair_ref.shape
    quarter = chan_count // 4
    pairs = [(pair_hbm.at[r], pair_ref.at[r]) for r in range(row_count)]
    for i in range(0, chan_count, quarter):
        rows = pl.ds(i, quarter)
        pairs.append((w_hbm.at[rows, : 4 * chan_count], w_ref.at[rows]))
    pairs += [(gain_hbm, gain_ref), (bias_hbm, bias_ref), (valid_hbm, valid_ref)]
    needed = len(pairs)
    pairs += [
        (w_hbm.at[:, 4 * chan_count :], w_gate_ref), (out_gain_hbm, out_gain_ref),
        (out_bias_hbm, out_bias_ref), (w_out_hbm, w_out_ref),
    ]
    fetches = [
        pltpu.make_async_copy(source, held, sems.at[i]) for i, (source, held) in enumerate(pairs)
    ]
    for fetch in fetches:
        fetch.start()
    row_start = lax.axis_index(axes) * row_count
    for fetch in fetches[:needed]:
        fetch.wait()
    tokens = pair_ref[...].reshape(row_count * col_count, chan_count).astype(jnp.float32)
    normed = layer_norm(tokens, gain_ref[...], bias_ref[...], 1).astype(jnp.bfloat16)
    normed_ref[...] = normed
    projected = lax.dot_general(
        w_ref[...], normed, (((0,), (1,)), ((), ())),
        preferred_element_type=jnp.float32,
    )
    col_flags = valid_ref[...].astype(jnp.float32)
    places = lax.broadcasted_iota(jnp.int32, col_flags.shape, 1)
    row_flags = [
        jnp.sum(jnp.where(places == row_start + r, col_flags, 0.0), axis=1, keepdims=True)
        for r in range(row_count)
    ]
    flags = jnp.concatenate([col_flags * row_flag for row_flag in row_flags], axis=1)
    for chan in range(0, chan_count, 8):
        a_gate, a, b_gate, b = (
            projected[i * chan_count + chan : i * chan_count + chan + 8] for i in range(4)
        )
        left = sigmoid(a_gate) * a * flags
        right = sigmoid(b_gate) * b * flags
        for half, block in enumerate(swap_halves(left, right)):
            for r in range(0, row_count, 2):
                rows = jnp.concatenate(
                    [block[:, (r + i) * col_count : (r + i + 1) * col_count] for i in range(2)], axis=0
                )
                out_ref[(chan // 4 + half) ^ hub, r * 8 : (r + 2) * 8, :] = rows.astype(jnp.bfloat16)
    for fetch in fetches[needed:]:
        fetch.wait()


def receive_blocks(blocks_ref, held_ref):
    shards, rows, _ = blocks_ref.shape
    for i in range(shards):
        held_ref[(i ^ hub) * rows : ((i ^ hub) + 1) * rows, :] = blocks_ref[i].astype(jnp.float32)


def exchange(blocks):
    groups = [[i ^ hub for i in range(blocks.shape[0])]]
    return lax.all_to_all(
        blocks, axes, split_axis=0, concat_axis=0, axis_index_groups=groups, tiled=True
    )


def contract_kernel(
    blocks_ref, normed_ref, w_gate_ref, gain_ref, bias_ref,
    out_ref, gate_ref, scales_ref, held_ref,
):
    total = held_ref.shape[0] // 8
    receive_blocks(blocks_ref, held_ref)
    products = []
    for c in range(4):
        left = held_ref[pl.ds(c, total, stride=8), :].astype(jnp.bfloat16)
        right = held_ref[pl.ds(4 + c, total, stride=8), :].astype(jnp.bfloat16)
        products.append(
            lax.dot_general(
                left, right, (((1,), (1,)), ((), ())), preferred_element_type=jnp.float32
            )
        )
    for row in range(0, total, 8):
        pieces = [product[row : row + 8] for product in products]
        low, high = swap_halves(pieces[0], pieces[1]), swap_halves(pieces[2], pieces[3])
        for half in range(2):
            rows = jnp.concatenate([low[half], high[half]], axis=0)
            out_ref[(row // 4 + half) ^ hub] = rows.astype(jnp.bfloat16)
    gate = jnp.dot(normed_ref[...], w_gate_ref[...], preferred_element_type=jnp.float32)
    gate_ref[...] = sigmoid(gate).astype(jnp.bfloat16)
    for i, vector_ref in enumerate((gain_ref, bias_ref)):
        scales_ref[i] = jnp.transpose(jnp.broadcast_to(vector_ref[...], scales_ref.shape[1:]))


def finish_kernel(blocks_ref, gate_ref, scales_ref, w_ref, out_ref, held_ref):
    row_count, col_count, chan_count = out_ref.shape
    receive_blocks(blocks_ref, held_ref)
    for r in range(row_count):
        triangle = held_ref[pl.ds(r, chan_count, stride=row_count), :]
        normed = layer_norm(triangle, scales_ref[0], scales_ref[1], 0).astype(jnp.bfloat16)
        result = lax.dot_general(
            normed, w_ref[...], (((0,), (0,)), ((), ())), preferred_element_type=jnp.float32
        )
        gate = gate_ref[r * col_count : (r + 1) * col_count, :].astype(jnp.float32)
        out_ref[r] = (gate * result).astype(jnp.bfloat16)


def local_blocks(pair, valid, norm_gain, norm_bias, w_proj, out_gain, out_bias, w_out):
    row_count, col_count, chan_count = pair.shape
    shards = lax.axis_size(axes)
    tokens = row_count * col_count
    vmem = pl.BlockSpec(memory_space=pltpu.VMEM)
    hbm = pl.BlockSpec(memory_space=pltpu.HBM)

    def line(vector):
        return vector.reshape(1, -1)

    def shaped(*dims):
        return jax.ShapeDtypeStruct(dims, jnp.bfloat16)

    def in_hbm(array):
        return pltpu.with_memory_space_constraint(array, pltpu.HBM)

    limit = pltpu.CompilerParams(vmem_limit_bytes=kernel_vmem)
    vector = jax.ShapeDtypeStruct((1, chan_count), jnp.float32)
    square = shaped(chan_count, chan_count)
    sides, normed, w_gate, out_gain, out_bias, w_out = pl.pallas_call(
        project_kernel,
        out_shape=(
            shaped(shards, 8 * row_count, col_count), shaped(tokens, chan_count),
            square, vector, vector, square,
        ),
        in_specs=[hbm] * 8,
        out_specs=(vmem,) * 6,
        scratch_shapes=[
            pltpu.VMEM(pair.shape, jnp.bfloat16),
            pltpu.VMEM((1, col_count), jnp.int32),
            pltpu.VMEM((1, chan_count), jnp.float32),
            pltpu.VMEM((1, chan_count), jnp.float32),
            pltpu.VMEM((chan_count, 4 * chan_count), jnp.bfloat16),
            pltpu.SemaphoreType.DMA((row_count + 11,)),
        ],
        compiler_params=limit,
        name="project",
    )(*map(in_hbm, (
        pair, line(valid), line(norm_gain), line(norm_bias), w_proj,
        line(out_gain), line(out_bias), w_out,
    )))
    sides = exchange(sides)
    triangle, gate_values, scales = pl.pallas_call(
        contract_kernel,
        out_shape=(
            shaped(shards, 4 * row_count, col_count),
            shaped(tokens, chan_count),
            jax.ShapeDtypeStruct((2, chan_count, col_count), jnp.float32),
        ),
        in_specs=[vmem] * 5,
        out_specs=(vmem,) * 3,
        scratch_shapes=[pltpu.VMEM((8 * col_count, col_count), jnp.float32)],
        compiler_params=limit,
        name="contract",
    )(sides, normed, w_gate, out_gain, out_bias)
    triangle = exchange(triangle)
    return pl.pallas_call(
        finish_kernel,
        out_shape=shaped(row_count, col_count, chan_count),
        in_specs=[vmem] * 4,
        out_specs=vmem,
        scratch_shapes=[pltpu.VMEM((tokens, chan_count), jnp.float32)],
        compiler_params=limit,
        name="finish",
    )(triangle, gate_values, scales, w_out)


def local_arrays(pair, valid, norm_gain, norm_bias, w_proj, out_gain, out_bias, w_out):
    row_count, col_count, chan_count = pair.shape
    row_start = lax.axis_index(("wide", "narrow")) * row_count
    col_start = lax.axis_index("sub") * col_count
    row_flags = lax.dynamic_slice_in_dim(valid, row_start, row_count, 0).astype(jnp.float32)
    col_flags = lax.dynamic_slice_in_dim(valid, col_start, col_count, 0).astype(jnp.float32)
    pair_flags = row_flags[:, None] * col_flags[None, :]
    normed = layer_norm(pair.astype(jnp.float32), norm_gain, norm_bias, 2).astype(jnp.bfloat16)
    projected = jnp.einsum(
        "rkc,cd->drk", normed, w_proj[:, : 4 * chan_count], preferred_element_type=jnp.float32
    )
    left_side = (
        jax.nn.sigmoid(projected[:chan_count]) * projected[chan_count : 2 * chan_count] * pair_flags
    ).astype(jnp.bfloat16)
    right_side = (
        jax.nn.sigmoid(projected[2 * chan_count : 3 * chan_count])
        * projected[3 * chan_count :]
        * pair_flags
    ).astype(jnp.bfloat16)
    gate_values = jax.nn.sigmoid(
        jnp.einsum(
            "rkc,cd->rkd", normed, w_proj[:, 4 * chan_count :], preferred_element_type=jnp.float32
        )
    ).astype(jnp.bfloat16)
    both_sides = jnp.stack([left_side, right_side], axis=1)
    both_group = lax.all_to_all(
        both_sides, ("wide", "narrow"), split_axis=0, concat_axis=2, tiled=True
    )
    left_group, right_group = both_group[:, 0], both_group[:, 1]
    partial_sums = jnp.einsum(
        "cik,cjk->cij", left_group, right_group, preferred_element_type=jnp.float32
    )
    summed = lax.psum_scatter(partial_sums, "sub", scatter_dimension=2, tiled=True).astype(
        jnp.bfloat16
    )
    returned = lax.all_to_all(summed, ("wide", "narrow"), split_axis=1, concat_axis=0, tiled=True)
    normed_out = layer_norm(
        returned.astype(jnp.float32), out_gain[:, None, None], out_bias[:, None, None], 0
    ).astype(jnp.bfloat16)
    result_out = jnp.einsum("crj,cd->rjd", normed_out, w_out, preferred_element_type=jnp.float32)
    return (gate_values.astype(jnp.float32) * result_out).astype(jnp.bfloat16)


def local(pair, *rest):
    row_count, col_count, chan_count = pair.shape
    shards = lax.axis_size(axes)
    fits = (
        lax.axis_size("sub") == 1
        and (row_count, col_count, chan_count) == (4, 128, 128)
        and shards * row_count == col_count
        and shards * 4 == chan_count
        and shards == 32
    )
    return (local_blocks if fits else local_arrays)(pair, *rest)


def solution(mesh):
    in_specs = (
        P(("parts", "wide", "narrow"), "sub", None),
        P("parts"),
        P(),
        P(),
        P(),
        P(),
        P(),
        P(),
    )
    out_specs = P(("parts", "wide", "narrow"), "sub", None)
    return jax.shard_map(local, mesh=mesh, in_specs=in_specs, out_specs=out_specs, check_vma=False)
```

```python
import functools

import jax
import jax.numpy as jnp
from jax import lax
from jax.experimental import pallas as pl
from jax.experimental.pallas import tpu as pltpu
from jax.sharding import PartitionSpec as P

epsilon = 1e-05
axes = ("wide", "narrow")
kernel_vmem = 8 * 2**20
hub = 7


def layer_norm(values, gain_vec, bias_vec, axis_dim):
    average = jnp.mean(values, axis=axis_dim, keepdims=True)
    centered = values - average
    variance = jnp.mean(centered * centered, axis=axis_dim, keepdims=True)
    return centered * lax.rsqrt(variance + epsilon) * gain_vec + bias_vec


def sigmoid(values):
    return 0.5 + 0.5 * jnp.tanh(0.5 * values)


def swap_halves(low, high):
    first = lax.broadcasted_iota(jnp.int32, low.shape, 0) < 4
    return (
        jnp.where(first, low, pltpu.roll(high, 4, 0)),
        jnp.where(first, pltpu.roll(low, 4, 0), high),
    )


def project_kernel(
    pair_hbm, valid_hbm, gain_hbm, bias_hbm, w_hbm, out_gain_hbm, out_bias_hbm, w_out_hbm,
    out_ref, normed_ref, w_gate_ref, out_gain_ref, out_bias_ref, w_out_ref,
    pair_ref, valid_ref, gain_ref, bias_ref, w_ref, sems,
):
    row_count, col_count, chan_count = pair_ref.shape
    quarter = chan_count // 4
    pairs = [(pair_hbm.at[r], pair_ref.at[r]) for r in range(row_count)]
    for i in range(0, chan_count, quarter):
        rows = pl.ds(i, quarter)
        pairs.append((w_hbm.at[rows, : 4 * chan_count], w_ref.at[rows]))
    pairs += [(gain_hbm, gain_ref), (bias_hbm, bias_ref), (valid_hbm, valid_ref)]
    needed = len(pairs)
    pairs += [
        (w_hbm.at[:, 4 * chan_count :], w_gate_ref), (out_gain_hbm, out_gain_ref),
        (out_bias_hbm, out_bias_ref), (w_out_hbm, w_out_ref),
    ]
    fetches = [
        pltpu.make_async_copy(source, held, sems.at[i]) for i, (source, held) in enumerate(pairs)
    ]
    for fetch in fetches:
        fetch.start()
    row_start = lax.axis_index(axes) * row_count
    for fetch in fetches[:needed]:
        fetch.wait()
    tokens = pair_ref[...].reshape(row_count * col_count, chan_count).astype(jnp.float32)
    normed = layer_norm(tokens, gain_ref[...], bias_ref[...], 1).astype(jnp.bfloat16)
    normed_ref[...] = normed
    projected = lax.dot_general(
        w_ref[...], normed, (((0,), (1,)), ((), ())),
        preferred_element_type=jnp.float32,
    )
    col_flags = valid_ref[...].astype(jnp.float32)
    places = lax.broadcasted_iota(jnp.int32, col_flags.shape, 1)
    row_flags = [
        jnp.sum(jnp.where(places == row_start + r, col_flags, 0.0), axis=1, keepdims=True)
        for r in range(row_count)
    ]
    flags = jnp.concatenate([col_flags * row_flag for row_flag in row_flags], axis=1)
    for chan in range(0, chan_count, 8):
        a_gate, a, b_gate, b = (
            projected[i * chan_count + chan : i * chan_count + chan + 8] for i in range(4)
        )
        left = sigmoid(a_gate) * a * flags
        right = sigmoid(b_gate) * b * flags
        for half, block in enumerate(swap_halves(left, right)):
            for r in range(0, row_count, 2):
                rows = jnp.concatenate(
                    [block[:, (r + i) * col_count : (r + i + 1) * col_count] for i in range(2)], axis=0
                )
                out_ref[(chan // 4 + half) ^ hub, r * 8 : (r + 2) * 8, :] = rows.astype(jnp.bfloat16)
    for fetch in fetches[needed:]:
        fetch.wait()


def receive_blocks(blocks_ref, held_ref):
    shards, rows, _ = blocks_ref.shape
    for i in range(shards):
        held_ref[(i ^ hub) * rows : ((i ^ hub) + 1) * rows, :] = blocks_ref[i].astype(jnp.float32)


def exchange(blocks):
    groups = [[i ^ hub for i in range(blocks.shape[0])]]
    return lax.all_to_all(
        blocks, axes, split_axis=0, concat_axis=0, axis_index_groups=groups, tiled=True
    )


def contract_kernel(
    blocks_ref, normed_ref, w_gate_ref, gain_ref, bias_ref,
    out_ref, gate_ref, scales_ref, held_ref,
):
    total = held_ref.shape[0] // 8
    receive_blocks(blocks_ref, held_ref)
    products = []
    for c in range(4):
        left = held_ref[pl.ds(c, total, stride=8), :].astype(jnp.bfloat16)
        right = held_ref[pl.ds(4 + c, total, stride=8), :].astype(jnp.bfloat16)
        products.append(
            lax.dot_general(
                left, right, (((1,), (1,)), ((), ())), preferred_element_type=jnp.float32
            )
        )
    for row in range(0, total, 8):
        pieces = [product[row : row + 8] for product in products]
        low, high = swap_halves(pieces[0], pieces[1]), swap_halves(pieces[2], pieces[3])
        for half in range(2):
            rows = jnp.concatenate([low[half], high[half]], axis=0)
            out_ref[(row // 4 + half) ^ hub] = rows.astype(jnp.bfloat16)
    gate = jnp.dot(normed_ref[...], w_gate_ref[...], preferred_element_type=jnp.float32)
    gate_ref[...] = sigmoid(gate).astype(jnp.bfloat16)
    for i, vector_ref in enumerate((gain_ref, bias_ref)):
        scales_ref[i] = jnp.transpose(jnp.broadcast_to(vector_ref[...], scales_ref.shape[1:]))


def finish_kernel(blocks_ref, gate_ref, scales_ref, w_ref, out_ref, held_ref):
    row_count, col_count, chan_count = out_ref.shape
    receive_blocks(blocks_ref, held_ref)
    for r in range(row_count):
        triangle = held_ref[pl.ds(r, chan_count, stride=row_count), :]
        normed = layer_norm(triangle, scales_ref[0], scales_ref[1], 0).astype(jnp.bfloat16)
        result = lax.dot_general(
            normed, w_ref[...], (((0,), (0,)), ((), ())), preferred_element_type=jnp.float32
        )
        gate = gate_ref[r * col_count : (r + 1) * col_count, :].astype(jnp.float32)
        out_ref[r] = (gate * result).astype(jnp.bfloat16)


def local_blocks(pair, valid, norm_gain, norm_bias, w_proj, out_gain, out_bias, w_out):
    row_count, col_count, chan_count = pair.shape
    shards = lax.axis_size(axes)
    tokens = row_count * col_count
    vmem = pl.BlockSpec(memory_space=pltpu.VMEM)
    hbm = pl.BlockSpec(memory_space=pltpu.HBM)

    def line(vector):
        return vector.reshape(1, -1)

    def shaped(*dims):
        return jax.ShapeDtypeStruct(dims, jnp.bfloat16)

    def in_hbm(array):
        return pltpu.with_memory_space_constraint(array, pltpu.HBM)

    limit = pltpu.CompilerParams(vmem_limit_bytes=kernel_vmem)
    vector = jax.ShapeDtypeStruct((1, chan_count), jnp.float32)
    square = shaped(chan_count, chan_count)
    sides, normed, w_gate, out_gain, out_bias, w_out = pl.pallas_call(
        project_kernel,
        out_shape=(
            shaped(shards, 8 * row_count, col_count), shaped(tokens, chan_count),
            square, vector, vector, square,
        ),
        in_specs=[hbm] * 8,
        out_specs=(vmem,) * 6,
        scratch_shapes=[
            pltpu.VMEM(pair.shape, jnp.bfloat16),
            pltpu.VMEM((1, col_count), jnp.int32),
            pltpu.VMEM((1, chan_count), jnp.float32),
            pltpu.VMEM((1, chan_count), jnp.float32),
            pltpu.VMEM((chan_count, 4 * chan_count), jnp.bfloat16),
            pltpu.SemaphoreType.DMA((row_count + 11,)),
        ],
        compiler_params=limit,
        name="project",
    )(*map(in_hbm, (
        pair, line(valid), line(norm_gain), line(norm_bias), w_proj,
        line(out_gain), line(out_bias), w_out,
    )))
    sides = exchange(sides)
    triangle, gate_values, scales = pl.pallas_call(
        contract_kernel,
        out_shape=(
            shaped(shards, 4 * row_count, col_count),
            shaped(tokens, chan_count),
            jax.ShapeDtypeStruct((2, chan_count, col_count), jnp.float32),
        ),
        in_specs=[vmem] * 5,
        out_specs=(vmem,) * 3,
        scratch_shapes=[pltpu.VMEM((8 * col_count, col_count), jnp.float32)],
        compiler_params=limit,
        name="contract",
    )(sides, normed, w_gate, out_gain, out_bias)
    triangle = exchange(triangle)
    return pl.pallas_call(
        finish_kernel,
        out_shape=shaped(row_count, col_count, chan_count),
        in_specs=[vmem] * 4,
        out_specs=vmem,
        scratch_shapes=[pltpu.VMEM((tokens, chan_count), jnp.float32)],
        compiler_params=limit,
        name="finish",
    )(triangle, gate_values, scales, w_out)


def local_arrays(pair, valid, norm_gain, norm_bias, w_proj, out_gain, out_bias, w_out):
    row_count, col_count, chan_count = pair.shape
    row_start = lax.axis_index(("wide", "narrow")) * row_count
    col_start = lax.axis_index("sub") * col_count
    row_flags = lax.dynamic_slice_in_dim(valid, row_start, row_count, 0).astype(jnp.float32)
    col_flags = lax.dynamic_slice_in_dim(valid, col_start, col_count, 0).astype(jnp.float32)
    pair_flags = row_flags[:, None] * col_flags[None, :]
    normed = layer_norm(pair.astype(jnp.float32), norm_gain, norm_bias, 2).astype(jnp.bfloat16)
    projected = jnp.einsum(
        "rkc,cd->drk", normed, w_proj[:, : 4 * chan_count], preferred_element_type=jnp.float32
    )
    left_side = (
        jax.nn.sigmoid(projected[:chan_count]) * projected[chan_count : 2 * chan_count] * pair_flags
    ).astype(jnp.bfloat16)
    right_side = (
        jax.nn.sigmoid(projected[2 * chan_count : 3 * chan_count])
        * projected[3 * chan_count :]
        * pair_flags
    ).astype(jnp.bfloat16)
    gate_values = jax.nn.sigmoid(
        jnp.einsum(
            "rkc,cd->rkd", normed, w_proj[:, 4 * chan_count :], preferred_element_type=jnp.float32
        )
    ).astype(jnp.bfloat16)
    both_sides = jnp.stack([left_side, right_side], axis=1)
    both_group = lax.all_to_all(
        both_sides, ("wide", "narrow"), split_axis=0, concat_axis=2, tiled=True
    )
    left_group, right_group = both_group[:, 0], both_group[:, 1]
    partial_sums = jnp.einsum(
        "cik,cjk->cij", left_group, right_group, preferred_element_type=jnp.float32
    )
    summed = lax.psum_scatter(partial_sums, "sub", scatter_dimension=2, tiled=True).astype(
        jnp.bfloat16
    )
    returned = lax.all_to_all(summed, ("wide", "narrow"), split_axis=1, concat_axis=0, tiled=True)
    normed_out = layer_norm(
        returned.astype(jnp.float32), out_gain[:, None, None], out_bias[:, None, None], 0
    ).astype(jnp.bfloat16)
    result_out = jnp.einsum("crj,cd->rjd", normed_out, w_out, preferred_element_type=jnp.float32)
    return (gate_values.astype(jnp.float32) * result_out).astype(jnp.bfloat16)


def local(pair, *rest):
    row_count, col_count, chan_count = pair.shape
    shards = lax.axis_size(axes)
    fits = (
        lax.axis_size("sub") == 1
        and (row_count, col_count, chan_count) == (4, 128, 128)
        and shards * row_count == col_count
        and shards * 4 == chan_count
        and shards == 32
    )
    return (local_blocks if fits else local_arrays)(pair, *rest)


def solution(mesh):
    in_specs = (
        P(("parts", "wide", "narrow"), "sub", None),
        P("parts"),
        P(),
        P(),
        P(),
        P(),
        P(),
        P(),
    )
    out_specs = P(("parts", "wide", "narrow"), "sub", None)
    return jax.shard_map(local, mesh=mesh, in_specs=in_specs, out_specs=out_specs, check_vma=False)
```

```python
import functools

import jax
import jax.numpy as jnp
from jax import lax
from jax.experimental import pallas as pl
from jax.experimental.pallas import tpu as pltpu
from jax.sharding import PartitionSpec as P

epsilon = 1e-05
axes = ("wide", "narrow")
kernel_vmem = 8 * 2**20
hub = 31


def layer_norm(values, gain_vec, bias_vec, axis_dim):
    average = jnp.mean(values, axis=axis_dim, keepdims=True)
    centered = values - average
    variance = jnp.mean(centered * centered, axis=axis_dim, keepdims=True)
    return centered * lax.rsqrt(variance + epsilon) * gain_vec + bias_vec


def sigmoid(values):
    return 0.5 + 0.5 * jnp.tanh(0.5 * values)


def swap_halves(low, high):
    first = lax.broadcasted_iota(jnp.int32, low.shape, 0) < 4
    return (
        jnp.where(first, low, pltpu.roll(high, 4, 0)),
        jnp.where(first, pltpu.roll(low, 4, 0), high),
    )


def project_kernel(
    pair_hbm, valid_hbm, gain_hbm, bias_hbm, w_hbm, out_gain_hbm, out_bias_hbm, w_out_hbm,
    out_ref, normed_ref, w_gate_ref, out_gain_ref, out_bias_ref, w_out_ref,
    pair_ref, valid_ref, gain_ref, bias_ref, w_ref, sems,
):
    row_count, col_count, chan_count = pair_ref.shape
    shards = out_ref.shape[0]
    quarter = chan_count // 4
    pairs = [(pair_hbm.at[r], pair_ref.at[r]) for r in range(row_count)]
    for i in range(0, chan_count, quarter):
        rows = pl.ds(i, quarter)
        pairs.append((w_hbm.at[rows, : 4 * chan_count], w_ref.at[rows]))
    pairs += [(gain_hbm, gain_ref), (bias_hbm, bias_ref), (valid_hbm, valid_ref)]
    needed = len(pairs)
    pairs += [
        (w_hbm.at[:, 4 * chan_count :], w_gate_ref), (out_gain_hbm, out_gain_ref),
        (out_bias_hbm, out_bias_ref), (w_out_hbm, w_out_ref),
    ]
    fetches = [
        pltpu.make_async_copy(source, held, sems.at[i]) for i, (source, held) in enumerate(pairs)
    ]
    for fetch in fetches:
        fetch.start()
    row_start = lax.axis_index(axes) * row_count
    place = lax.broadcasted_iota(jnp.int32, (2 * chan_count, 2 * chan_count), 0)
    column = lax.broadcasted_iota(jnp.int32, (2 * chan_count, 2 * chan_count), 1)
    wanted = (place >> 3) * 4 + (place & 3) + ((place >> 2) & 1) * chan_count
    spread = jnp.where(column == wanted, 1.0, 0.0).astype(jnp.bfloat16)
    for fetch in fetches[:needed]:
        fetch.wait()
    tokens = pair_ref[...].reshape(row_count * col_count, chan_count).astype(jnp.float32)
    normed = layer_norm(tokens, gain_ref[...], bias_ref[...], 1).astype(jnp.bfloat16)
    normed_ref[...] = normed
    def project(first):
        columns = [w_ref[:, i * chan_count : (i + 1) * chan_count] for i in (first, first + 2)]
        turned = lax.dot_general(
            spread, jnp.concatenate(columns, axis=1), (((1,), (1,)), ((), ())),
            preferred_element_type=jnp.float32,
        ).astype(jnp.bfloat16)
        return lax.dot_general(
            turned, normed, (((1,), (1,)), ((), ())), preferred_element_type=jnp.float32
        )

    col_flags = valid_ref[...].astype(jnp.float32)
    places = lax.broadcasted_iota(jnp.int32, col_flags.shape, 1)
    row_flags = [
        jnp.sum(jnp.where(places == row_start + r, col_flags, 0.0), axis=1, keepdims=True)
        for r in range(row_count)
    ]
    flags = jnp.concatenate([col_flags * row_flag for row_flag in row_flags], axis=1)
    sides = sigmoid(project(0)) * project(1) * flags
    for device in range(shards):
        block = sides[device * 8 : (device + 1) * 8]
        for r in range(0, row_count, 2):
            rows = jnp.concatenate(
                [block[:, (r + i) * col_count : (r + i + 1) * col_count] for i in range(2)], axis=0
            )
            out_ref[device ^ hub, r * 8 : (r + 2) * 8, :] = rows.astype(jnp.bfloat16)
    for fetch in fetches[needed:]:
        fetch.wait()


def receive_blocks(blocks_ref, held_ref):
    shards, rows, _ = blocks_ref.shape
    for i in range(shards):
        held_ref[(i ^ hub) * rows : ((i ^ hub) + 1) * rows, :] = blocks_ref[i].astype(jnp.float32)


def exchange(blocks):
    groups = [[i ^ hub for i in range(blocks.shape[0])]]
    return lax.all_to_all(
        blocks, axes, split_axis=0, concat_axis=0, axis_index_groups=groups, tiled=True
    )


def contract_kernel(
    blocks_ref, normed_ref, w_gate_ref, gain_ref, bias_ref,
    out_ref, gate_ref, scales_ref, held_ref,
):
    total = held_ref.shape[0] // 8
    receive_blocks(blocks_ref, held_ref)
    products = []
    for c in range(4):
        left = held_ref[pl.ds(c, total, stride=8), :].astype(jnp.bfloat16)
        right = held_ref[pl.ds(4 + c, total, stride=8), :].astype(jnp.bfloat16)
        products.append(
            lax.dot_general(
                left, right, (((1,), (1,)), ((), ())), preferred_element_type=jnp.float32
            )
        )
    for row in range(0, total, 8):
        pieces = [product[row : row + 8] for product in products]
        low, high = swap_halves(pieces[0], pieces[1]), swap_halves(pieces[2], pieces[3])
        for half in range(2):
            rows = jnp.concatenate([low[half], high[half]], axis=0)
            out_ref[(row // 4 + half) ^ hub] = rows.astype(jnp.bfloat16)
    gate = jnp.dot(normed_ref[...], w_gate_ref[...], preferred_element_type=jnp.float32)
    gate_ref[...] = sigmoid(gate).astype(jnp.bfloat16)
    for i, vector_ref in enumerate((gain_ref, bias_ref)):
        scales_ref[i] = jnp.transpose(jnp.broadcast_to(vector_ref[...], scales_ref.shape[1:]))


def finish_kernel(blocks_ref, gate_ref, scales_ref, w_ref, out_ref, held_ref):
    row_count, col_count, chan_count = out_ref.shape
    receive_blocks(blocks_ref, held_ref)
    for r in range(row_count):
        triangle = held_ref[pl.ds(r, chan_count, stride=row_count), :]
        normed = layer_norm(triangle, scales_ref[0], scales_ref[1], 0).astype(jnp.bfloat16)
        result = lax.dot_general(
            normed, w_ref[...], (((0,), (0,)), ((), ())), preferred_element_type=jnp.float32
        )
        gate = gate_ref[r * col_count : (r + 1) * col_count, :].astype(jnp.float32)
        out_ref[r] = (gate * result).astype(jnp.bfloat16)


def local_blocks(pair, valid, norm_gain, norm_bias, w_proj, out_gain, out_bias, w_out):
    row_count, col_count, chan_count = pair.shape
    shards = lax.axis_size(axes)
    tokens = row_count * col_count
    vmem = pl.BlockSpec(memory_space=pltpu.VMEM)
    hbm = pl.BlockSpec(memory_space=pltpu.HBM)

    def line(vector):
        return vector.reshape(1, -1)

    def shaped(*dims):
        return jax.ShapeDtypeStruct(dims, jnp.bfloat16)

    def in_hbm(array):
        return pltpu.with_memory_space_constraint(array, pltpu.HBM)

    limit = pltpu.CompilerParams(vmem_limit_bytes=kernel_vmem)
    vector = jax.ShapeDtypeStruct((1, chan_count), jnp.float32)
    square = shaped(chan_count, chan_count)
    sides, normed, w_gate, out_gain, out_bias, w_out = pl.pallas_call(
        project_kernel,
        out_shape=(
            shaped(shards, 8 * row_count, col_count), shaped(tokens, chan_count),
            square, vector, vector, square,
        ),
        in_specs=[hbm] * 8,
        out_specs=(vmem,) * 6,
        scratch_shapes=[
            pltpu.VMEM(pair.shape, jnp.bfloat16),
            pltpu.VMEM((1, col_count), jnp.int32),
            pltpu.VMEM((1, chan_count), jnp.float32),
            pltpu.VMEM((1, chan_count), jnp.float32),
            pltpu.VMEM((chan_count, 4 * chan_count), jnp.bfloat16),
            pltpu.SemaphoreType.DMA((row_count + 11,)),
        ],
        compiler_params=limit,
        name="project",
    )(*map(in_hbm, (
        pair, line(valid), line(norm_gain), line(norm_bias), w_proj,
        line(out_gain), line(out_bias), w_out,
    )))
    sides = exchange(sides)
    triangle, gate_values, scales = pl.pallas_call(
        contract_kernel,
        out_shape=(
            shaped(shards, 4 * row_count, col_count),
            shaped(tokens, chan_count),
            jax.ShapeDtypeStruct((2, chan_count, col_count), jnp.float32),
        ),
        in_specs=[vmem] * 5,
        out_specs=(vmem,) * 3,
        scratch_shapes=[pltpu.VMEM((8 * col_count, col_count), jnp.float32)],
        compiler_params=limit,
        name="contract",
    )(sides, normed, w_gate, out_gain, out_bias)
    triangle = exchange(triangle)
    return pl.pallas_call(
        finish_kernel,
        out_shape=shaped(row_count, col_count, chan_count),
        in_specs=[vmem] * 4,
        out_specs=vmem,
        scratch_shapes=[pltpu.VMEM((tokens, chan_count), jnp.float32)],
        compiler_params=limit,
        name="finish",
    )(triangle, gate_values, scales, w_out)


def local_arrays(pair, valid, norm_gain, norm_bias, w_proj, out_gain, out_bias, w_out):
    row_count, col_count, chan_count = pair.shape
    row_start = lax.axis_index(("wide", "narrow")) * row_count
    col_start = lax.axis_index("sub") * col_count
    row_flags = lax.dynamic_slice_in_dim(valid, row_start, row_count, 0).astype(jnp.float32)
    col_flags = lax.dynamic_slice_in_dim(valid, col_start, col_count, 0).astype(jnp.float32)
    pair_flags = row_flags[:, None] * col_flags[None, :]
    normed = layer_norm(pair.astype(jnp.float32), norm_gain, norm_bias, 2).astype(jnp.bfloat16)
    projected = jnp.einsum(
        "rkc,cd->drk", normed, w_proj[:, : 4 * chan_count], preferred_element_type=jnp.float32
    )
    left_side = (
        jax.nn.sigmoid(projected[:chan_count]) * projected[chan_count : 2 * chan_count] * pair_flags
    ).astype(jnp.bfloat16)
    right_side = (
        jax.nn.sigmoid(projected[2 * chan_count : 3 * chan_count])
        * projected[3 * chan_count :]
        * pair_flags
    ).astype(jnp.bfloat16)
    gate_values = jax.nn.sigmoid(
        jnp.einsum(
            "rkc,cd->rkd", normed, w_proj[:, 4 * chan_count :], preferred_element_type=jnp.float32
        )
    ).astype(jnp.bfloat16)
    both_sides = jnp.stack([left_side, right_side], axis=1)
    both_group = lax.all_to_all(
        both_sides, ("wide", "narrow"), split_axis=0, concat_axis=2, tiled=True
    )
    left_group, right_group = both_group[:, 0], both_group[:, 1]
    partial_sums = jnp.einsum(
        "cik,cjk->cij", left_group, right_group, preferred_element_type=jnp.float32
    )
    summed = lax.psum_scatter(partial_sums, "sub", scatter_dimension=2, tiled=True).astype(
        jnp.bfloat16
    )
    returned = lax.all_to_all(summed, ("wide", "narrow"), split_axis=1, concat_axis=0, tiled=True)
    normed_out = layer_norm(
        returned.astype(jnp.float32), out_gain[:, None, None], out_bias[:, None, None], 0
    ).astype(jnp.bfloat16)
    result_out = jnp.einsum("crj,cd->rjd", normed_out, w_out, preferred_element_type=jnp.float32)
    return (gate_values.astype(jnp.float32) * result_out).astype(jnp.bfloat16)


def local(pair, *rest):
    row_count, col_count, chan_count = pair.shape
    shards = lax.axis_size(axes)
    fits = (
        lax.axis_size("sub") == 1
        and (row_count, col_count, chan_count) == (4, 128, 128)
        and shards * row_count == col_count
        and shards * 4 == chan_count
        and shards == hub + 1
    )
    return (local_blocks if fits else local_arrays)(pair, *rest)


def solution(mesh):
    in_specs = (
        P(("parts", "wide", "narrow"), "sub", None),
        P("parts"),
        P(),
        P(),
        P(),
        P(),
        P(),
        P(),
    )
    out_specs = P(("parts", "wide", "narrow"), "sub", None)
    return jax.shard_map(local, mesh=mesh, in_specs=in_specs, out_specs=out_specs, check_vma=False)
```

```python
import functools

import jax
import jax.numpy as jnp
from jax import lax
from jax.experimental import pallas as pl
from jax.experimental.pallas import tpu as pltpu
from jax.sharding import PartitionSpec as P

epsilon = 1e-05
axes = ("wide", "narrow")
kernel_vmem = 8 * 2**20
hub = 6


def layer_norm(values, gain_vec, bias_vec, axis_dim):
    average = jnp.mean(values, axis=axis_dim, keepdims=True)
    centered = values - average
    variance = jnp.mean(centered * centered, axis=axis_dim, keepdims=True)
    return centered * lax.rsqrt(variance + epsilon) * gain_vec + bias_vec


def sigmoid(values):
    return 0.5 + 0.5 * jnp.tanh(0.5 * values)


def swap_halves(low, high):
    first = lax.broadcasted_iota(jnp.int32, low.shape, 0) < 4
    return (
        jnp.where(first, low, pltpu.roll(high, 4, 0)),
        jnp.where(first, pltpu.roll(low, 4, 0), high),
    )


def project_kernel(
    pair_hbm, valid_hbm, gain_hbm, bias_hbm, w_hbm, out_gain_hbm, out_bias_hbm, w_out_hbm,
    out_ref, normed_ref, w_gate_ref, out_gain_ref, out_bias_ref, w_out_ref,
    pair_ref, valid_ref, gain_ref, bias_ref, w_ref, sems,
):
    row_count, col_count, chan_count = pair_ref.shape
    quarter = chan_count // 4
    pairs = [(pair_hbm.at[r], pair_ref.at[r]) for r in range(row_count)]
    for i in range(0, chan_count, quarter):
        rows = pl.ds(i, quarter)
        pairs.append((w_hbm.at[rows, : 4 * chan_count], w_ref.at[rows]))
    pairs += [(gain_hbm, gain_ref), (bias_hbm, bias_ref), (valid_hbm, valid_ref)]
    needed = len(pairs)
    pairs += [
        (w_hbm.at[:, 4 * chan_count :], w_gate_ref), (out_gain_hbm, out_gain_ref),
        (out_bias_hbm, out_bias_ref), (w_out_hbm, w_out_ref),
    ]
    fetches = [
        pltpu.make_async_copy(source, held, sems.at[i]) for i, (source, held) in enumerate(pairs)
    ]
    for fetch in fetches:
        fetch.start()
    row_start = lax.axis_index(axes) * row_count
    for fetch in fetches[:needed]:
        fetch.wait()
    tokens = pair_ref[...].reshape(row_count * col_count, chan_count).astype(jnp.float32)
    normed = layer_norm(tokens, gain_ref[...], bias_ref[...], 1).astype(jnp.bfloat16)
    normed_ref[...] = normed
    projected = lax.dot_general(
        w_ref[...], normed, (((0,), (1,)), ((), ())),
        preferred_element_type=jnp.float32,
    )
    col_flags = valid_ref[...].astype(jnp.float32)
    places = lax.broadcasted_iota(jnp.int32, col_flags.shape, 1)
    row_flags = [
        jnp.sum(jnp.where(places == row_start + r, col_flags, 0.0), axis=1, keepdims=True)
        for r in range(row_count)
    ]
    flags = jnp.concatenate([col_flags * row_flag for row_flag in row_flags], axis=1)
    for chan in range(0, chan_count, 8):
        a_gate, a, b_gate, b = (
            projected[i * chan_count + chan : i * chan_count + chan + 8] for i in range(4)
        )
        left = sigmoid(a_gate) * a * flags
        right = sigmoid(b_gate) * b * flags
        for half, block in enumerate(swap_halves(left, right)):
            for r in range(0, row_count, 2):
                rows = jnp.concatenate(
                    [block[:, (r + i) * col_count : (r + i + 1) * col_count] for i in range(2)], axis=0
                )
                out_ref[(chan // 4 + half) ^ hub, r * 8 : (r + 2) * 8, :] = rows.astype(jnp.bfloat16)
    for fetch in fetches[needed:]:
        fetch.wait()


def receive_blocks(blocks_ref, held_ref):
    shards, rows, _ = blocks_ref.shape
    for i in range(shards):
        held_ref[(i ^ hub) * rows : ((i ^ hub) + 1) * rows, :] = blocks_ref[i].astype(jnp.float32)


def exchange(blocks):
    groups = [[i ^ hub for i in range(blocks.shape[0])]]
    return lax.all_to_all(
        blocks, axes, split_axis=0, concat_axis=0, axis_index_groups=groups, tiled=True
    )


def contract_kernel(
    blocks_ref, normed_ref, w_gate_ref, gain_ref, bias_ref,
    out_ref, gate_ref, scales_ref, held_ref,
):
    total = held_ref.shape[0] // 8
    receive_blocks(blocks_ref, held_ref)
    products = []
    for c in range(4):
        left = held_ref[pl.ds(c, total, stride=8), :].astype(jnp.bfloat16)
        right = held_ref[pl.ds(4 + c, total, stride=8), :].astype(jnp.bfloat16)
        products.append(
            lax.dot_general(
                left, right, (((1,), (1,)), ((), ())), preferred_element_type=jnp.float32
            )
        )
    for row in range(0, total, 8):
        pieces = [product[row : row + 8] for product in products]
        low, high = swap_halves(pieces[0], pieces[1]), swap_halves(pieces[2], pieces[3])
        for half in range(2):
            rows = jnp.concatenate([low[half], high[half]], axis=0)
            out_ref[(row // 4 + half) ^ hub] = rows.astype(jnp.bfloat16)
    gate = jnp.dot(normed_ref[...], w_gate_ref[...], preferred_element_type=jnp.float32)
    gate_ref[...] = sigmoid(gate).astype(jnp.bfloat16)
    for i, vector_ref in enumerate((gain_ref, bias_ref)):
        scales_ref[i] = jnp.transpose(jnp.broadcast_to(vector_ref[...], scales_ref.shape[1:]))


def finish_kernel(blocks_ref, gate_ref, scales_ref, w_ref, out_ref, held_ref):
    row_count, col_count, chan_count = out_ref.shape
    receive_blocks(blocks_ref, held_ref)
    for r in range(row_count):
        triangle = held_ref[pl.ds(r, chan_count, stride=row_count), :]
        normed = layer_norm(triangle, scales_ref[0], scales_ref[1], 0).astype(jnp.bfloat16)
        result = lax.dot_general(
            normed, w_ref[...], (((0,), (0,)), ((), ())), preferred_element_type=jnp.float32
        )
        gate = gate_ref[r * col_count : (r + 1) * col_count, :].astype(jnp.float32)
        out_ref[r] = (gate * result).astype(jnp.bfloat16)


def local_blocks(pair, valid, norm_gain, norm_bias, w_proj, out_gain, out_bias, w_out):
    row_count, col_count, chan_count = pair.shape
    shards = lax.axis_size(axes)
    tokens = row_count * col_count
    vmem = pl.BlockSpec(memory_space=pltpu.VMEM)
    hbm = pl.BlockSpec(memory_space=pltpu.HBM)

    def line(vector):
        return vector.reshape(1, -1)

    def shaped(*dims):
        return jax.ShapeDtypeStruct(dims, jnp.bfloat16)

    def in_hbm(array):
        return pltpu.with_memory_space_constraint(array, pltpu.HBM)

    limit = pltpu.CompilerParams(vmem_limit_bytes=kernel_vmem)
    vector = jax.ShapeDtypeStruct((1, chan_count), jnp.float32)
    square = shaped(chan_count, chan_count)
    sides, normed, w_gate, out_gain, out_bias, w_out = pl.pallas_call(
        project_kernel,
        out_shape=(
            shaped(shards, 8 * row_count, col_count), shaped(tokens, chan_count),
            square, vector, vector, square,
        ),
        in_specs=[hbm] * 8,
        out_specs=(vmem,) * 6,
        scratch_shapes=[
            pltpu.VMEM(pair.shape, jnp.bfloat16),
            pltpu.VMEM((1, col_count), jnp.int32),
            pltpu.VMEM((1, chan_count), jnp.float32),
            pltpu.VMEM((1, chan_count), jnp.float32),
            pltpu.VMEM((chan_count, 4 * chan_count), jnp.bfloat16),
            pltpu.SemaphoreType.DMA((row_count + 11,)),
        ],
        compiler_params=limit,
        name="project",
    )(*map(in_hbm, (
        pair, line(valid), line(norm_gain), line(norm_bias), w_proj,
        line(out_gain), line(out_bias), w_out,
    )))
    sides = exchange(sides)
    triangle, gate_values, scales = pl.pallas_call(
        contract_kernel,
        out_shape=(
            shaped(shards, 4 * row_count, col_count),
            shaped(tokens, chan_count),
            jax.ShapeDtypeStruct((2, chan_count, col_count), jnp.float32),
        ),
        in_specs=[vmem] * 5,
        out_specs=(vmem,) * 3,
        scratch_shapes=[pltpu.VMEM((8 * col_count, col_count), jnp.float32)],
        compiler_params=limit,
        name="contract",
    )(sides, normed, w_gate, out_gain, out_bias)
    triangle = exchange(triangle)
    return pl.pallas_call(
        finish_kernel,
        out_shape=shaped(row_count, col_count, chan_count),
        in_specs=[vmem] * 4,
        out_specs=vmem,
        scratch_shapes=[pltpu.VMEM((tokens, chan_count), jnp.float32)],
        compiler_params=limit,
        name="finish",
    )(triangle, gate_values, scales, w_out)


def local_arrays(pair, valid, norm_gain, norm_bias, w_proj, out_gain, out_bias, w_out):
    row_count, col_count, chan_count = pair.shape
    row_start = lax.axis_index(("wide", "narrow")) * row_count
    col_start = lax.axis_index("sub") * col_count
    row_flags = lax.dynamic_slice_in_dim(valid, row_start, row_count, 0).astype(jnp.float32)
    col_flags = lax.dynamic_slice_in_dim(valid, col_start, col_count, 0).astype(jnp.float32)
    pair_flags = row_flags[:, None] * col_flags[None, :]
    normed = layer_norm(pair.astype(jnp.float32), norm_gain, norm_bias, 2).astype(jnp.bfloat16)
    projected = jnp.einsum(
        "rkc,cd->drk", normed, w_proj[:, : 4 * chan_count], preferred_element_type=jnp.float32
    )
    left_side = (
        jax.nn.sigmoid(projected[:chan_count]) * projected[chan_count : 2 * chan_count] * pair_flags
    ).astype(jnp.bfloat16)
    right_side = (
        jax.nn.sigmoid(projected[2 * chan_count : 3 * chan_count])
        * projected[3 * chan_count :]
        * pair_flags
    ).astype(jnp.bfloat16)
    gate_values = jax.nn.sigmoid(
        jnp.einsum(
            "rkc,cd->rkd", normed, w_proj[:, 4 * chan_count :], preferred_element_type=jnp.float32
        )
    ).astype(jnp.bfloat16)
    both_sides = jnp.stack([left_side, right_side], axis=1)
    both_group = lax.all_to_all(
        both_sides, ("wide", "narrow"), split_axis=0, concat_axis=2, tiled=True
    )
    left_group, right_group = both_group[:, 0], both_group[:, 1]
    partial_sums = jnp.einsum(
        "cik,cjk->cij", left_group, right_group, preferred_element_type=jnp.float32
    )
    summed = lax.psum_scatter(partial_sums, "sub", scatter_dimension=2, tiled=True).astype(
        jnp.bfloat16
    )
    returned = lax.all_to_all(summed, ("wide", "narrow"), split_axis=1, concat_axis=0, tiled=True)
    normed_out = layer_norm(
        returned.astype(jnp.float32), out_gain[:, None, None], out_bias[:, None, None], 0
    ).astype(jnp.bfloat16)
    result_out = jnp.einsum("crj,cd->rjd", normed_out, w_out, preferred_element_type=jnp.float32)
    return (gate_values.astype(jnp.float32) * result_out).astype(jnp.bfloat16)


def local(pair, *rest):
    row_count, col_count, chan_count = pair.shape
    shards = lax.axis_size(axes)
    fits = (
        lax.axis_size("sub") == 1
        and (row_count, col_count, chan_count) == (4, 128, 128)
        and shards * row_count == col_count
        and shards * 4 == chan_count
        and shards == 32
    )
    return (local_blocks if fits else local_arrays)(pair, *rest)


def solution(mesh):
    in_specs = (
        P(("parts", "wide", "narrow"), "sub", None),
        P("parts"),
        P(),
        P(),
        P(),
        P(),
        P(),
        P(),
    )
    out_specs = P(("parts", "wide", "narrow"), "sub", None)
    return jax.shard_map(local, mesh=mesh, in_specs=in_specs, out_specs=out_specs, check_vma=False)
```

```python
import functools

import jax
import jax.numpy as jnp
from jax import lax
from jax.experimental import pallas as pl
from jax.experimental.pallas import tpu as pltpu
from jax.sharding import PartitionSpec as P

epsilon = 1e-05
axes = ("wide", "narrow")
kernel_vmem = 8 * 2**20
hub = 31


def layer_norm(values, gain_vec, bias_vec, axis_dim):
    average = jnp.mean(values, axis=axis_dim, keepdims=True)
    centered = values - average
    variance = jnp.mean(centered * centered, axis=axis_dim, keepdims=True)
    return centered * lax.rsqrt(variance + epsilon) * gain_vec + bias_vec


def sigmoid(values):
    return 0.5 + 0.5 * jnp.tanh(0.5 * values)


def swap_halves(low, high):
    first = lax.broadcasted_iota(jnp.int32, low.shape, 0) < 4
    return (
        jnp.where(first, low, pltpu.roll(high, 4, 0)),
        jnp.where(first, pltpu.roll(low, 4, 0), high),
    )


def row_means(values):
    ones = jnp.ones((values.shape[1], values.shape[1]), jnp.bfloat16)
    return jnp.dot(values, ones, preferred_element_type=jnp.float32) * (1 / values.shape[1])


def project_kernel(
    pair_hbm, valid_hbm, gain_hbm, bias_hbm, w_hbm, out_gain_hbm, out_bias_hbm, w_out_hbm,
    out_ref, normed_ref, w_gate_ref, out_gain_ref, out_bias_ref, w_out_ref,
    pair_ref, valid_ref, gain_ref, bias_ref, w_ref, sems,
):
    row_count, col_count, chan_count = pair_ref.shape
    quarter = chan_count // 4
    pairs = [(pair_hbm.at[r], pair_ref.at[r]) for r in range(row_count)]
    for i in range(0, chan_count, quarter):
        rows = pl.ds(i, quarter)
        pairs.append((w_hbm.at[rows, : 4 * chan_count], w_ref.at[rows]))
    pairs += [(gain_hbm, gain_ref), (bias_hbm, bias_ref), (valid_hbm, valid_ref)]
    needed = len(pairs)
    pairs += [
        (w_hbm.at[:, 4 * chan_count :], w_gate_ref), (out_gain_hbm, out_gain_ref),
        (out_bias_hbm, out_bias_ref), (w_out_hbm, w_out_ref),
    ]
    fetches = [
        pltpu.make_async_copy(source, held, sems.at[i]) for i, (source, held) in enumerate(pairs)
    ]
    for fetch in fetches:
        fetch.start()
    row_start = lax.axis_index(axes) * row_count
    for fetch in fetches[:needed]:
        fetch.wait()
    tokens = pair_ref[...].reshape(row_count * col_count, chan_count)
    centered = tokens.astype(jnp.float32) - row_means(tokens)
    squares = centered * centered
    high = squares.astype(jnp.bfloat16)
    low = (squares - high.astype(jnp.float32)).astype(jnp.bfloat16)
    scale = lax.rsqrt(row_means(high) + row_means(low) + epsilon)
    normed = (centered * scale * gain_ref[...] + bias_ref[...]).astype(jnp.bfloat16)
    normed_ref[...] = normed
    projected = lax.dot_general(
        w_ref[...], normed, (((0,), (1,)), ((), ())),
        preferred_element_type=jnp.float32,
    )
    col_flags = valid_ref[...].astype(jnp.float32)
    places = lax.broadcasted_iota(jnp.int32, col_flags.shape, 1)
    row_flags = [
        jnp.sum(jnp.where(places == row_start + r, col_flags, 0.0), axis=1, keepdims=True)
        for r in range(row_count)
    ]
    flags = jnp.concatenate([col_flags * row_flag for row_flag in row_flags], axis=1)
    for chan in range(0, chan_count, 8):
        a_gate, a, b_gate, b = (
            projected[i * chan_count + chan : i * chan_count + chan + 8] for i in range(4)
        )
        left = sigmoid(a_gate) * a * flags
        right = sigmoid(b_gate) * b * flags
        for half, block in enumerate(swap_halves(left, right)):
            for r in range(0, row_count, 2):
                rows = jnp.concatenate(
                    [block[:, (r + i) * col_count : (r + i + 1) * col_count] for i in range(2)], axis=0
                )
                out_ref[(chan // 4 + half) ^ hub, r * 8 : (r + 2) * 8, :] = rows.astype(jnp.bfloat16)
    for fetch in fetches[needed:]:
        fetch.wait()


def receive_blocks(blocks_ref, held_ref):
    shards, rows, _ = blocks_ref.shape
    for i in range(shards):
        held_ref[(i ^ hub) * rows : ((i ^ hub) + 1) * rows, :] = blocks_ref[i].astype(jnp.float32)


def exchange(blocks):
    groups = [[i ^ hub for i in range(blocks.shape[0])]]
    return lax.all_to_all(
        blocks, axes, split_axis=0, concat_axis=0, axis_index_groups=groups, tiled=True
    )


def contract_kernel(
    blocks_ref, normed_ref, w_gate_ref, gain_ref, bias_ref,
    out_ref, gate_ref, scales_ref, held_ref,
):
    total = held_ref.shape[0] // 8
    receive_blocks(blocks_ref, held_ref)
    products = []
    for c in range(4):
        left = held_ref[pl.ds(c, total, stride=8), :].astype(jnp.bfloat16)
        right = held_ref[pl.ds(4 + c, total, stride=8), :].astype(jnp.bfloat16)
        products.append(
            lax.dot_general(
                left, right, (((1,), (1,)), ((), ())), preferred_element_type=jnp.float32
            )
        )
    for row in range(0, total, 8):
        pieces = [product[row : row + 8] for product in products]
        low, high = swap_halves(pieces[0], pieces[1]), swap_halves(pieces[2], pieces[3])
        for half in range(2):
            rows = jnp.concatenate([low[half], high[half]], axis=0)
            out_ref[(row // 4 + half) ^ hub] = rows.astype(jnp.bfloat16)
    gate = jnp.dot(normed_ref[...], w_gate_ref[...], preferred_element_type=jnp.float32)
    gate_ref[...] = sigmoid(gate).astype(jnp.bfloat16)
    for i, vector_ref in enumerate((gain_ref, bias_ref)):
        scales_ref[i] = jnp.transpose(jnp.broadcast_to(vector_ref[...], scales_ref.shape[1:]))


def finish_kernel(blocks_ref, gate_ref, scales_ref, w_ref, out_ref, held_ref):
    row_count, col_count, chan_count = out_ref.shape
    receive_blocks(blocks_ref, held_ref)
    for r in range(row_count):
        triangle = held_ref[pl.ds(r, chan_count, stride=row_count), :]
        normed = layer_norm(triangle, scales_ref[0], scales_ref[1], 0).astype(jnp.bfloat16)
        result = lax.dot_general(
            normed, w_ref[...], (((0,), (0,)), ((), ())), preferred_element_type=jnp.float32
        )
        gate = gate_ref[r * col_count : (r + 1) * col_count, :].astype(jnp.float32)
        out_ref[r] = (gate * result).astype(jnp.bfloat16)


def local_blocks(pair, valid, norm_gain, norm_bias, w_proj, out_gain, out_bias, w_out):
    row_count, col_count, chan_count = pair.shape
    shards = lax.axis_size(axes)
    tokens = row_count * col_count
    vmem = pl.BlockSpec(memory_space=pltpu.VMEM)
    hbm = pl.BlockSpec(memory_space=pltpu.HBM)

    def line(vector):
        return vector.reshape(1, -1)

    def shaped(*dims):
        return jax.ShapeDtypeStruct(dims, jnp.bfloat16)

    def in_hbm(array):
        return pltpu.with_memory_space_constraint(array, pltpu.HBM)

    limit = pltpu.CompilerParams(vmem_limit_bytes=kernel_vmem)
    vector = jax.ShapeDtypeStruct((1, chan_count), jnp.float32)
    square = shaped(chan_count, chan_count)
    sides, normed, w_gate, out_gain, out_bias, w_out = pl.pallas_call(
        project_kernel,
        out_shape=(
            shaped(shards, 8 * row_count, col_count), shaped(tokens, chan_count),
            square, vector, vector, square,
        ),
        in_specs=[hbm] * 8,
        out_specs=(vmem,) * 6,
        scratch_shapes=[
            pltpu.VMEM(pair.shape, jnp.bfloat16),
            pltpu.VMEM((1, col_count), jnp.int32),
            pltpu.VMEM((1, chan_count), jnp.float32),
            pltpu.VMEM((1, chan_count), jnp.float32),
            pltpu.VMEM((chan_count, 4 * chan_count), jnp.bfloat16),
            pltpu.SemaphoreType.DMA((row_count + 11,)),
        ],
        compiler_params=limit,
        name="project",
    )(*map(in_hbm, (
        pair, line(valid), line(norm_gain), line(norm_bias), w_proj,
        line(out_gain), line(out_bias), w_out,
    )))
    sides = exchange(sides)
    triangle, gate_values, scales = pl.pallas_call(
        contract_kernel,
        out_shape=(
            shaped(shards, 4 * row_count, col_count),
            shaped(tokens, chan_count),
            jax.ShapeDtypeStruct((2, chan_count, col_count), jnp.float32),
        ),
        in_specs=[vmem] * 5,
        out_specs=(vmem,) * 3,
        scratch_shapes=[pltpu.VMEM((8 * col_count, col_count), jnp.float32)],
        compiler_params=limit,
        name="contract",
    )(sides, normed, w_gate, out_gain, out_bias)
    triangle = exchange(triangle)
    return pl.pallas_call(
        finish_kernel,
        out_shape=shaped(row_count, col_count, chan_count),
        in_specs=[vmem] * 4,
        out_specs=vmem,
        scratch_shapes=[pltpu.VMEM((tokens, chan_count), jnp.float32)],
        compiler_params=limit,
        name="finish",
    )(triangle, gate_values, scales, w_out)


def local_arrays(pair, valid, norm_gain, norm_bias, w_proj, out_gain, out_bias, w_out):
    row_count, col_count, chan_count = pair.shape
    row_start = lax.axis_index(("wide", "narrow")) * row_count
    col_start = lax.axis_index("sub") * col_count
    row_flags = lax.dynamic_slice_in_dim(valid, row_start, row_count, 0).astype(jnp.float32)
    col_flags = lax.dynamic_slice_in_dim(valid, col_start, col_count, 0).astype(jnp.float32)
    pair_flags = row_flags[:, None] * col_flags[None, :]
    normed = layer_norm(pair.astype(jnp.float32), norm_gain, norm_bias, 2).astype(jnp.bfloat16)
    projected = jnp.einsum(
        "rkc,cd->drk", normed, w_proj[:, : 4 * chan_count], preferred_element_type=jnp.float32
    )
    left_side = (
        jax.nn.sigmoid(projected[:chan_count]) * projected[chan_count : 2 * chan_count] * pair_flags
    ).astype(jnp.bfloat16)
    right_side = (
        jax.nn.sigmoid(projected[2 * chan_count : 3 * chan_count])
        * projected[3 * chan_count :]
        * pair_flags
    ).astype(jnp.bfloat16)
    gate_values = jax.nn.sigmoid(
        jnp.einsum(
            "rkc,cd->rkd", normed, w_proj[:, 4 * chan_count :], preferred_element_type=jnp.float32
        )
    ).astype(jnp.bfloat16)
    both_sides = jnp.stack([left_side, right_side], axis=1)
    both_group = lax.all_to_all(
        both_sides, ("wide", "narrow"), split_axis=0, concat_axis=2, tiled=True
    )
    left_group, right_group = both_group[:, 0], both_group[:, 1]
    partial_sums = jnp.einsum(
        "cik,cjk->cij", left_group, right_group, preferred_element_type=jnp.float32
    )
    summed = lax.psum_scatter(partial_sums, "sub", scatter_dimension=2, tiled=True).astype(
        jnp.bfloat16
    )
    returned = lax.all_to_all(summed, ("wide", "narrow"), split_axis=1, concat_axis=0, tiled=True)
    normed_out = layer_norm(
        returned.astype(jnp.float32), out_gain[:, None, None], out_bias[:, None, None], 0
    ).astype(jnp.bfloat16)
    result_out = jnp.einsum("crj,cd->rjd", normed_out, w_out, preferred_element_type=jnp.float32)
    return (gate_values.astype(jnp.float32) * result_out).astype(jnp.bfloat16)


def local(pair, *rest):
    row_count, col_count, chan_count = pair.shape
    shards = lax.axis_size(axes)
    fits = (
        lax.axis_size("sub") == 1
        and (row_count, col_count, chan_count) == (4, 128, 128)
        and shards * row_count == col_count
        and shards * 4 == chan_count
        and shards == hub + 1
    )
    return (local_blocks if fits else local_arrays)(pair, *rest)


def solution(mesh):
    in_specs = (
        P(("parts", "wide", "narrow"), "sub", None),
        P("parts"),
        P(),
        P(),
        P(),
        P(),
        P(),
        P(),
    )
    out_specs = P(("parts", "wide", "narrow"), "sub", None)
    return jax.shard_map(local, mesh=mesh, in_specs=in_specs, out_specs=out_specs, check_vma=False)
```

```python
import functools

import jax
import jax.numpy as jnp
from jax import lax
from jax.experimental import pallas as pl
from jax.experimental.pallas import tpu as pltpu
from jax.sharding import PartitionSpec as P

epsilon = 1e-05
axes = ("wide", "narrow")
kernel_vmem = 8 * 2**20
planes = 4


def layer_norm(values, gain_vec, bias_vec, axis_dim):
    average = jnp.mean(values, axis=axis_dim, keepdims=True)
    centered = values - average
    variance = jnp.mean(centered * centered, axis=axis_dim, keepdims=True)
    return centered * lax.rsqrt(variance + epsilon) * gain_vec + bias_vec


def sigmoid(values):
    return 0.5 + 0.5 * jnp.tanh(0.5 * values)


def swap_halves(low, high):
    first = lax.broadcasted_iota(jnp.int32, low.shape, 0) < 4
    return (
        jnp.where(first, low, pltpu.roll(high, 4, 0)),
        jnp.where(first, pltpu.roll(low, 4, 0), high),
    )


def project_kernel(
    pair_hbm, valid_hbm, gain_hbm, bias_hbm, w_hbm, out_gain_hbm, out_bias_hbm, w_out_hbm,
    out_ref, normed_ref, w_gate_ref, out_gain_ref, out_bias_ref, w_out_ref,
    pair_ref, valid_ref, gain_ref, bias_ref, w_ref, sems,
):
    row_count, col_count, chan_count = pair_ref.shape
    quarter = chan_count // 4
    pairs = [(pair_hbm.at[r], pair_ref.at[r]) for r in range(row_count)]
    for i in range(0, chan_count, quarter):
        rows = pl.ds(i, quarter)
        pairs.append((w_hbm.at[rows, : 4 * chan_count], w_ref.at[rows]))
    pairs += [(gain_hbm, gain_ref), (bias_hbm, bias_ref), (valid_hbm, valid_ref)]
    needed = len(pairs)
    pairs += [
        (w_hbm.at[:, 4 * chan_count :], w_gate_ref), (out_gain_hbm, out_gain_ref),
        (out_bias_hbm, out_bias_ref), (w_out_hbm, w_out_ref),
    ]
    fetches = [
        pltpu.make_async_copy(source, held, sems.at[i]) for i, (source, held) in enumerate(pairs)
    ]
    for fetch in fetches:
        fetch.start()
    row_start = lax.axis_index(axes) * row_count
    for fetch in fetches[:needed]:
        fetch.wait()
    tokens = pair_ref[...].reshape(row_count * col_count, chan_count).astype(jnp.float32)
    normed = layer_norm(tokens, gain_ref[...], bias_ref[...], 1).astype(jnp.bfloat16)
    normed_ref[...] = normed
    projected = lax.dot_general(
        w_ref[...], normed, (((0,), (1,)), ((), ())),
        preferred_element_type=jnp.float32,
    )
    col_flags = valid_ref[...].astype(jnp.float32)
    places = lax.broadcasted_iota(jnp.int32, col_flags.shape, 1)
    row_flags = [
        jnp.sum(jnp.where(places == row_start + r, col_flags, 0.0), axis=1, keepdims=True)
        for r in range(row_count)
    ]
    flags = jnp.concatenate([col_flags * row_flag for row_flag in row_flags], axis=1)
    for chan in range(0, chan_count, 8):
        a_gate, a, b_gate, b = (
            projected[i * chan_count + chan : i * chan_count + chan + 8] for i in range(4)
        )
        left = sigmoid(a_gate) * a * flags
        right = sigmoid(b_gate) * b * flags
        for half, block in enumerate(swap_halves(left, right)):
            for r in range(0, row_count, 2):
                rows = jnp.concatenate(
                    [block[:, (r + i) * col_count : (r + i + 1) * col_count] for i in range(2)], axis=0
                )
                out_ref[spot(chan // 4 + half), r * 8 : (r + 2) * 8, :] = rows.astype(jnp.bfloat16)
    for fetch in fetches[needed:]:
        fetch.wait()


def group_order():
    chips = []
    for turn, place in enumerate((0, 1, 3, 2)):
        chips += [plane * 4 + place for plane in range(planes)][:: 1 - 2 * (turn % 2)]
    return [2 * chip + core for chip in chips for core in range(2)]


def spot(device):
    return group_order().index(device)


def receive_blocks(blocks_ref, held_ref):
    rows = blocks_ref.shape[1]
    for i, device in enumerate(group_order()):
        held_ref[device * rows : (device + 1) * rows, :] = blocks_ref[i].astype(jnp.float32)


def exchange(blocks):
    return lax.all_to_all(
        blocks, axes, split_axis=0, concat_axis=0, axis_index_groups=[group_order()], tiled=True
    )


def contract_kernel(
    blocks_ref, normed_ref, w_gate_ref, gain_ref, bias_ref,
    out_ref, gate_ref, scales_ref, held_ref,
):
    total = held_ref.shape[0] // 8
    receive_blocks(blocks_ref, held_ref)
    products = []
    for c in range(4):
        left = held_ref[pl.ds(c, total, stride=8), :].astype(jnp.bfloat16)
        right = held_ref[pl.ds(4 + c, total, stride=8), :].astype(jnp.bfloat16)
        products.append(
            lax.dot_general(
                left, right, (((1,), (1,)), ((), ())), preferred_element_type=jnp.float32
            )
        )
    for row in range(0, total, 8):
        pieces = [product[row : row + 8] for product in products]
        low, high = swap_halves(pieces[0], pieces[1]), swap_halves(pieces[2], pieces[3])
        for half in range(2):
            rows = jnp.concatenate([low[half], high[half]], axis=0)
            out_ref[spot(row // 4 + half)] = rows.astype(jnp.bfloat16)
    gate = jnp.dot(normed_ref[...], w_gate_ref[...], preferred_element_type=jnp.float32)
    gate_ref[...] = sigmoid(gate).astype(jnp.bfloat16)
    for i, vector_ref in enumerate((gain_ref, bias_ref)):
        scales_ref[i] = jnp.transpose(jnp.broadcast_to(vector_ref[...], scales_ref.shape[1:]))


def finish_kernel(blocks_ref, gate_ref, scales_ref, w_ref, out_ref, held_ref):
    row_count, col_count, chan_count = out_ref.shape
    receive_blocks(blocks_ref, held_ref)
    for r in range(row_count):
        triangle = held_ref[pl.ds(r, chan_count, stride=row_count), :]
        normed = layer_norm(triangle, scales_ref[0], scales_ref[1], 0).astype(jnp.bfloat16)
        result = lax.dot_general(
            normed, w_ref[...], (((0,), (0,)), ((), ())), preferred_element_type=jnp.float32
        )
        gate = gate_ref[r * col_count : (r + 1) * col_count, :].astype(jnp.float32)
        out_ref[r] = (gate * result).astype(jnp.bfloat16)


def local_blocks(pair, valid, norm_gain, norm_bias, w_proj, out_gain, out_bias, w_out):
    row_count, col_count, chan_count = pair.shape
    shards = lax.axis_size(axes)
    tokens = row_count * col_count
    vmem = pl.BlockSpec(memory_space=pltpu.VMEM)
    hbm = pl.BlockSpec(memory_space=pltpu.HBM)

    def line(vector):
        return vector.reshape(1, -1)

    def shaped(*dims):
        return jax.ShapeDtypeStruct(dims, jnp.bfloat16)

    def in_hbm(array):
        return pltpu.with_memory_space_constraint(array, pltpu.HBM)

    limit = pltpu.CompilerParams(vmem_limit_bytes=kernel_vmem)
    vector = jax.ShapeDtypeStruct((1, chan_count), jnp.float32)
    square = shaped(chan_count, chan_count)
    sides, normed, w_gate, out_gain, out_bias, w_out = pl.pallas_call(
        project_kernel,
        out_shape=(
            shaped(shards, 8 * row_count, col_count), shaped(tokens, chan_count),
            square, vector, vector, square,
        ),
        in_specs=[hbm] * 8,
        out_specs=(vmem,) * 6,
        scratch_shapes=[
            pltpu.VMEM(pair.shape, jnp.bfloat16),
            pltpu.VMEM((1, col_count), jnp.int32),
            pltpu.VMEM((1, chan_count), jnp.float32),
            pltpu.VMEM((1, chan_count), jnp.float32),
            pltpu.VMEM((chan_count, 4 * chan_count), jnp.bfloat16),
            pltpu.SemaphoreType.DMA((row_count + 11,)),
        ],
        compiler_params=limit,
        name="project",
    )(*map(in_hbm, (
        pair, line(valid), line(norm_gain), line(norm_bias), w_proj,
        line(out_gain), line(out_bias), w_out,
    )))
    sides = exchange(sides)
    triangle, gate_values, scales = pl.pallas_call(
        contract_kernel,
        out_shape=(
            shaped(shards, 4 * row_count, col_count),
            shaped(tokens, chan_count),
            jax.ShapeDtypeStruct((2, chan_count, col_count), jnp.float32),
        ),
        in_specs=[vmem] * 5,
        out_specs=(vmem,) * 3,
        scratch_shapes=[pltpu.VMEM((8 * col_count, col_count), jnp.float32)],
        compiler_params=limit,
        name="contract",
    )(sides, normed, w_gate, out_gain, out_bias)
    triangle = exchange(triangle)
    return pl.pallas_call(
        finish_kernel,
        out_shape=shaped(row_count, col_count, chan_count),
        in_specs=[vmem] * 4,
        out_specs=vmem,
        scratch_shapes=[pltpu.VMEM((tokens, chan_count), jnp.float32)],
        compiler_params=limit,
        name="finish",
    )(triangle, gate_values, scales, w_out)


def local_arrays(pair, valid, norm_gain, norm_bias, w_proj, out_gain, out_bias, w_out):
    row_count, col_count, chan_count = pair.shape
    row_start = lax.axis_index(("wide", "narrow")) * row_count
    col_start = lax.axis_index("sub") * col_count
    row_flags = lax.dynamic_slice_in_dim(valid, row_start, row_count, 0).astype(jnp.float32)
    col_flags = lax.dynamic_slice_in_dim(valid, col_start, col_count, 0).astype(jnp.float32)
    pair_flags = row_flags[:, None] * col_flags[None, :]
    normed = layer_norm(pair.astype(jnp.float32), norm_gain, norm_bias, 2).astype(jnp.bfloat16)
    projected = jnp.einsum(
        "rkc,cd->drk", normed, w_proj[:, : 4 * chan_count], preferred_element_type=jnp.float32
    )
    left_side = (
        jax.nn.sigmoid(projected[:chan_count]) * projected[chan_count : 2 * chan_count] * pair_flags
    ).astype(jnp.bfloat16)
    right_side = (
        jax.nn.sigmoid(projected[2 * chan_count : 3 * chan_count])
        * projected[3 * chan_count :]
        * pair_flags
    ).astype(jnp.bfloat16)
    gate_values = jax.nn.sigmoid(
        jnp.einsum(
            "rkc,cd->rkd", normed, w_proj[:, 4 * chan_count :], preferred_element_type=jnp.float32
        )
    ).astype(jnp.bfloat16)
    both_sides = jnp.stack([left_side, right_side], axis=1)
    both_group = lax.all_to_all(
        both_sides, ("wide", "narrow"), split_axis=0, concat_axis=2, tiled=True
    )
    left_group, right_group = both_group[:, 0], both_group[:, 1]
    partial_sums = jnp.einsum(
        "cik,cjk->cij", left_group, right_group, preferred_element_type=jnp.float32
    )
    summed = lax.psum_scatter(partial_sums, "sub", scatter_dimension=2, tiled=True).astype(
        jnp.bfloat16
    )
    returned = lax.all_to_all(summed, ("wide", "narrow"), split_axis=1, concat_axis=0, tiled=True)
    normed_out = layer_norm(
        returned.astype(jnp.float32), out_gain[:, None, None], out_bias[:, None, None], 0
    ).astype(jnp.bfloat16)
    result_out = jnp.einsum("crj,cd->rjd", normed_out, w_out, preferred_element_type=jnp.float32)
    return (gate_values.astype(jnp.float32) * result_out).astype(jnp.bfloat16)


def local(pair, *rest):
    row_count, col_count, chan_count = pair.shape
    shards = lax.axis_size(axes)
    fits = (
        lax.axis_size("sub") == 1
        and (row_count, col_count, chan_count) == (4, 128, 128)
        and shards * row_count == col_count
        and shards * 4 == chan_count
        and shards == 8 * planes
    )
    return (local_blocks if fits else local_arrays)(pair, *rest)


def solution(mesh):
    in_specs = (
        P(("parts", "wide", "narrow"), "sub", None),
        P("parts"),
        P(),
        P(),
        P(),
        P(),
        P(),
        P(),
    )
    out_specs = P(("parts", "wide", "narrow"), "sub", None)
    return jax.shard_map(local, mesh=mesh, in_specs=in_specs, out_specs=out_specs, check_vma=False)
```

```python
import functools

import jax
import jax.numpy as jnp
from jax import lax
from jax.experimental import pallas as pl
from jax.experimental.pallas import tpu as pltpu
from jax.sharding import PartitionSpec as P

epsilon = 1e-05
axes = ("wide", "narrow")
kernel_vmem = 8 * 2**20
planes = 4


def layer_norm(values, gain_vec, bias_vec, axis_dim):
    average = jnp.mean(values, axis=axis_dim, keepdims=True)
    centered = values - average
    variance = jnp.mean(centered * centered, axis=axis_dim, keepdims=True)
    return centered * lax.rsqrt(variance + epsilon) * gain_vec + bias_vec


def sigmoid(values):
    return 0.5 + 0.5 * jnp.tanh(0.5 * values)


def swap_halves(low, high):
    first = lax.broadcasted_iota(jnp.int32, low.shape, 0) < 4
    return (
        jnp.where(first, low, pltpu.roll(high, 4, 0)),
        jnp.where(first, pltpu.roll(low, 4, 0), high),
    )


def project_kernel(
    pair_hbm, valid_hbm, gain_hbm, bias_hbm, w_hbm, out_gain_hbm, out_bias_hbm, w_out_hbm,
    out_ref, normed_ref, w_gate_ref, out_gain_ref, out_bias_ref, w_out_ref,
    pair_ref, valid_ref, gain_ref, bias_ref, w_ref, sems,
):
    row_count, col_count, chan_count = pair_ref.shape
    quarter = chan_count // 4
    pairs = [(pair_hbm.at[r], pair_ref.at[r]) for r in range(row_count)]
    for i in range(0, chan_count, quarter):
        rows = pl.ds(i, quarter)
        pairs.append((w_hbm.at[rows, : 4 * chan_count], w_ref.at[rows]))
    pairs += [(gain_hbm, gain_ref), (bias_hbm, bias_ref), (valid_hbm, valid_ref)]
    needed = len(pairs)
    pairs += [
        (w_hbm.at[:, 4 * chan_count :], w_gate_ref), (out_gain_hbm, out_gain_ref),
        (out_bias_hbm, out_bias_ref), (w_out_hbm, w_out_ref),
    ]
    fetches = [
        pltpu.make_async_copy(source, held, sems.at[i]) for i, (source, held) in enumerate(pairs)
    ]
    for fetch in fetches:
        fetch.start()
    row_start = lax.axis_index(axes) * row_count
    for fetch in fetches[:needed]:
        fetch.wait()
    tokens = pair_ref[...].reshape(row_count * col_count, chan_count).astype(jnp.float32)
    normed = layer_norm(tokens, gain_ref[...], bias_ref[...], 1).astype(jnp.bfloat16)
    normed_ref[...] = normed
    projected = lax.dot_general(
        w_ref[...], normed, (((0,), (1,)), ((), ())),
        preferred_element_type=jnp.float32,
    )
    col_flags = valid_ref[...].astype(jnp.float32)
    places = lax.broadcasted_iota(jnp.int32, col_flags.shape, 1)
    row_flags = [
        jnp.sum(jnp.where(places == row_start + r, col_flags, 0.0), axis=1, keepdims=True)
        for r in range(row_count)
    ]
    flags = jnp.concatenate([col_flags * row_flag for row_flag in row_flags], axis=1)
    for chan in range(0, chan_count, 8):
        a_gate, a, b_gate, b = (
            projected[i * chan_count + chan : i * chan_count + chan + 8] for i in range(4)
        )
        left = sigmoid(a_gate) * a * flags
        right = sigmoid(b_gate) * b * flags
        for half, block in enumerate(swap_halves(left, right)):
            for r in range(0, row_count, 2):
                rows = jnp.concatenate(
                    [block[:, (r + i) * col_count : (r + i + 1) * col_count] for i in range(2)], axis=0
                )
                out_ref[spot(chan // 4 + half), r * 8 : (r + 2) * 8, :] = rows.astype(jnp.bfloat16)
    for fetch in fetches[needed:]:
        fetch.wait()


def group_order():
    chips = []
    for turn, place in enumerate((0, 1, 3, 2)):
        chips += [plane * 4 + place for plane in range(planes)][:: 1 - 2 * (turn % 2)]
    return [2 * chip + core for chip in chips for core in range(2)][::-1]


def spot(device):
    return group_order().index(device)


def receive_blocks(blocks_ref, held_ref):
    rows = blocks_ref.shape[1]
    for i, device in enumerate(group_order()):
        held_ref[device * rows : (device + 1) * rows, :] = blocks_ref[i].astype(jnp.float32)


def exchange(blocks):
    return lax.all_to_all(
        blocks, axes, split_axis=0, concat_axis=0, axis_index_groups=[group_order()], tiled=True
    )


def contract_kernel(
    blocks_ref, normed_ref, w_gate_ref, gain_ref, bias_ref,
    out_ref, gate_ref, scales_ref, held_ref,
):
    total = held_ref.shape[0] // 8
    receive_blocks(blocks_ref, held_ref)
    products = []
    for c in range(4):
        left = held_ref[pl.ds(c, total, stride=8), :].astype(jnp.bfloat16)
        right = held_ref[pl.ds(4 + c, total, stride=8), :].astype(jnp.bfloat16)
        products.append(
            lax.dot_general(
                left, right, (((1,), (1,)), ((), ())), preferred_element_type=jnp.float32
            )
        )
    for row in range(0, total, 8):
        pieces = [product[row : row + 8] for product in products]
        low, high = swap_halves(pieces[0], pieces[1]), swap_halves(pieces[2], pieces[3])
        for half in range(2):
            rows = jnp.concatenate([low[half], high[half]], axis=0)
            out_ref[spot(row // 4 + half)] = rows.astype(jnp.bfloat16)
    gate = jnp.dot(normed_ref[...], w_gate_ref[...], preferred_element_type=jnp.float32)
    gate_ref[...] = sigmoid(gate).astype(jnp.bfloat16)
    for i, vector_ref in enumerate((gain_ref, bias_ref)):
        scales_ref[i] = jnp.transpose(jnp.broadcast_to(vector_ref[...], scales_ref.shape[1:]))


def finish_kernel(blocks_ref, gate_ref, scales_ref, w_ref, out_ref, held_ref):
    row_count, col_count, chan_count = out_ref.shape
    receive_blocks(blocks_ref, held_ref)
    for r in range(row_count):
        triangle = held_ref[pl.ds(r, chan_count, stride=row_count), :]
        normed = layer_norm(triangle, scales_ref[0], scales_ref[1], 0).astype(jnp.bfloat16)
        result = lax.dot_general(
            normed, w_ref[...], (((0,), (0,)), ((), ())), preferred_element_type=jnp.float32
        )
        gate = gate_ref[r * col_count : (r + 1) * col_count, :].astype(jnp.float32)
        out_ref[r] = (gate * result).astype(jnp.bfloat16)


def local_blocks(pair, valid, norm_gain, norm_bias, w_proj, out_gain, out_bias, w_out):
    row_count, col_count, chan_count = pair.shape
    shards = lax.axis_size(axes)
    tokens = row_count * col_count
    vmem = pl.BlockSpec(memory_space=pltpu.VMEM)
    hbm = pl.BlockSpec(memory_space=pltpu.HBM)

    def line(vector):
        return vector.reshape(1, -1)

    def shaped(*dims):
        return jax.ShapeDtypeStruct(dims, jnp.bfloat16)

    def in_hbm(array):
        return pltpu.with_memory_space_constraint(array, pltpu.HBM)

    limit = pltpu.CompilerParams(vmem_limit_bytes=kernel_vmem)
    vector = jax.ShapeDtypeStruct((1, chan_count), jnp.float32)
    square = shaped(chan_count, chan_count)
    sides, normed, w_gate, out_gain, out_bias, w_out = pl.pallas_call(
        project_kernel,
        out_shape=(
            shaped(shards, 8 * row_count, col_count), shaped(tokens, chan_count),
            square, vector, vector, square,
        ),
        in_specs=[hbm] * 8,
        out_specs=(vmem,) * 6,
        scratch_shapes=[
            pltpu.VMEM(pair.shape, jnp.bfloat16),
            pltpu.VMEM((1, col_count), jnp.int32),
            pltpu.VMEM((1, chan_count), jnp.float32),
            pltpu.VMEM((1, chan_count), jnp.float32),
            pltpu.VMEM((chan_count, 4 * chan_count), jnp.bfloat16),
            pltpu.SemaphoreType.DMA((row_count + 11,)),
        ],
        compiler_params=limit,
        name="project",
    )(*map(in_hbm, (
        pair, line(valid), line(norm_gain), line(norm_bias), w_proj,
        line(out_gain), line(out_bias), w_out,
    )))
    sides = exchange(sides)
    triangle, gate_values, scales = pl.pallas_call(
        contract_kernel,
        out_shape=(
            shaped(shards, 4 * row_count, col_count),
            shaped(tokens, chan_count),
            jax.ShapeDtypeStruct((2, chan_count, col_count), jnp.float32),
        ),
        in_specs=[vmem] * 5,
        out_specs=(vmem,) * 3,
        scratch_shapes=[pltpu.VMEM((8 * col_count, col_count), jnp.float32)],
        compiler_params=limit,
        name="contract",
    )(sides, normed, w_gate, out_gain, out_bias)
    triangle = exchange(triangle)
    return pl.pallas_call(
        finish_kernel,
        out_shape=shaped(row_count, col_count, chan_count),
        in_specs=[vmem] * 4,
        out_specs=vmem,
        scratch_shapes=[pltpu.VMEM((tokens, chan_count), jnp.float32)],
        compiler_params=limit,
        name="finish",
    )(triangle, gate_values, scales, w_out)


def local_arrays(pair, valid, norm_gain, norm_bias, w_proj, out_gain, out_bias, w_out):
    row_count, col_count, chan_count = pair.shape
    row_start = lax.axis_index(("wide", "narrow")) * row_count
    col_start = lax.axis_index("sub") * col_count
    row_flags = lax.dynamic_slice_in_dim(valid, row_start, row_count, 0).astype(jnp.float32)
    col_flags = lax.dynamic_slice_in_dim(valid, col_start, col_count, 0).astype(jnp.float32)
    pair_flags = row_flags[:, None] * col_flags[None, :]
    normed = layer_norm(pair.astype(jnp.float32), norm_gain, norm_bias, 2).astype(jnp.bfloat16)
    projected = jnp.einsum(
        "rkc,cd->drk", normed, w_proj[:, : 4 * chan_count], preferred_element_type=jnp.float32
    )
    left_side = (
        jax.nn.sigmoid(projected[:chan_count]) * projected[chan_count : 2 * chan_count] * pair_flags
    ).astype(jnp.bfloat16)
    right_side = (
        jax.nn.sigmoid(projected[2 * chan_count : 3 * chan_count])
        * projected[3 * chan_count :]
        * pair_flags
    ).astype(jnp.bfloat16)
    gate_values = jax.nn.sigmoid(
        jnp.einsum(
            "rkc,cd->rkd", normed, w_proj[:, 4 * chan_count :], preferred_element_type=jnp.float32
        )
    ).astype(jnp.bfloat16)
    both_sides = jnp.stack([left_side, right_side], axis=1)
    both_group = lax.all_to_all(
        both_sides, ("wide", "narrow"), split_axis=0, concat_axis=2, tiled=True
    )
    left_group, right_group = both_group[:, 0], both_group[:, 1]
    partial_sums = jnp.einsum(
        "cik,cjk->cij", left_group, right_group, preferred_element_type=jnp.float32
    )
    summed = lax.psum_scatter(partial_sums, "sub", scatter_dimension=2, tiled=True).astype(
        jnp.bfloat16
    )
    returned = lax.all_to_all(summed, ("wide", "narrow"), split_axis=1, concat_axis=0, tiled=True)
    normed_out = layer_norm(
        returned.astype(jnp.float32), out_gain[:, None, None], out_bias[:, None, None], 0
    ).astype(jnp.bfloat16)
    result_out = jnp.einsum("crj,cd->rjd", normed_out, w_out, preferred_element_type=jnp.float32)
    return (gate_values.astype(jnp.float32) * result_out).astype(jnp.bfloat16)


def local(pair, *rest):
    row_count, col_count, chan_count = pair.shape
    shards = lax.axis_size(axes)
    fits = (
        lax.axis_size("sub") == 1
        and (row_count, col_count, chan_count) == (4, 128, 128)
        and shards * row_count == col_count
        and shards * 4 == chan_count
        and shards == 8 * planes
    )
    return (local_blocks if fits else local_arrays)(pair, *rest)


def solution(mesh):
    in_specs = (
        P(("parts", "wide", "narrow"), "sub", None),
        P("parts"),
        P(),
        P(),
        P(),
        P(),
        P(),
        P(),
    )
    out_specs = P(("parts", "wide", "narrow"), "sub", None)
    return jax.shard_map(local, mesh=mesh, in_specs=in_specs, out_specs=out_specs, check_vma=False)
```

```python
import functools

import jax
import jax.numpy as jnp
from jax import lax
from jax.experimental import pallas as pl
from jax.experimental.pallas import tpu as pltpu
from jax.sharding import PartitionSpec as P

epsilon = 1e-05
axes = ("wide", "narrow")
kernel_vmem = 8 * 2**20
planes = 4


def layer_norm(values, gain_vec, bias_vec, axis_dim):
    average = jnp.mean(values, axis=axis_dim, keepdims=True)
    centered = values - average
    variance = jnp.mean(centered * centered, axis=axis_dim, keepdims=True)
    return centered * lax.rsqrt(variance + epsilon) * gain_vec + bias_vec


def sigmoid(values):
    return 0.5 + 0.5 * jnp.tanh(0.5 * values)


def swap_halves(low, high):
    first = lax.broadcasted_iota(jnp.int32, low.shape, 0) < 4
    return (
        jnp.where(first, low, pltpu.roll(high, 4, 0)),
        jnp.where(first, pltpu.roll(low, 4, 0), high),
    )


def project_kernel(
    pair_hbm, valid_hbm, gain_hbm, bias_hbm, w_hbm, out_gain_hbm, out_bias_hbm, w_out_hbm,
    out_ref, normed_ref, w_gate_ref, out_gain_ref, out_bias_ref, w_out_ref,
    pair_ref, valid_ref, gain_ref, bias_ref, w_ref, sems,
):
    row_count, col_count, chan_count = pair_ref.shape
    quarter = chan_count // 4
    pairs = [(pair_hbm.at[r], pair_ref.at[r]) for r in range(row_count)]
    for i in range(0, chan_count, quarter):
        rows = pl.ds(i, quarter)
        pairs.append((w_hbm.at[rows, : 4 * chan_count], w_ref.at[rows]))
    pairs += [(gain_hbm, gain_ref), (bias_hbm, bias_ref), (valid_hbm, valid_ref)]
    needed = len(pairs)
    pairs += [
        (w_hbm.at[:, 4 * chan_count :], w_gate_ref), (out_gain_hbm, out_gain_ref),
        (out_bias_hbm, out_bias_ref), (w_out_hbm, w_out_ref),
    ]
    fetches = [
        pltpu.make_async_copy(source, held, sems.at[i]) for i, (source, held) in enumerate(pairs)
    ]
    for fetch in fetches:
        fetch.start()
    row_start = lax.axis_index(axes) * row_count
    for fetch in fetches[:needed]:
        fetch.wait()
    tokens = pair_ref[...].reshape(row_count * col_count, chan_count).astype(jnp.float32)
    normed = layer_norm(tokens, gain_ref[...], bias_ref[...], 1).astype(jnp.bfloat16)
    normed_ref[...] = normed
    projected = lax.dot_general(
        w_ref[...], normed, (((0,), (1,)), ((), ())),
        preferred_element_type=jnp.float32,
    )
    col_flags = valid_ref[...].astype(jnp.float32)
    places = lax.broadcasted_iota(jnp.int32, col_flags.shape, 1)
    row_flags = [
        jnp.sum(jnp.where(places == row_start + r, col_flags, 0.0), axis=1, keepdims=True)
        for r in range(row_count)
    ]
    flags = jnp.concatenate([col_flags * row_flag for row_flag in row_flags], axis=1)
    for chan in range(0, chan_count, 8):
        a_gate, a, b_gate, b = (
            projected[i * chan_count + chan : i * chan_count + chan + 8] for i in range(4)
        )
        left = sigmoid(a_gate) * a * flags
        right = sigmoid(b_gate) * b * flags
        for half, block in enumerate(swap_halves(left, right)):
            for r in range(0, row_count, 2):
                rows = jnp.concatenate(
                    [block[:, (r + i) * col_count : (r + i + 1) * col_count] for i in range(2)], axis=0
                )
                out_ref[spot(chan // 4 + half), r * 8 : (r + 2) * 8, :] = rows.astype(jnp.bfloat16)
    for fetch in fetches[needed:]:
        fetch.wait()


def group_order():
    chips = []
    for turn, place in enumerate((3, 2, 0, 1)):
        chips += [plane * 4 + place for plane in range(planes)][:: 1 - 2 * (turn % 2)]
    return [2 * chip + core for chip in chips for core in range(2)]


def spot(device):
    return group_order().index(device)


def receive_blocks(blocks_ref, held_ref):
    rows = blocks_ref.shape[1]
    for i, device in enumerate(group_order()):
        held_ref[device * rows : (device + 1) * rows, :] = blocks_ref[i].astype(jnp.float32)


def exchange(blocks):
    return lax.all_to_all(
        blocks, axes, split_axis=0, concat_axis=0, axis_index_groups=[group_order()], tiled=True
    )


def contract_kernel(
    blocks_ref, normed_ref, w_gate_ref, gain_ref, bias_ref,
    out_ref, gate_ref, scales_ref, held_ref,
):
    total = held_ref.shape[0] // 8
    receive_blocks(blocks_ref, held_ref)
    products = []
    for c in range(4):
        left = held_ref[pl.ds(c, total, stride=8), :].astype(jnp.bfloat16)
        right = held_ref[pl.ds(4 + c, total, stride=8), :].astype(jnp.bfloat16)
        products.append(
            lax.dot_general(
                left, right, (((1,), (1,)), ((), ())), preferred_element_type=jnp.float32
            )
        )
    for row in range(0, total, 8):
        pieces = [product[row : row + 8] for product in products]
        low, high = swap_halves(pieces[0], pieces[1]), swap_halves(pieces[2], pieces[3])
        for half in range(2):
            rows = jnp.concatenate([low[half], high[half]], axis=0)
            out_ref[spot(row // 4 + half)] = rows.astype(jnp.bfloat16)
    gate = jnp.dot(normed_ref[...], w_gate_ref[...], preferred_element_type=jnp.float32)
    gate_ref[...] = sigmoid(gate).astype(jnp.bfloat16)
    for i, vector_ref in enumerate((gain_ref, bias_ref)):
        scales_ref[i] = jnp.transpose(jnp.broadcast_to(vector_ref[...], scales_ref.shape[1:]))


def finish_kernel(blocks_ref, gate_ref, scales_ref, w_ref, out_ref, held_ref):
    row_count, col_count, chan_count = out_ref.shape
    receive_blocks(blocks_ref, held_ref)
    for r in range(row_count):
        triangle = held_ref[pl.ds(r, chan_count, stride=row_count), :]
        normed = layer_norm(triangle, scales_ref[0], scales_ref[1], 0).astype(jnp.bfloat16)
        result = lax.dot_general(
            normed, w_ref[...], (((0,), (0,)), ((), ())), preferred_element_type=jnp.float32
        )
        gate = gate_ref[r * col_count : (r + 1) * col_count, :].astype(jnp.float32)
        out_ref[r] = (gate * result).astype(jnp.bfloat16)


def local_blocks(pair, valid, norm_gain, norm_bias, w_proj, out_gain, out_bias, w_out):
    row_count, col_count, chan_count = pair.shape
    shards = lax.axis_size(axes)
    tokens = row_count * col_count
    vmem = pl.BlockSpec(memory_space=pltpu.VMEM)
    hbm = pl.BlockSpec(memory_space=pltpu.HBM)

    def line(vector):
        return vector.reshape(1, -1)

    def shaped(*dims):
        return jax.ShapeDtypeStruct(dims, jnp.bfloat16)

    def in_hbm(array):
        return pltpu.with_memory_space_constraint(array, pltpu.HBM)

    limit = pltpu.CompilerParams(vmem_limit_bytes=kernel_vmem)
    vector = jax.ShapeDtypeStruct((1, chan_count), jnp.float32)
    square = shaped(chan_count, chan_count)
    sides, normed, w_gate, out_gain, out_bias, w_out = pl.pallas_call(
        project_kernel,
        out_shape=(
            shaped(shards, 8 * row_count, col_count), shaped(tokens, chan_count),
            square, vector, vector, square,
        ),
        in_specs=[hbm] * 8,
        out_specs=(vmem,) * 6,
        scratch_shapes=[
            pltpu.VMEM(pair.shape, jnp.bfloat16),
            pltpu.VMEM((1, col_count), jnp.int32),
            pltpu.VMEM((1, chan_count), jnp.float32),
            pltpu.VMEM((1, chan_count), jnp.float32),
            pltpu.VMEM((chan_count, 4 * chan_count), jnp.bfloat16),
            pltpu.SemaphoreType.DMA((row_count + 11,)),
        ],
        compiler_params=limit,
        name="project",
    )(*map(in_hbm, (
        pair, line(valid), line(norm_gain), line(norm_bias), w_proj,
        line(out_gain), line(out_bias), w_out,
    )))
    sides = exchange(sides)
    triangle, gate_values, scales = pl.pallas_call(
        contract_kernel,
        out_shape=(
            shaped(shards, 4 * row_count, col_count),
            shaped(tokens, chan_count),
            jax.ShapeDtypeStruct((2, chan_count, col_count), jnp.float32),
        ),
        in_specs=[vmem] * 5,
        out_specs=(vmem,) * 3,
        scratch_shapes=[pltpu.VMEM((8 * col_count, col_count), jnp.float32)],
        compiler_params=limit,
        name="contract",
    )(sides, normed, w_gate, out_gain, out_bias)
    triangle = exchange(triangle)
    return pl.pallas_call(
        finish_kernel,
        out_shape=shaped(row_count, col_count, chan_count),
        in_specs=[vmem] * 4,
        out_specs=vmem,
        scratch_shapes=[pltpu.VMEM((tokens, chan_count), jnp.float32)],
        compiler_params=limit,
        name="finish",
    )(triangle, gate_values, scales, w_out)


def local_arrays(pair, valid, norm_gain, norm_bias, w_proj, out_gain, out_bias, w_out):
    row_count, col_count, chan_count = pair.shape
    row_start = lax.axis_index(("wide", "narrow")) * row_count
    col_start = lax.axis_index("sub") * col_count
    row_flags = lax.dynamic_slice_in_dim(valid, row_start, row_count, 0).astype(jnp.float32)
    col_flags = lax.dynamic_slice_in_dim(valid, col_start, col_count, 0).astype(jnp.float32)
    pair_flags = row_flags[:, None] * col_flags[None, :]
    normed = layer_norm(pair.astype(jnp.float32), norm_gain, norm_bias, 2).astype(jnp.bfloat16)
    projected = jnp.einsum(
        "rkc,cd->drk", normed, w_proj[:, : 4 * chan_count], preferred_element_type=jnp.float32
    )
    left_side = (
        jax.nn.sigmoid(projected[:chan_count]) * projected[chan_count : 2 * chan_count] * pair_flags
    ).astype(jnp.bfloat16)
    right_side = (
        jax.nn.sigmoid(projected[2 * chan_count : 3 * chan_count])
        * projected[3 * chan_count :]
        * pair_flags
    ).astype(jnp.bfloat16)
    gate_values = jax.nn.sigmoid(
        jnp.einsum(
            "rkc,cd->rkd", normed, w_proj[:, 4 * chan_count :], preferred_element_type=jnp.float32
        )
    ).astype(jnp.bfloat16)
    both_sides = jnp.stack([left_side, right_side], axis=1)
    both_group = lax.all_to_all(
        both_sides, ("wide", "narrow"), split_axis=0, concat_axis=2, tiled=True
    )
    left_group, right_group = both_group[:, 0], both_group[:, 1]
    partial_sums = jnp.einsum(
        "cik,cjk->cij", left_group, right_group, preferred_element_type=jnp.float32
    )
    summed = lax.psum_scatter(partial_sums, "sub", scatter_dimension=2, tiled=True).astype(
        jnp.bfloat16
    )
    returned = lax.all_to_all(summed, ("wide", "narrow"), split_axis=1, concat_axis=0, tiled=True)
    normed_out = layer_norm(
        returned.astype(jnp.float32), out_gain[:, None, None], out_bias[:, None, None], 0
    ).astype(jnp.bfloat16)
    result_out = jnp.einsum("crj,cd->rjd", normed_out, w_out, preferred_element_type=jnp.float32)
    return (gate_values.astype(jnp.float32) * result_out).astype(jnp.bfloat16)


def local(pair, *rest):
    row_count, col_count, chan_count = pair.shape
    shards = lax.axis_size(axes)
    fits = (
        lax.axis_size("sub") == 1
        and (row_count, col_count, chan_count) == (4, 128, 128)
        and shards * row_count == col_count
        and shards * 4 == chan_count
        and shards == 8 * planes
    )
    return (local_blocks if fits else local_arrays)(pair, *rest)


def solution(mesh):
    in_specs = (
        P(("parts", "wide", "narrow"), "sub", None),
        P("parts"),
        P(),
        P(),
        P(),
        P(),
        P(),
        P(),
    )
    out_specs = P(("parts", "wide", "narrow"), "sub", None)
    return jax.shard_map(local, mesh=mesh, in_specs=in_specs, out_specs=out_specs, check_vma=False)
```

```python
import functools

import jax
import jax.numpy as jnp
from jax import lax
from jax.experimental import pallas as pl
from jax.experimental.pallas import tpu as pltpu
from jax.sharding import PartitionSpec as P

epsilon = 1e-05
axes = ("wide", "narrow")
kernel_vmem = 8 * 2**20
planes = 4


def layer_norm(values, gain_vec, bias_vec, axis_dim):
    average = jnp.mean(values, axis=axis_dim, keepdims=True)
    centered = values - average
    variance = jnp.mean(centered * centered, axis=axis_dim, keepdims=True)
    return centered * lax.rsqrt(variance + epsilon) * gain_vec + bias_vec


def sigmoid(values):
    return 0.5 + 0.5 * jnp.tanh(0.5 * values)


def swap_halves(low, high):
    first = lax.broadcasted_iota(jnp.int32, low.shape, 0) < 4
    return (
        jnp.where(first, low, pltpu.roll(high, 4, 0)),
        jnp.where(first, pltpu.roll(low, 4, 0), high),
    )


def project_kernel(
    pair_hbm, valid_hbm, gain_hbm, bias_hbm, w_hbm, out_gain_hbm, out_bias_hbm, w_out_hbm,
    out_ref, normed_ref, w_gate_ref, out_gain_ref, out_bias_ref, w_out_ref,
    pair_ref, valid_ref, gain_ref, bias_ref, w_ref, sems,
):
    row_count, col_count, chan_count = pair_ref.shape
    quarter = chan_count // 4
    pairs = [(pair_hbm.at[r], pair_ref.at[r]) for r in range(row_count)]
    for i in range(0, chan_count, quarter):
        rows = pl.ds(i, quarter)
        pairs.append((w_hbm.at[rows, : 4 * chan_count], w_ref.at[rows]))
    pairs += [(gain_hbm, gain_ref), (bias_hbm, bias_ref), (valid_hbm, valid_ref)]
    needed = len(pairs)
    pairs += [
        (w_hbm.at[:, 4 * chan_count :], w_gate_ref), (out_gain_hbm, out_gain_ref),
        (out_bias_hbm, out_bias_ref), (w_out_hbm, w_out_ref),
    ]
    fetches = [
        pltpu.make_async_copy(source, held, sems.at[i]) for i, (source, held) in enumerate(pairs)
    ]
    for fetch in fetches:
        fetch.start()
    row_start = lax.axis_index(axes) * row_count
    for fetch in fetches[:needed]:
        fetch.wait()
    tokens = pair_ref[...].reshape(row_count * col_count, chan_count).astype(jnp.float32)
    normed = layer_norm(tokens, gain_ref[...], bias_ref[...], 1).astype(jnp.bfloat16)
    normed_ref[...] = normed
    projected = lax.dot_general(
        w_ref[...], normed, (((0,), (1,)), ((), ())),
        preferred_element_type=jnp.float32,
    )
    col_flags = valid_ref[...].astype(jnp.float32)
    places = lax.broadcasted_iota(jnp.int32, col_flags.shape, 1)
    row_flags = [
        jnp.sum(jnp.where(places == row_start + r, col_flags, 0.0), axis=1, keepdims=True)
        for r in range(row_count)
    ]
    flags = jnp.concatenate([col_flags * row_flag for row_flag in row_flags], axis=1)
    for chan in range(0, chan_count, 8):
        a_gate, a, b_gate, b = (
            projected[i * chan_count + chan : i * chan_count + chan + 8] for i in range(4)
        )
        left = sigmoid(a_gate) * a * flags
        right = sigmoid(b_gate) * b * flags
        for half, block in enumerate(swap_halves(left, right)):
            for r in range(0, row_count, 2):
                rows = jnp.concatenate(
                    [block[:, (r + i) * col_count : (r + i + 1) * col_count] for i in range(2)], axis=0
                )
                out_ref[spot(chan // 4 + half), r * 8 : (r + 2) * 8, :] = rows.astype(jnp.bfloat16)
    for fetch in fetches[needed:]:
        fetch.wait()


def group_order():
    chips = []
    for turn, place in enumerate((0, 1, 3, 2)):
        chips += [plane * 4 + place for plane in range(planes)][:: 1 - 2 * (turn % 2)]
    return [2 * chip + core for chip in chips for core in (1, 0)]


def spot(device):
    return group_order().index(device)


def receive_blocks(blocks_ref, held_ref):
    rows = blocks_ref.shape[1]
    for i, device in enumerate(group_order()):
        held_ref[device * rows : (device + 1) * rows, :] = blocks_ref[i].astype(jnp.float32)


def exchange(blocks):
    return lax.all_to_all(
        blocks, axes, split_axis=0, concat_axis=0, axis_index_groups=[group_order()], tiled=True
    )


def contract_kernel(
    blocks_ref, normed_ref, w_gate_ref, gain_ref, bias_ref,
    out_ref, gate_ref, scales_ref, held_ref,
):
    total = held_ref.shape[0] // 8
    receive_blocks(blocks_ref, held_ref)
    products = []
    for c in range(4):
        left = held_ref[pl.ds(c, total, stride=8), :].astype(jnp.bfloat16)
        right = held_ref[pl.ds(4 + c, total, stride=8), :].astype(jnp.bfloat16)
        products.append(
            lax.dot_general(
                left, right, (((1,), (1,)), ((), ())), preferred_element_type=jnp.float32
            )
        )
    for row in range(0, total, 8):
        pieces = [product[row : row + 8] for product in products]
        low, high = swap_halves(pieces[0], pieces[1]), swap_halves(pieces[2], pieces[3])
        for half in range(2):
            rows = jnp.concatenate([low[half], high[half]], axis=0)
            out_ref[spot(row // 4 + half)] = rows.astype(jnp.bfloat16)
    gate = jnp.dot(normed_ref[...], w_gate_ref[...], preferred_element_type=jnp.float32)
    gate_ref[...] = sigmoid(gate).astype(jnp.bfloat16)
    for i, vector_ref in enumerate((gain_ref, bias_ref)):
        scales_ref[i] = jnp.transpose(jnp.broadcast_to(vector_ref[...], scales_ref.shape[1:]))


def finish_kernel(blocks_ref, gate_ref, scales_ref, w_ref, out_ref, held_ref):
    row_count, col_count, chan_count = out_ref.shape
    receive_blocks(blocks_ref, held_ref)
    for r in range(row_count):
        triangle = held_ref[pl.ds(r, chan_count, stride=row_count), :]
        normed = layer_norm(triangle, scales_ref[0], scales_ref[1], 0).astype(jnp.bfloat16)
        result = lax.dot_general(
            normed, w_ref[...], (((0,), (0,)), ((), ())), preferred_element_type=jnp.float32
        )
        gate = gate_ref[r * col_count : (r + 1) * col_count, :].astype(jnp.float32)
        out_ref[r] = (gate * result).astype(jnp.bfloat16)


def local_blocks(pair, valid, norm_gain, norm_bias, w_proj, out_gain, out_bias, w_out):
    row_count, col_count, chan_count = pair.shape
    shards = lax.axis_size(axes)
    tokens = row_count * col_count
    vmem = pl.BlockSpec(memory_space=pltpu.VMEM)
    hbm = pl.BlockSpec(memory_space=pltpu.HBM)

    def line(vector):
        return vector.reshape(1, -1)

    def shaped(*dims):
        return jax.ShapeDtypeStruct(dims, jnp.bfloat16)

    def in_hbm(array):
        return pltpu.with_memory_space_constraint(array, pltpu.HBM)

    limit = pltpu.CompilerParams(vmem_limit_bytes=kernel_vmem)
    vector = jax.ShapeDtypeStruct((1, chan_count), jnp.float32)
    square = shaped(chan_count, chan_count)
    sides, normed, w_gate, out_gain, out_bias, w_out = pl.pallas_call(
        project_kernel,
        out_shape=(
            shaped(shards, 8 * row_count, col_count), shaped(tokens, chan_count),
            square, vector, vector, square,
        ),
        in_specs=[hbm] * 8,
        out_specs=(vmem,) * 6,
        scratch_shapes=[
            pltpu.VMEM(pair.shape, jnp.bfloat16),
            pltpu.VMEM((1, col_count), jnp.int32),
            pltpu.VMEM((1, chan_count), jnp.float32),
            pltpu.VMEM((1, chan_count), jnp.float32),
            pltpu.VMEM((chan_count, 4 * chan_count), jnp.bfloat16),
            pltpu.SemaphoreType.DMA((row_count + 11,)),
        ],
        compiler_params=limit,
        name="project",
    )(*map(in_hbm, (
        pair, line(valid), line(norm_gain), line(norm_bias), w_proj,
        line(out_gain), line(out_bias), w_out,
    )))
    sides = exchange(sides)
    triangle, gate_values, scales = pl.pallas_call(
        contract_kernel,
        out_shape=(
            shaped(shards, 4 * row_count, col_count),
            shaped(tokens, chan_count),
            jax.ShapeDtypeStruct((2, chan_count, col_count), jnp.float32),
        ),
        in_specs=[vmem] * 5,
        out_specs=(vmem,) * 3,
        scratch_shapes=[pltpu.VMEM((8 * col_count, col_count), jnp.float32)],
        compiler_params=limit,
        name="contract",
    )(sides, normed, w_gate, out_gain, out_bias)
    triangle = exchange(triangle)
    return pl.pallas_call(
        finish_kernel,
        out_shape=shaped(row_count, col_count, chan_count),
        in_specs=[vmem] * 4,
        out_specs=vmem,
        scratch_shapes=[pltpu.VMEM((tokens, chan_count), jnp.float32)],
        compiler_params=limit,
        name="finish",
    )(triangle, gate_values, scales, w_out)


def local_arrays(pair, valid, norm_gain, norm_bias, w_proj, out_gain, out_bias, w_out):
    row_count, col_count, chan_count = pair.shape
    row_start = lax.axis_index(("wide", "narrow")) * row_count
    col_start = lax.axis_index("sub") * col_count
    row_flags = lax.dynamic_slice_in_dim(valid, row_start, row_count, 0).astype(jnp.float32)
    col_flags = lax.dynamic_slice_in_dim(valid, col_start, col_count, 0).astype(jnp.float32)
    pair_flags = row_flags[:, None] * col_flags[None, :]
    normed = layer_norm(pair.astype(jnp.float32), norm_gain, norm_bias, 2).astype(jnp.bfloat16)
    projected = jnp.einsum(
        "rkc,cd->drk", normed, w_proj[:, : 4 * chan_count], preferred_element_type=jnp.float32
    )
    left_side = (
        jax.nn.sigmoid(projected[:chan_count]) * projected[chan_count : 2 * chan_count] * pair_flags
    ).astype(jnp.bfloat16)
    right_side = (
        jax.nn.sigmoid(projected[2 * chan_count : 3 * chan_count])
        * projected[3 * chan_count :]
        * pair_flags
    ).astype(jnp.bfloat16)
    gate_values = jax.nn.sigmoid(
        jnp.einsum(
            "rkc,cd->rkd", normed, w_proj[:, 4 * chan_count :], preferred_element_type=jnp.float32
        )
    ).astype(jnp.bfloat16)
    both_sides = jnp.stack([left_side, right_side], axis=1)
    both_group = lax.all_to_all(
        both_sides, ("wide", "narrow"), split_axis=0, concat_axis=2, tiled=True
    )
    left_group, right_group = both_group[:, 0], both_group[:, 1]
    partial_sums = jnp.einsum(
        "cik,cjk->cij", left_group, right_group, preferred_element_type=jnp.float32
    )
    summed = lax.psum_scatter(partial_sums, "sub", scatter_dimension=2, tiled=True).astype(
        jnp.bfloat16
    )
    returned = lax.all_to_all(summed, ("wide", "narrow"), split_axis=1, concat_axis=0, tiled=True)
    normed_out = layer_norm(
        returned.astype(jnp.float32), out_gain[:, None, None], out_bias[:, None, None], 0
    ).astype(jnp.bfloat16)
    result_out = jnp.einsum("crj,cd->rjd", normed_out, w_out, preferred_element_type=jnp.float32)
    return (gate_values.astype(jnp.float32) * result_out).astype(jnp.bfloat16)


def local(pair, *rest):
    row_count, col_count, chan_count = pair.shape
    shards = lax.axis_size(axes)
    fits = (
        lax.axis_size("sub") == 1
        and (row_count, col_count, chan_count) == (4, 128, 128)
        and shards * row_count == col_count
        and shards * 4 == chan_count
        and shards == 8 * planes
    )
    return (local_blocks if fits else local_arrays)(pair, *rest)


def solution(mesh):
    in_specs = (
        P(("parts", "wide", "narrow"), "sub", None),
        P("parts"),
        P(),
        P(),
        P(),
        P(),
        P(),
        P(),
    )
    out_specs = P(("parts", "wide", "narrow"), "sub", None)
    return jax.shard_map(local, mesh=mesh, in_specs=in_specs, out_specs=out_specs, check_vma=False)
```

```python
import functools

import jax
import jax.numpy as jnp
from jax import lax
from jax.experimental import pallas as pl
from jax.experimental.pallas import tpu as pltpu
from jax.sharding import PartitionSpec as P

epsilon = 1e-05
axes = ("wide", "narrow")
kernel_vmem = 8 * 2**20
planes = 4


def layer_norm(values, gain_vec, bias_vec, axis_dim):
    average = jnp.mean(values, axis=axis_dim, keepdims=True)
    centered = values - average
    variance = jnp.mean(centered * centered, axis=axis_dim, keepdims=True)
    return centered * lax.rsqrt(variance + epsilon) * gain_vec + bias_vec


def sigmoid(values):
    return 0.5 + 0.5 * jnp.tanh(0.5 * values)


def swap_halves(low, high):
    first = lax.broadcasted_iota(jnp.int32, low.shape, 0) < 4
    return (
        jnp.where(first, low, pltpu.roll(high, 4, 0)),
        jnp.where(first, pltpu.roll(low, 4, 0), high),
    )


def project_kernel(
    pair_hbm, valid_hbm, gain_hbm, bias_hbm, w_hbm, out_gain_hbm, out_bias_hbm, w_out_hbm,
    out_ref, normed_ref, w_gate_ref, out_gain_ref, out_bias_ref, w_out_ref,
    pair_ref, valid_ref, gain_ref, bias_ref, w_ref, sems,
):
    row_count, col_count, chan_count = pair_ref.shape
    quarter = chan_count // 4
    pairs = [(pair_hbm.at[r], pair_ref.at[r]) for r in range(row_count)]
    for i in range(0, chan_count, quarter):
        rows = pl.ds(i, quarter)
        pairs.append((w_hbm.at[rows, : 4 * chan_count], w_ref.at[rows]))
    pairs += [(gain_hbm, gain_ref), (bias_hbm, bias_ref), (valid_hbm, valid_ref)]
    needed = len(pairs)
    pairs += [
        (w_hbm.at[:, 4 * chan_count :], w_gate_ref), (out_gain_hbm, out_gain_ref),
        (out_bias_hbm, out_bias_ref), (w_out_hbm, w_out_ref),
    ]
    fetches = [
        pltpu.make_async_copy(source, held, sems.at[i]) for i, (source, held) in enumerate(pairs)
    ]
    for fetch in fetches:
        fetch.start()
    row_start = lax.axis_index(axes) * row_count
    for fetch in fetches[:needed]:
        fetch.wait()
    tokens = pair_ref[...].reshape(row_count * col_count, chan_count).astype(jnp.float32)
    normed = layer_norm(tokens, gain_ref[...], bias_ref[...], 1).astype(jnp.bfloat16)
    normed_ref[...] = normed
    projected = lax.dot_general(
        w_ref[...], normed, (((0,), (1,)), ((), ())),
        preferred_element_type=jnp.float32,
    )
    col_flags = valid_ref[...].astype(jnp.float32)
    places = lax.broadcasted_iota(jnp.int32, col_flags.shape, 1)
    row_flags = [
        jnp.sum(jnp.where(places == row_start + r, col_flags, 0.0), axis=1, keepdims=True)
        for r in range(row_count)
    ]
    flags = jnp.concatenate([col_flags * row_flag for row_flag in row_flags], axis=1)
    for chan in range(0, chan_count, 8):
        a_gate, a, b_gate, b = (
            projected[i * chan_count + chan : i * chan_count + chan + 8] for i in range(4)
        )
        left = sigmoid(a_gate) * a * flags
        right = sigmoid(b_gate) * b * flags
        for half, block in enumerate(swap_halves(left, right)):
            for r in range(0, row_count, 2):
                rows = jnp.concatenate(
                    [block[:, (r + i) * col_count : (r + i + 1) * col_count] for i in range(2)], axis=0
                )
                out_ref[sides_order().index(chan // 4 + half), r * 8 : (r + 2) * 8, :] = rows.astype(jnp.bfloat16)
    for fetch in fetches[needed:]:
        fetch.wait()


def sides_order():
    return list(range(8 * planes))[::-1]


def triangle_order():
    chips = []
    for turn, place in enumerate((0, 1, 3, 2)):
        chips += [plane * 4 + place for plane in range(planes)][:: 1 - 2 * (turn % 2)]
    return [2 * chip + core for chip in chips for core in range(2)][::-1]


def receive_blocks(blocks_ref, held_ref, order):
    rows = blocks_ref.shape[1]
    for i, device in enumerate(order):
        held_ref[device * rows : (device + 1) * rows, :] = blocks_ref[i].astype(jnp.float32)


def exchange(blocks, order):
    return lax.all_to_all(
        blocks, axes, split_axis=0, concat_axis=0, axis_index_groups=[order], tiled=True
    )


def contract_kernel(
    blocks_ref, normed_ref, w_gate_ref, gain_ref, bias_ref,
    out_ref, gate_ref, scales_ref, held_ref,
):
    total = held_ref.shape[0] // 8
    receive_blocks(blocks_ref, held_ref, sides_order())
    products = []
    for c in range(4):
        left = held_ref[pl.ds(c, total, stride=8), :].astype(jnp.bfloat16)
        right = held_ref[pl.ds(4 + c, total, stride=8), :].astype(jnp.bfloat16)
        products.append(
            lax.dot_general(
                left, right, (((1,), (1,)), ((), ())), preferred_element_type=jnp.float32
            )
        )
    for row in range(0, total, 8):
        pieces = [product[row : row + 8] for product in products]
        low, high = swap_halves(pieces[0], pieces[1]), swap_halves(pieces[2], pieces[3])
        for half in range(2):
            rows = jnp.concatenate([low[half], high[half]], axis=0)
            out_ref[triangle_order().index(row // 4 + half)] = rows.astype(jnp.bfloat16)
    gate = jnp.dot(normed_ref[...], w_gate_ref[...], preferred_element_type=jnp.float32)
    gate_ref[...] = sigmoid(gate).astype(jnp.bfloat16)
    for i, vector_ref in enumerate((gain_ref, bias_ref)):
        scales_ref[i] = jnp.transpose(jnp.broadcast_to(vector_ref[...], scales_ref.shape[1:]))


def finish_kernel(blocks_ref, gate_ref, scales_ref, w_ref, out_ref, held_ref):
    row_count, col_count, chan_count = out_ref.shape
    receive_blocks(blocks_ref, held_ref, triangle_order())
    for r in range(row_count):
        triangle = held_ref[pl.ds(r, chan_count, stride=row_count), :]
        normed = layer_norm(triangle, scales_ref[0], scales_ref[1], 0).astype(jnp.bfloat16)
        result = lax.dot_general(
            normed, w_ref[...], (((0,), (0,)), ((), ())), preferred_element_type=jnp.float32
        )
        gate = gate_ref[r * col_count : (r + 1) * col_count, :].astype(jnp.float32)
        out_ref[r] = (gate * result).astype(jnp.bfloat16)


def local_blocks(pair, valid, norm_gain, norm_bias, w_proj, out_gain, out_bias, w_out):
    row_count, col_count, chan_count = pair.shape
    shards = lax.axis_size(axes)
    tokens = row_count * col_count
    vmem = pl.BlockSpec(memory_space=pltpu.VMEM)
    hbm = pl.BlockSpec(memory_space=pltpu.HBM)

    def line(vector):
        return vector.reshape(1, -1)

    def shaped(*dims):
        return jax.ShapeDtypeStruct(dims, jnp.bfloat16)

    def in_hbm(array):
        return pltpu.with_memory_space_constraint(array, pltpu.HBM)

    limit = pltpu.CompilerParams(vmem_limit_bytes=kernel_vmem)
    vector = jax.ShapeDtypeStruct((1, chan_count), jnp.float32)
    square = shaped(chan_count, chan_count)
    sides, normed, w_gate, out_gain, out_bias, w_out = pl.pallas_call(
        project_kernel,
        out_shape=(
            shaped(shards, 8 * row_count, col_count), shaped(tokens, chan_count),
            square, vector, vector, square,
        ),
        in_specs=[hbm] * 8,
        out_specs=(vmem,) * 6,
        scratch_shapes=[
            pltpu.VMEM(pair.shape, jnp.bfloat16),
            pltpu.VMEM((1, col_count), jnp.int32),
            pltpu.VMEM((1, chan_count), jnp.float32),
            pltpu.VMEM((1, chan_count), jnp.float32),
            pltpu.VMEM((chan_count, 4 * chan_count), jnp.bfloat16),
            pltpu.SemaphoreType.DMA((row_count + 11,)),
        ],
        compiler_params=limit,
        name="project",
    )(*map(in_hbm, (
        pair, line(valid), line(norm_gain), line(norm_bias), w_proj,
        line(out_gain), line(out_bias), w_out,
    )))
    sides = exchange(sides, sides_order())
    triangle, gate_values, scales = pl.pallas_call(
        contract_kernel,
        out_shape=(
            shaped(shards, 4 * row_count, col_count),
            shaped(tokens, chan_count),
            jax.ShapeDtypeStruct((2, chan_count, col_count), jnp.float32),
        ),
        in_specs=[vmem] * 5,
        out_specs=(vmem,) * 3,
        scratch_shapes=[pltpu.VMEM((8 * col_count, col_count), jnp.float32)],
        compiler_params=limit,
        name="contract",
    )(sides, normed, w_gate, out_gain, out_bias)
    triangle = exchange(triangle, triangle_order())
    return pl.pallas_call(
        finish_kernel,
        out_shape=shaped(row_count, col_count, chan_count),
        in_specs=[vmem] * 4,
        out_specs=vmem,
        scratch_shapes=[pltpu.VMEM((tokens, chan_count), jnp.float32)],
        compiler_params=limit,
        name="finish",
    )(triangle, gate_values, scales, w_out)


def local_arrays(pair, valid, norm_gain, norm_bias, w_proj, out_gain, out_bias, w_out):
    row_count, col_count, chan_count = pair.shape
    row_start = lax.axis_index(("wide", "narrow")) * row_count
    col_start = lax.axis_index("sub") * col_count
    row_flags = lax.dynamic_slice_in_dim(valid, row_start, row_count, 0).astype(jnp.float32)
    col_flags = lax.dynamic_slice_in_dim(valid, col_start, col_count, 0).astype(jnp.float32)
    pair_flags = row_flags[:, None] * col_flags[None, :]
    normed = layer_norm(pair.astype(jnp.float32), norm_gain, norm_bias, 2).astype(jnp.bfloat16)
    projected = jnp.einsum(
        "rkc,cd->drk", normed, w_proj[:, : 4 * chan_count], preferred_element_type=jnp.float32
    )
    left_side = (
        jax.nn.sigmoid(projected[:chan_count]) * projected[chan_count : 2 * chan_count] * pair_flags
    ).astype(jnp.bfloat16)
    right_side = (
        jax.nn.sigmoid(projected[2 * chan_count : 3 * chan_count])
        * projected[3 * chan_count :]
        * pair_flags
    ).astype(jnp.bfloat16)
    gate_values = jax.nn.sigmoid(
        jnp.einsum(
            "rkc,cd->rkd", normed, w_proj[:, 4 * chan_count :], preferred_element_type=jnp.float32
        )
    ).astype(jnp.bfloat16)
    both_sides = jnp.stack([left_side, right_side], axis=1)
    both_group = lax.all_to_all(
        both_sides, ("wide", "narrow"), split_axis=0, concat_axis=2, tiled=True
    )
    left_group, right_group = both_group[:, 0], both_group[:, 1]
    partial_sums = jnp.einsum(
        "cik,cjk->cij", left_group, right_group, preferred_element_type=jnp.float32
    )
    summed = lax.psum_scatter(partial_sums, "sub", scatter_dimension=2, tiled=True).astype(
        jnp.bfloat16
    )
    returned = lax.all_to_all(summed, ("wide", "narrow"), split_axis=1, concat_axis=0, tiled=True)
    normed_out = layer_norm(
        returned.astype(jnp.float32), out_gain[:, None, None], out_bias[:, None, None], 0
    ).astype(jnp.bfloat16)
    result_out = jnp.einsum("crj,cd->rjd", normed_out, w_out, preferred_element_type=jnp.float32)
    return (gate_values.astype(jnp.float32) * result_out).astype(jnp.bfloat16)


def local(pair, *rest):
    row_count, col_count, chan_count = pair.shape
    shards = lax.axis_size(axes)
    fits = (
        lax.axis_size("sub") == 1
        and (row_count, col_count, chan_count) == (4, 128, 128)
        and shards * row_count == col_count
        and shards * 4 == chan_count
        and shards == 8 * planes
    )
    return (local_blocks if fits else local_arrays)(pair, *rest)


def solution(mesh):
    in_specs = (
        P(("parts", "wide", "narrow"), "sub", None),
        P("parts"),
        P(),
        P(),
        P(),
        P(),
        P(),
        P(),
    )
    out_specs = P(("parts", "wide", "narrow"), "sub", None)
    return jax.shard_map(local, mesh=mesh, in_specs=in_specs, out_specs=out_specs, check_vma=False)
```

```python
import functools

import jax
import jax.numpy as jnp
from jax import lax
from jax.experimental import pallas as pl
from jax.experimental.pallas import tpu as pltpu
from jax.sharding import PartitionSpec as P

epsilon = 1e-05
axes = ("wide", "narrow")
kernel_vmem = 8 * 2**20
hub = 31


def layer_norm(values, gain_vec, bias_vec, axis_dim):
    average = jnp.mean(values, axis=axis_dim, keepdims=True)
    centered = values - average
    variance = jnp.mean(centered * centered, axis=axis_dim, keepdims=True)
    return centered * lax.rsqrt(variance + epsilon) * gain_vec + bias_vec


def sigmoid(values):
    return 0.5 + 0.5 * jnp.tanh(0.5 * values)


def swap_halves(low, high):
    first = lax.broadcasted_iota(jnp.int32, low.shape, 0) < 4
    return (
        jnp.where(first, low, pltpu.roll(high, 4, 0)),
        jnp.where(first, pltpu.roll(low, 4, 0), high),
    )


def project_kernel(
    pair_hbm, valid_hbm, gain_hbm, bias_hbm, w_hbm, out_gain_hbm, out_bias_hbm, w_out_hbm,
    out_ref, normed_ref, w_gate_ref, out_gain_ref, out_bias_ref, w_out_ref,
    pair_ref, valid_ref, gain_ref, bias_ref, w_ref, sems,
):
    row_count, col_count, chan_count = pair_ref.shape
    quarter = chan_count // 4
    pairs = [(pair_hbm.at[r], pair_ref.at[r]) for r in range(row_count)]
    for i in range(0, chan_count, quarter):
        rows = pl.ds(i, quarter)
        pairs.append((w_hbm.at[rows, : 4 * chan_count], w_ref.at[rows]))
    pairs += [(gain_hbm, gain_ref), (bias_hbm, bias_ref), (valid_hbm, valid_ref)]
    needed = len(pairs)
    pairs += [
        (w_hbm.at[:, 4 * chan_count :], w_gate_ref), (out_gain_hbm, out_gain_ref),
        (out_bias_hbm, out_bias_ref), (w_out_hbm, w_out_ref),
    ]
    fetches = [
        pltpu.make_async_copy(source, held, sems.at[i]) for i, (source, held) in enumerate(pairs)
    ]
    for fetch in fetches:
        fetch.start()
    row_start = lax.axis_index(axes) * row_count
    for fetch in fetches[:needed]:
        fetch.wait()
    tokens = pair_ref[...].reshape(row_count * col_count, chan_count).astype(jnp.float32)
    normed = layer_norm(tokens, gain_ref[...], bias_ref[...], 1).astype(jnp.bfloat16)
    normed_ref[...] = normed
    projected = lax.dot_general(
        w_ref[...], normed, (((0,), (1,)), ((), ())),
        preferred_element_type=jnp.float32,
    )
    col_flags = valid_ref[...].astype(jnp.float32)
    places = lax.broadcasted_iota(jnp.int32, col_flags.shape, 1)
    row_flags = [
        jnp.sum(jnp.where(places == row_start + r, col_flags, 0.0), axis=1, keepdims=True)
        for r in range(row_count)
    ]
    flags = jnp.concatenate([col_flags * row_flag for row_flag in row_flags], axis=1)
    for chan in range(0, chan_count, 8):
        a_gate, a, b_gate, b = (
            projected[i * chan_count + chan : i * chan_count + chan + 8] for i in range(4)
        )
        left = sigmoid(a_gate) * a * flags
        right = sigmoid(b_gate) * b * flags
        for half, block in enumerate(swap_halves(left, right)):
            for r in range(0, row_count, 2):
                rows = jnp.concatenate(
                    [block[:, (r + i) * col_count : (r + i + 1) * col_count] for i in range(2)], axis=0
                )
                out_ref[(chan // 4 + half) ^ hub, r * 8 : (r + 2) * 8, :] = rows.astype(jnp.bfloat16)
    for fetch in fetches[needed:]:
        fetch.wait()


def receive_blocks(blocks_ref, held_ref):
    shards, rows, _ = blocks_ref.shape
    for i in range(shards):
        held_ref[(i ^ hub) * rows : ((i ^ hub) + 1) * rows, :] = blocks_ref[i].astype(jnp.float32)


def exchange(blocks):
    groups = [[i ^ hub for i in range(blocks.shape[0])]]
    return lax.all_to_all(
        blocks, axes, split_axis=0, concat_axis=0, axis_index_groups=groups, tiled=True
    )


def contract_kernel(
    blocks_ref, normed_ref, w_gate_ref, gain_ref, bias_ref,
    out_ref, gate_ref, scales_ref, held_ref,
):
    total = held_ref.shape[0] // 8
    receive_blocks(blocks_ref, held_ref)
    products = []
    for c in range(4):
        left = held_ref[pl.ds(c, total, stride=8), :].astype(jnp.bfloat16)
        right = held_ref[pl.ds(4 + c, total, stride=8), :].astype(jnp.bfloat16)
        products.append(
            lax.dot_general(
                left, right, (((1,), (1,)), ((), ())), preferred_element_type=jnp.float32
            )
        )
    for row in range(0, total, 8):
        pieces = [product[row : row + 8] for product in products]
        low, high = swap_halves(pieces[0], pieces[1]), swap_halves(pieces[2], pieces[3])
        for half in range(2):
            rows = jnp.concatenate([low[half], high[half]], axis=0)
            out_ref[(row // 4 + half) ^ hub] = rows.astype(jnp.bfloat16)
    gate = jnp.dot(normed_ref[...], w_gate_ref[...], preferred_element_type=jnp.float32)
    gate_ref[...] = sigmoid(gate).astype(jnp.bfloat16)
    for i, vector_ref in enumerate((gain_ref, bias_ref)):
        scales_ref[i] = jnp.transpose(jnp.broadcast_to(vector_ref[...], scales_ref.shape[1:]))


def finish_kernel(blocks_ref, gate_ref, scales_ref, w_ref, out_ref, held_ref):
    row_count, col_count, chan_count = out_ref.shape
    receive_blocks(blocks_ref, held_ref)
    rows = range(row_count)
    triangle = jnp.concatenate(
        [held_ref[pl.ds(r, chan_count, stride=row_count), :] for r in rows], axis=1
    )
    gain, bias = (jnp.concatenate([scales_ref[i] for r in rows], axis=1) for i in range(2))
    normed = layer_norm(triangle, gain, bias, 0).astype(jnp.bfloat16)
    result = lax.dot_general(
        normed, w_ref[...], (((0,), (0,)), ((), ())), preferred_element_type=jnp.float32
    )
    update = (gate_ref[...].astype(jnp.float32) * result).astype(jnp.bfloat16)
    out_ref[...] = update.reshape(out_ref.shape)


def local_blocks(pair, valid, norm_gain, norm_bias, w_proj, out_gain, out_bias, w_out):
    row_count, col_count, chan_count = pair.shape
    shards = lax.axis_size(axes)
    tokens = row_count * col_count
    vmem = pl.BlockSpec(memory_space=pltpu.VMEM)
    hbm = pl.BlockSpec(memory_space=pltpu.HBM)

    def line(vector):
        return vector.reshape(1, -1)

    def shaped(*dims):
        return jax.ShapeDtypeStruct(dims, jnp.bfloat16)

    def in_hbm(array):
        return pltpu.with_memory_space_constraint(array, pltpu.HBM)

    limit = pltpu.CompilerParams(vmem_limit_bytes=kernel_vmem)
    vector = jax.ShapeDtypeStruct((1, chan_count), jnp.float32)
    square = shaped(chan_count, chan_count)
    sides, normed, w_gate, out_gain, out_bias, w_out = pl.pallas_call(
        project_kernel,
        out_shape=(
            shaped(shards, 8 * row_count, col_count), shaped(tokens, chan_count),
            square, vector, vector, square,
        ),
        in_specs=[hbm] * 8,
        out_specs=(vmem,) * 6,
        scratch_shapes=[
            pltpu.VMEM(pair.shape, jnp.bfloat16),
            pltpu.VMEM((1, col_count), jnp.int32),
            pltpu.VMEM((1, chan_count), jnp.float32),
            pltpu.VMEM((1, chan_count), jnp.float32),
            pltpu.VMEM((chan_count, 4 * chan_count), jnp.bfloat16),
            pltpu.SemaphoreType.DMA((row_count + 11,)),
        ],
        compiler_params=limit,
        name="project",
    )(*map(in_hbm, (
        pair, line(valid), line(norm_gain), line(norm_bias), w_proj,
        line(out_gain), line(out_bias), w_out,
    )))
    sides = exchange(sides)
    triangle, gate_values, scales = pl.pallas_call(
        contract_kernel,
        out_shape=(
            shaped(shards, 4 * row_count, col_count),
            shaped(tokens, chan_count),
            jax.ShapeDtypeStruct((2, chan_count, col_count), jnp.float32),
        ),
        in_specs=[vmem] * 5,
        out_specs=(vmem,) * 3,
        scratch_shapes=[pltpu.VMEM((8 * col_count, col_count), jnp.float32)],
        compiler_params=limit,
        name="contract",
    )(sides, normed, w_gate, out_gain, out_bias)
    triangle = exchange(triangle)
    return pl.pallas_call(
        finish_kernel,
        out_shape=shaped(row_count, col_count, chan_count),
        in_specs=[vmem] * 4,
        out_specs=vmem,
        scratch_shapes=[pltpu.VMEM((tokens, chan_count), jnp.float32)],
        compiler_params=limit,
        name="finish",
    )(triangle, gate_values, scales, w_out)


def local_arrays(pair, valid, norm_gain, norm_bias, w_proj, out_gain, out_bias, w_out):
    row_count, col_count, chan_count = pair.shape
    row_start = lax.axis_index(("wide", "narrow")) * row_count
    col_start = lax.axis_index("sub") * col_count
    row_flags = lax.dynamic_slice_in_dim(valid, row_start, row_count, 0).astype(jnp.float32)
    col_flags = lax.dynamic_slice_in_dim(valid, col_start, col_count, 0).astype(jnp.float32)
    pair_flags = row_flags[:, None] * col_flags[None, :]
    normed = layer_norm(pair.astype(jnp.float32), norm_gain, norm_bias, 2).astype(jnp.bfloat16)
    projected = jnp.einsum(
        "rkc,cd->drk", normed, w_proj[:, : 4 * chan_count], preferred_element_type=jnp.float32
    )
    left_side = (
        jax.nn.sigmoid(projected[:chan_count]) * projected[chan_count : 2 * chan_count] * pair_flags
    ).astype(jnp.bfloat16)
    right_side = (
        jax.nn.sigmoid(projected[2 * chan_count : 3 * chan_count])
        * projected[3 * chan_count :]
        * pair_flags
    ).astype(jnp.bfloat16)
    gate_values = jax.nn.sigmoid(
        jnp.einsum(
            "rkc,cd->rkd", normed, w_proj[:, 4 * chan_count :], preferred_element_type=jnp.float32
        )
    ).astype(jnp.bfloat16)
    both_sides = jnp.stack([left_side, right_side], axis=1)
    both_group = lax.all_to_all(
        both_sides, ("wide", "narrow"), split_axis=0, concat_axis=2, tiled=True
    )
    left_group, right_group = both_group[:, 0], both_group[:, 1]
    partial_sums = jnp.einsum(
        "cik,cjk->cij", left_group, right_group, preferred_element_type=jnp.float32
    )
    summed = lax.psum_scatter(partial_sums, "sub", scatter_dimension=2, tiled=True).astype(
        jnp.bfloat16
    )
    returned = lax.all_to_all(summed, ("wide", "narrow"), split_axis=1, concat_axis=0, tiled=True)
    normed_out = layer_norm(
        returned.astype(jnp.float32), out_gain[:, None, None], out_bias[:, None, None], 0
    ).astype(jnp.bfloat16)
    result_out = jnp.einsum("crj,cd->rjd", normed_out, w_out, preferred_element_type=jnp.float32)
    return (gate_values.astype(jnp.float32) * result_out).astype(jnp.bfloat16)


def local(pair, *rest):
    row_count, col_count, chan_count = pair.shape
    shards = lax.axis_size(axes)
    fits = (
        lax.axis_size("sub") == 1
        and (row_count, col_count, chan_count) == (4, 128, 128)
        and shards * row_count == col_count
        and shards * 4 == chan_count
        and shards == hub + 1
    )
    return (local_blocks if fits else local_arrays)(pair, *rest)


def solution(mesh):
    in_specs = (
        P(("parts", "wide", "narrow"), "sub", None),
        P("parts"),
        P(),
        P(),
        P(),
        P(),
        P(),
        P(),
    )
    out_specs = P(("parts", "wide", "narrow"), "sub", None)
    return jax.shard_map(local, mesh=mesh, in_specs=in_specs, out_specs=out_specs, check_vma=False)
```

```python
import functools

import jax
import jax.numpy as jnp
from jax import lax
from jax.experimental import pallas as pl
from jax.experimental.pallas import tpu as pltpu
from jax.sharding import PartitionSpec as P

epsilon = 1e-05
axes = ("wide", "narrow")
kernel_vmem = 8 * 2**20
hub = 31


def layer_norm(values, gain_vec, bias_vec, axis_dim):
    average = jnp.mean(values, axis=axis_dim, keepdims=True)
    centered = values - average
    variance = jnp.mean(centered * centered, axis=axis_dim, keepdims=True)
    return centered * lax.rsqrt(variance + epsilon) * gain_vec + bias_vec


def sigmoid(values):
    return 0.5 + 0.5 * jnp.tanh(0.5 * values)


def swap_halves(low, high):
    first = lax.broadcasted_iota(jnp.int32, low.shape, 0) < 4
    return (
        jnp.where(first, low, pltpu.roll(high, 4, 0)),
        jnp.where(first, pltpu.roll(low, 4, 0), high),
    )


def project_kernel(
    pair_hbm, valid_hbm, gain_hbm, bias_hbm, w_hbm, out_gain_hbm, out_bias_hbm, w_out_hbm,
    out_ref, normed_ref, w_gate_ref, out_gain_ref, out_bias_ref, w_out_ref,
    pair_ref, valid_ref, gain_ref, bias_ref, w_ref, sems,
):
    row_count, col_count, chan_count = pair_ref.shape
    quarter = chan_count // 4
    pairs = [(pair_hbm.at[r], pair_ref.at[r]) for r in range(row_count)]
    for i in range(0, chan_count, quarter):
        rows = pl.ds(i, quarter)
        pairs.append((w_hbm.at[rows, : 4 * chan_count], w_ref.at[rows]))
    pairs += [(gain_hbm, gain_ref), (bias_hbm, bias_ref), (valid_hbm, valid_ref)]
    needed = len(pairs)
    pairs += [
        (w_hbm.at[:, 4 * chan_count :], w_gate_ref), (out_gain_hbm, out_gain_ref),
        (out_bias_hbm, out_bias_ref), (w_out_hbm, w_out_ref),
    ]
    fetches = [
        pltpu.make_async_copy(source, held, sems.at[i]) for i, (source, held) in enumerate(pairs)
    ]
    for i, fetch in enumerate(fetches):
        fetch.start(priority=i % 2)
    row_start = lax.axis_index(axes) * row_count
    for fetch in fetches[:needed]:
        fetch.wait()
    tokens = pair_ref[...].reshape(row_count * col_count, chan_count).astype(jnp.float32)
    normed = layer_norm(tokens, gain_ref[...], bias_ref[...], 1).astype(jnp.bfloat16)
    normed_ref[...] = normed
    projected = lax.dot_general(
        w_ref[...], normed, (((0,), (1,)), ((), ())),
        preferred_element_type=jnp.float32,
    )
    col_flags = valid_ref[...].astype(jnp.float32)
    places = lax.broadcasted_iota(jnp.int32, col_flags.shape, 1)
    row_flags = [
        jnp.sum(jnp.where(places == row_start + r, col_flags, 0.0), axis=1, keepdims=True)
        for r in range(row_count)
    ]
    flags = jnp.concatenate([col_flags * row_flag for row_flag in row_flags], axis=1)
    for chan in range(0, chan_count, 8):
        a_gate, a, b_gate, b = (
            projected[i * chan_count + chan : i * chan_count + chan + 8] for i in range(4)
        )
        left = sigmoid(a_gate) * a * flags
        right = sigmoid(b_gate) * b * flags
        for half, block in enumerate(swap_halves(left, right)):
            for r in range(0, row_count, 2):
                rows = jnp.concatenate(
                    [block[:, (r + i) * col_count : (r + i + 1) * col_count] for i in range(2)], axis=0
                )
                out_ref[(chan // 4 + half) ^ hub, r * 8 : (r + 2) * 8, :] = rows.astype(jnp.bfloat16)
    for fetch in fetches[needed:]:
        fetch.wait()


def receive_blocks(blocks_ref, held_ref):
    shards, rows, _ = blocks_ref.shape
    for i in range(shards):
        held_ref[(i ^ hub) * rows : ((i ^ hub) + 1) * rows, :] = blocks_ref[i].astype(jnp.float32)


def exchange(blocks):
    groups = [[i ^ hub for i in range(blocks.shape[0])]]
    return lax.all_to_all(
        blocks, axes, split_axis=0, concat_axis=0, axis_index_groups=groups, tiled=True
    )


def contract_kernel(
    blocks_ref, normed_ref, w_gate_ref, gain_ref, bias_ref,
    out_ref, gate_ref, scales_ref, held_ref,
):
    total = held_ref.shape[0] // 8
    receive_blocks(blocks_ref, held_ref)
    products = []
    for c in range(4):
        left = held_ref[pl.ds(c, total, stride=8), :].astype(jnp.bfloat16)
        right = held_ref[pl.ds(4 + c, total, stride=8), :].astype(jnp.bfloat16)
        products.append(
            lax.dot_general(
                left, right, (((1,), (1,)), ((), ())), preferred_element_type=jnp.float32
            )
        )
    for row in range(0, total, 8):
        pieces = [product[row : row + 8] for product in products]
        low, high = swap_halves(pieces[0], pieces[1]), swap_halves(pieces[2], pieces[3])
        for half in range(2):
            rows = jnp.concatenate([low[half], high[half]], axis=0)
            out_ref[(row // 4 + half) ^ hub] = rows.astype(jnp.bfloat16)
    gate = jnp.dot(normed_ref[...], w_gate_ref[...], preferred_element_type=jnp.float32)
    gate_ref[...] = sigmoid(gate).astype(jnp.bfloat16)
    for i, vector_ref in enumerate((gain_ref, bias_ref)):
        scales_ref[i] = jnp.transpose(jnp.broadcast_to(vector_ref[...], scales_ref.shape[1:]))


def finish_kernel(blocks_ref, gate_ref, scales_ref, w_ref, out_ref, held_ref):
    row_count, col_count, chan_count = out_ref.shape
    receive_blocks(blocks_ref, held_ref)
    for r in range(row_count):
        triangle = held_ref[pl.ds(r, chan_count, stride=row_count), :]
        normed = layer_norm(triangle, scales_ref[0], scales_ref[1], 0).astype(jnp.bfloat16)
        result = lax.dot_general(
            normed, w_ref[...], (((0,), (0,)), ((), ())), preferred_element_type=jnp.float32
        )
        gate = gate_ref[r * col_count : (r + 1) * col_count, :].astype(jnp.float32)
        out_ref[r] = (gate * result).astype(jnp.bfloat16)


def local_blocks(pair, valid, norm_gain, norm_bias, w_proj, out_gain, out_bias, w_out):
    row_count, col_count, chan_count = pair.shape
    shards = lax.axis_size(axes)
    tokens = row_count * col_count
    vmem = pl.BlockSpec(memory_space=pltpu.VMEM)
    hbm = pl.BlockSpec(memory_space=pltpu.HBM)

    def line(vector):
        return vector.reshape(1, -1)

    def shaped(*dims):
        return jax.ShapeDtypeStruct(dims, jnp.bfloat16)

    def in_hbm(array):
        return pltpu.with_memory_space_constraint(array, pltpu.HBM)

    limit = pltpu.CompilerParams(vmem_limit_bytes=kernel_vmem)
    vector = jax.ShapeDtypeStruct((1, chan_count), jnp.float32)
    square = shaped(chan_count, chan_count)
    sides, normed, w_gate, out_gain, out_bias, w_out = pl.pallas_call(
        project_kernel,
        out_shape=(
            shaped(shards, 8 * row_count, col_count), shaped(tokens, chan_count),
            square, vector, vector, square,
        ),
        in_specs=[hbm] * 8,
        out_specs=(vmem,) * 6,
        scratch_shapes=[
            pltpu.VMEM(pair.shape, jnp.bfloat16),
            pltpu.VMEM((1, col_count), jnp.int32),
            pltpu.VMEM((1, chan_count), jnp.float32),
            pltpu.VMEM((1, chan_count), jnp.float32),
            pltpu.VMEM((chan_count, 4 * chan_count), jnp.bfloat16),
            pltpu.SemaphoreType.DMA((row_count + 11,)),
        ],
        compiler_params=limit,
        name="project",
    )(*map(in_hbm, (
        pair, line(valid), line(norm_gain), line(norm_bias), w_proj,
        line(out_gain), line(out_bias), w_out,
    )))
    sides = exchange(sides)
    triangle, gate_values, scales = pl.pallas_call(
        contract_kernel,
        out_shape=(
            shaped(shards, 4 * row_count, col_count),
            shaped(tokens, chan_count),
            jax.ShapeDtypeStruct((2, chan_count, col_count), jnp.float32),
        ),
        in_specs=[vmem] * 5,
        out_specs=(vmem,) * 3,
        scratch_shapes=[pltpu.VMEM((8 * col_count, col_count), jnp.float32)],
        compiler_params=limit,
        name="contract",
    )(sides, normed, w_gate, out_gain, out_bias)
    triangle = exchange(triangle)
    return pl.pallas_call(
        finish_kernel,
        out_shape=shaped(row_count, col_count, chan_count),
        in_specs=[vmem] * 4,
        out_specs=vmem,
        scratch_shapes=[pltpu.VMEM((tokens, chan_count), jnp.float32)],
        compiler_params=limit,
        name="finish",
    )(triangle, gate_values, scales, w_out)


def local_arrays(pair, valid, norm_gain, norm_bias, w_proj, out_gain, out_bias, w_out):
    row_count, col_count, chan_count = pair.shape
    row_start = lax.axis_index(("wide", "narrow")) * row_count
    col_start = lax.axis_index("sub") * col_count
    row_flags = lax.dynamic_slice_in_dim(valid, row_start, row_count, 0).astype(jnp.float32)
    col_flags = lax.dynamic_slice_in_dim(valid, col_start, col_count, 0).astype(jnp.float32)
    pair_flags = row_flags[:, None] * col_flags[None, :]
    normed = layer_norm(pair.astype(jnp.float32), norm_gain, norm_bias, 2).astype(jnp.bfloat16)
    projected = jnp.einsum(
        "rkc,cd->drk", normed, w_proj[:, : 4 * chan_count], preferred_element_type=jnp.float32
    )
    left_side = (
        jax.nn.sigmoid(projected[:chan_count]) * projected[chan_count : 2 * chan_count] * pair_flags
    ).astype(jnp.bfloat16)
    right_side = (
        jax.nn.sigmoid(projected[2 * chan_count : 3 * chan_count])
        * projected[3 * chan_count :]
        * pair_flags
    ).astype(jnp.bfloat16)
    gate_values = jax.nn.sigmoid(
        jnp.einsum(
            "rkc,cd->rkd", normed, w_proj[:, 4 * chan_count :], preferred_element_type=jnp.float32
        )
    ).astype(jnp.bfloat16)
    both_sides = jnp.stack([left_side, right_side], axis=1)
    both_group = lax.all_to_all(
        both_sides, ("wide", "narrow"), split_axis=0, concat_axis=2, tiled=True
    )
    left_group, right_group = both_group[:, 0], both_group[:, 1]
    partial_sums = jnp.einsum(
        "cik,cjk->cij", left_group, right_group, preferred_element_type=jnp.float32
    )
    summed = lax.psum_scatter(partial_sums, "sub", scatter_dimension=2, tiled=True).astype(
        jnp.bfloat16
    )
    returned = lax.all_to_all(summed, ("wide", "narrow"), split_axis=1, concat_axis=0, tiled=True)
    normed_out = layer_norm(
        returned.astype(jnp.float32), out_gain[:, None, None], out_bias[:, None, None], 0
    ).astype(jnp.bfloat16)
    result_out = jnp.einsum("crj,cd->rjd", normed_out, w_out, preferred_element_type=jnp.float32)
    return (gate_values.astype(jnp.float32) * result_out).astype(jnp.bfloat16)


def local(pair, *rest):
    row_count, col_count, chan_count = pair.shape
    shards = lax.axis_size(axes)
    fits = (
        lax.axis_size("sub") == 1
        and (row_count, col_count, chan_count) == (4, 128, 128)
        and shards * row_count == col_count
        and shards * 4 == chan_count
        and shards == hub + 1
    )
    return (local_blocks if fits else local_arrays)(pair, *rest)


def solution(mesh):
    in_specs = (
        P(("parts", "wide", "narrow"), "sub", None),
        P("parts"),
        P(),
        P(),
        P(),
        P(),
        P(),
        P(),
    )
    out_specs = P(("parts", "wide", "narrow"), "sub", None)
    return jax.shard_map(local, mesh=mesh, in_specs=in_specs, out_specs=out_specs, check_vma=False)
```

```python
import functools

import jax
import jax.numpy as jnp
from jax import lax
from jax.experimental import pallas as pl
from jax.experimental.pallas import tpu as pltpu
from jax.sharding import PartitionSpec as P

epsilon = 1e-05
axes = ("wide", "narrow")
kernel_vmem = 8 * 2**20
hub = 31


def layer_norm(values, gain_vec, bias_vec, axis_dim):
    average = jnp.mean(values, axis=axis_dim, keepdims=True)
    centered = values - average
    variance = jnp.mean(centered * centered, axis=axis_dim, keepdims=True)
    return centered * lax.rsqrt(variance + epsilon) * gain_vec + bias_vec


def sigmoid(values):
    return 0.5 + 0.5 * jnp.tanh(0.5 * values)


def swap_halves(low, high):
    first = lax.broadcasted_iota(jnp.int32, low.shape, 0) < 4
    return (
        jnp.where(first, low, pltpu.roll(high, 4, 0)),
        jnp.where(first, pltpu.roll(low, 4, 0), high),
    )


def project_kernel(
    pair_hbm, valid_hbm, gain_hbm, bias_hbm, w_hbm, out_gain_hbm, out_bias_hbm, w_out_hbm,
    out_ref, normed_ref, w_gate_ref, out_gain_ref, out_bias_ref, w_out_ref,
    pair_ref, valid_ref, gain_ref, bias_ref, w_ref, sems,
):
    row_count, col_count, chan_count = pair_ref.shape
    half_rows = chan_count // 2
    pairs = [(pair_hbm.at[r], pair_ref.at[r]) for r in range(row_count)]
    for i in range(0, chan_count, half_rows):
        rows = pl.ds(i, half_rows)
        pairs.append((w_hbm.at[rows], w_ref.at[rows]))
    pairs += [(gain_hbm, gain_ref), (bias_hbm, bias_ref), (valid_hbm, valid_ref)]
    needed = len(pairs)
    pairs += [
        (out_gain_hbm, out_gain_ref), (out_bias_hbm, out_bias_ref), (w_out_hbm, w_out_ref),
    ]
    fetches = [
        pltpu.make_async_copy(source, held, sems.at[i]) for i, (source, held) in enumerate(pairs)
    ]
    for fetch in fetches:
        fetch.start()
    row_start = lax.axis_index(axes) * row_count
    for fetch in fetches[:needed]:
        fetch.wait()
    tokens = pair_ref[...].reshape(row_count * col_count, chan_count).astype(jnp.float32)
    normed = layer_norm(tokens, gain_ref[...], bias_ref[...], 1).astype(jnp.bfloat16)
    normed_ref[...] = normed
    w_gate_ref[...] = w_ref[:, 4 * chan_count :]
    projected = lax.dot_general(
        w_ref[:, : 4 * chan_count], normed, (((0,), (1,)), ((), ())),
        preferred_element_type=jnp.float32,
    )
    col_flags = valid_ref[...].astype(jnp.float32)
    places = lax.broadcasted_iota(jnp.int32, col_flags.shape, 1)
    row_flags = [
        jnp.sum(jnp.where(places == row_start + r, col_flags, 0.0), axis=1, keepdims=True)
        for r in range(row_count)
    ]
    flags = jnp.concatenate([col_flags * row_flag for row_flag in row_flags], axis=1)
    for chan in range(0, chan_count, 8):
        a_gate, a, b_gate, b = (
            projected[i * chan_count + chan : i * chan_count + chan + 8] for i in range(4)
        )
        left = sigmoid(a_gate) * a * flags
        right = sigmoid(b_gate) * b * flags
        for half, block in enumerate(swap_halves(left, right)):
            for r in range(0, row_count, 2):
                rows = jnp.concatenate(
                    [block[:, (r + i) * col_count : (r + i + 1) * col_count] for i in range(2)], axis=0
                )
                out_ref[(chan // 4 + half) ^ hub, r * 8 : (r + 2) * 8, :] = rows.astype(jnp.bfloat16)
    for fetch in fetches[needed:]:
        fetch.wait()


def receive_blocks(blocks_ref, held_ref):
    shards, rows, _ = blocks_ref.shape
    for i in range(shards):
        held_ref[(i ^ hub) * rows : ((i ^ hub) + 1) * rows, :] = blocks_ref[i].astype(jnp.float32)


def exchange(blocks):
    groups = [[i ^ hub for i in range(blocks.shape[0])]]
    return lax.all_to_all(
        blocks, axes, split_axis=0, concat_axis=0, axis_index_groups=groups, tiled=True
    )


def contract_kernel(
    blocks_ref, normed_ref, w_gate_ref, gain_ref, bias_ref,
    out_ref, gate_ref, scales_ref, held_ref,
):
    total = held_ref.shape[0] // 8
    receive_blocks(blocks_ref, held_ref)
    products = []
    for c in range(4):
        left = held_ref[pl.ds(c, total, stride=8), :].astype(jnp.bfloat16)
        right = held_ref[pl.ds(4 + c, total, stride=8), :].astype(jnp.bfloat16)
        products.append(
            lax.dot_general(
                left, right, (((1,), (1,)), ((), ())), preferred_element_type=jnp.float32
            )
        )
    for row in range(0, total, 8):
        pieces = [product[row : row + 8] for product in products]
        low, high = swap_halves(pieces[0], pieces[1]), swap_halves(pieces[2], pieces[3])
        for half in range(2):
            rows = jnp.concatenate([low[half], high[half]], axis=0)
            out_ref[(row // 4 + half) ^ hub] = rows.astype(jnp.bfloat16)
    gate = jnp.dot(normed_ref[...], w_gate_ref[...], preferred_element_type=jnp.float32)
    gate_ref[...] = sigmoid(gate).astype(jnp.bfloat16)
    for i, vector_ref in enumerate((gain_ref, bias_ref)):
        scales_ref[i] = jnp.transpose(jnp.broadcast_to(vector_ref[...], scales_ref.shape[1:]))


def finish_kernel(blocks_ref, gate_ref, scales_ref, w_ref, out_ref, held_ref):
    row_count, col_count, chan_count = out_ref.shape
    receive_blocks(blocks_ref, held_ref)
    for r in range(row_count):
        triangle = held_ref[pl.ds(r, chan_count, stride=row_count), :]
        normed = layer_norm(triangle, scales_ref[0], scales_ref[1], 0).astype(jnp.bfloat16)
        result = lax.dot_general(
            normed, w_ref[...], (((0,), (0,)), ((), ())), preferred_element_type=jnp.float32
        )
        gate = gate_ref[r * col_count : (r + 1) * col_count, :].astype(jnp.float32)
        out_ref[r] = (gate * result).astype(jnp.bfloat16)


def local_blocks(pair, valid, norm_gain, norm_bias, w_proj, out_gain, out_bias, w_out):
    row_count, col_count, chan_count = pair.shape
    shards = lax.axis_size(axes)
    tokens = row_count * col_count
    vmem = pl.BlockSpec(memory_space=pltpu.VMEM)
    hbm = pl.BlockSpec(memory_space=pltpu.HBM)

    def line(vector):
        return vector.reshape(1, -1)

    def shaped(*dims):
        return jax.ShapeDtypeStruct(dims, jnp.bfloat16)

    def in_hbm(array):
        return pltpu.with_memory_space_constraint(array, pltpu.HBM)

    limit = pltpu.CompilerParams(vmem_limit_bytes=kernel_vmem)
    vector = jax.ShapeDtypeStruct((1, chan_count), jnp.float32)
    square = shaped(chan_count, chan_count)
    sides, normed, w_gate, out_gain, out_bias, w_out = pl.pallas_call(
        project_kernel,
        out_shape=(
            shaped(shards, 8 * row_count, col_count), shaped(tokens, chan_count),
            square, vector, vector, square,
        ),
        in_specs=[hbm] * 8,
        out_specs=(vmem,) * 6,
        scratch_shapes=[
            pltpu.VMEM(pair.shape, jnp.bfloat16),
            pltpu.VMEM((1, col_count), jnp.int32),
            pltpu.VMEM((1, chan_count), jnp.float32),
            pltpu.VMEM((1, chan_count), jnp.float32),
            pltpu.VMEM(w_proj.shape, jnp.bfloat16),
            pltpu.SemaphoreType.DMA((row_count + 8,)),
        ],
        compiler_params=limit,
        name="project",
    )(*map(in_hbm, (
        pair, line(valid), line(norm_gain), line(norm_bias), w_proj,
        line(out_gain), line(out_bias), w_out,
    )))
    sides = exchange(sides)
    triangle, gate_values, scales = pl.pallas_call(
        contract_kernel,
        out_shape=(
            shaped(shards, 4 * row_count, col_count),
            shaped(tokens, chan_count),
            jax.ShapeDtypeStruct((2, chan_count, col_count), jnp.float32),
        ),
        in_specs=[vmem] * 5,
        out_specs=(vmem,) * 3,
        scratch_shapes=[pltpu.VMEM((8 * col_count, col_count), jnp.float32)],
        compiler_params=limit,
        name="contract",
    )(sides, normed, w_gate, out_gain, out_bias)
    triangle = exchange(triangle)
    return pl.pallas_call(
        finish_kernel,
        out_shape=shaped(row_count, col_count, chan_count),
        in_specs=[vmem] * 4,
        out_specs=vmem,
        scratch_shapes=[pltpu.VMEM((tokens, chan_count), jnp.float32)],
        compiler_params=limit,
        name="finish",
    )(triangle, gate_values, scales, w_out)


def local_arrays(pair, valid, norm_gain, norm_bias, w_proj, out_gain, out_bias, w_out):
    row_count, col_count, chan_count = pair.shape
    row_start = lax.axis_index(("wide", "narrow")) * row_count
    col_start = lax.axis_index("sub") * col_count
    row_flags = lax.dynamic_slice_in_dim(valid, row_start, row_count, 0).astype(jnp.float32)
    col_flags = lax.dynamic_slice_in_dim(valid, col_start, col_count, 0).astype(jnp.float32)
    pair_flags = row_flags[:, None] * col_flags[None, :]
    normed = layer_norm(pair.astype(jnp.float32), norm_gain, norm_bias, 2).astype(jnp.bfloat16)
    projected = jnp.einsum(
        "rkc,cd->drk", normed, w_proj[:, : 4 * chan_count], preferred_element_type=jnp.float32
    )
    left_side = (
        jax.nn.sigmoid(projected[:chan_count]) * projected[chan_count : 2 * chan_count] * pair_flags
    ).astype(jnp.bfloat16)
    right_side = (
        jax.nn.sigmoid(projected[2 * chan_count : 3 * chan_count])
        * projected[3 * chan_count :]
        * pair_flags
    ).astype(jnp.bfloat16)
    gate_values = jax.nn.sigmoid(
        jnp.einsum(
            "rkc,cd->rkd", normed, w_proj[:, 4 * chan_count :], preferred_element_type=jnp.float32
        )
    ).astype(jnp.bfloat16)
    both_sides = jnp.stack([left_side, right_side], axis=1)
    both_group = lax.all_to_all(
        both_sides, ("wide", "narrow"), split_axis=0, concat_axis=2, tiled=True
    )
    left_group, right_group = both_group[:, 0], both_group[:, 1]
    partial_sums = jnp.einsum(
        "cik,cjk->cij", left_group, right_group, preferred_element_type=jnp.float32
    )
    summed = lax.psum_scatter(partial_sums, "sub", scatter_dimension=2, tiled=True).astype(
        jnp.bfloat16
    )
    returned = lax.all_to_all(summed, ("wide", "narrow"), split_axis=1, concat_axis=0, tiled=True)
    normed_out = layer_norm(
        returned.astype(jnp.float32), out_gain[:, None, None], out_bias[:, None, None], 0
    ).astype(jnp.bfloat16)
    result_out = jnp.einsum("crj,cd->rjd", normed_out, w_out, preferred_element_type=jnp.float32)
    return (gate_values.astype(jnp.float32) * result_out).astype(jnp.bfloat16)


def local(pair, *rest):
    row_count, col_count, chan_count = pair.shape
    shards = lax.axis_size(axes)
    fits = (
        lax.axis_size("sub") == 1
        and (row_count, col_count, chan_count) == (4, 128, 128)
        and shards * row_count == col_count
        and shards * 4 == chan_count
        and shards == hub + 1
    )
    return (local_blocks if fits else local_arrays)(pair, *rest)


def solution(mesh):
    in_specs = (
        P(("parts", "wide", "narrow"), "sub", None),
        P("parts"),
        P(),
        P(),
        P(),
        P(),
        P(),
        P(),
    )
    out_specs = P(("parts", "wide", "narrow"), "sub", None)
    return jax.shard_map(local, mesh=mesh, in_specs=in_specs, out_specs=out_specs, check_vma=False)
```
